32 devices in a mesh: groups: 1, req: 32 (over z, y, x, core).
Axes of the slice: x: 2, y: 2, z: 4, core: 2. Of those that a mesh axis runs over, the one named last changes fastest.
Arguments:
- hidden: bfloat16 [2, 512, 2880], P(None, ('groups', 'req')), may hold values from -6 to 6
- norm_gain: bfloat16 [2880], replicated, may hold values from 0.099609375 to 1.8984375
- w_gate: bfloat16 [2880, 23040], P(None, 'req'), may hold values from -0.109375 to 0.109375
- w_up: bfloat16 [2880, 23040], P(None, 'req'), may hold values from -0.109375 to 0.109375
- w_down: bfloat16 [23040, 2880], P('req'), may hold values from -0.109375 to 0.109375
- expert_ids: int32 [2, 512, 4], P(None, ('groups', 'req')), may hold values from 0 to 7, as said below
- route_weight: float32 [2, 512, 4], P(None, ('groups', 'req')), may hold values from 0.1 to 1
Outputs:
- mixed: bfloat16 [2, 512, 2880], P(None, ('groups', 'req'))
The draws below stay inside these ranges and needn't reach their ends.
Inputs may be any that keep to these rules, and one draw needn't show every extreme that they name: `expert_ids`: each token names 4 different experts. In each micro-batch the 16 tokens of one device name any one expert at most 12 times, and every expert is named exactly 12 times by the tokens of some device.
All inputs are finite; a program needn't handle non-finite values.
Results may differ from the reference program's by a relative error of at most 0.0058.
Values may be sent and summed in bfloat16 or wider, within the bound.
No kernel may reach another device: no remote copies, remote signals or barrier semaphores. Data moves between devices by JAX's collectives and lax.ppermute only.
A program may use at most 128 MiB of HBM per device.

```python
import math
import jax
import jax.numpy as jnp
from jax import lax

D = 2880
FF = 2880
TOP = 4
MICRO = 2
MB_TOK = 16
EXPERTS = 8
CAP = 12
TOKENS = 512
N_REQ = 32


def draw_expert_ids(key, part):
    remaining = MB_TOK * TOP - CAP
    cycle = max(TOP, (remaining + CAP - 1) // CAP)
    flat = jnp.arange(MB_TOK * TOP, dtype=jnp.int32)
    token_pos = flat // TOP
    member = flat % TOP
    is_own = (member == 0) & (token_pos < CAP)
    before = jnp.minimum(CAP, (flat + TOP - 1) // TOP)
    ranked = flat - before

    def one_device(batch_index, device_index):
        device_key = jax.random.fold_in(jax.random.fold_in(key, 7919 + batch_index), device_index)
        own_expert = device_index % EXPERTS
        others = (own_expert + 1 + jax.random.permutation(device_key, EXPERTS - 1).astype(jnp.int32)) % EXPERTS
        picked = others[ranked % cycle]
        return jnp.where(is_own, own_expert, picked).astype(jnp.int32).reshape(MB_TOK, TOP)
    batches = jnp.arange(MICRO, dtype=jnp.int32)
    devices_all = jnp.arange(N_REQ, dtype=jnp.int32)
    table = jax.vmap(lambda batch_index: jax.vmap(lambda device_index: one_device(batch_index, device_index))(devices_all))(batches)
    return table.reshape(MICRO, TOKENS, TOP).astype(jnp.int32)


def level_of(rng, shape, pieces, low, high):
    gain, own = 1.0, jax.random.fold_in(rng, 6)
    for dim, blocks in pieces:
        steps = jnp.exp(jax.random.uniform(jax.random.fold_in(own, dim), (blocks,), jnp.float32, low / len(pieces), high / len(pieces)))
        gain = gain * jnp.repeat(steps, shape[dim] // blocks).reshape([-1 if axis == dim else 1 for axis in range(len(shape))])
    return gain


def gaussian(key, extent, spread, bound, pieces=(), held_as=jnp.bfloat16):
    level = level_of(key, extent, pieces, -0.22, 0.18) if pieces else 1.0
    values = jax.random.normal(key, extent, jnp.float32) * spread * level
    return jnp.minimum(jnp.maximum(values, -bound), bound).astype(held_as)


def setup_inputs(seed: int = 0, part: int = 0) -> dict:
    streams_of = jax.random.split(jax.random.key(seed), 8)
    part_splits = jax.random.split(jax.random.fold_in(streams_of[7], part), 8)
    hidden = gaussian(part_splits[0], (MICRO, TOKENS, D), 1.0, 6.0, ((1, 32),))
    norm_gain = jnp.clip(1.0 + 0.18 * jax.random.normal(streams_of[1], (D,), jnp.float32), 0.099609375, 1.8984375).astype(jnp.bfloat16)
    w_gate = gaussian(streams_of[2], (D, EXPERTS * FF), D ** -0.5, 0.109375, ((1, 32),))
    w_up = gaussian(streams_of[3], (D, EXPERTS * FF), D ** -0.5, 0.109375, ((1, 32),))
    w_down = gaussian(streams_of[4], (EXPERTS * FF, D), FF ** -0.5, 0.109375, ((0, 32),))
    expert_ids = draw_expert_ids(jax.random.fold_in(jax.random.fold_in(streams_of[7], part), 71), part)
    route_weight = jnp.clip(jnp.exp(math.log(1.0) - 2.3025851 * jax.random.uniform(part_splits[6], (MICRO, TOKENS, TOP), jnp.float32) ** level_of(part_splits[6], (MICRO, TOKENS, TOP), ((1, 32),), -0.2, 0.2)), 0.1, 1.0)
    return {"hidden": hidden, "norm_gain": norm_gain, "w_gate": w_gate, "w_up": w_up, "w_down": w_down, "expert_ids": expert_ids, "route_weight": route_weight}


epsilon = 1e-05
swish_scale = 1.702

def one_batch(hidden_rows, norm_gain, w_gate, w_up, w_down, chosen, weighing):
    residual = hidden_rows.astype(jnp.float32)
    normed = (residual * lax.rsqrt(lax.optimization_barrier(jnp.mean(residual * residual, axis=-1, keepdims=True)) + epsilon) * norm_gain.astype(jnp.float32)).astype(jnp.bfloat16)
    blocks = chosen.reshape(N_REQ, MB_TOK * TOP)
    onehot = (blocks[:, :, None] == jnp.arange(EXPERTS, dtype=jnp.int32)[None, None, :]).astype(jnp.int32)
    slot_index = lax.optimization_barrier(jnp.sum((jnp.cumsum(onehot, axis=1) - onehot) * onehot, axis=-1))
    source = jnp.broadcast_to(jnp.arange(N_REQ, dtype=jnp.int32)[:, None], blocks.shape)
    row_index = ((blocks * N_REQ + source) * CAP + slot_index).reshape(-1).astype(jnp.int32)
    token_of = (jnp.arange(TOKENS * TOP, dtype=jnp.int32) // TOP).astype(jnp.int32)
    buffer = jnp.zeros((EXPERTS * N_REQ * CAP, D), jnp.bfloat16).at[row_index].set(normed[token_of])
    buffer = buffer.reshape(EXPERTS, N_REQ * CAP, D)

    def run_expert(expert):
        slot_rows = buffer[expert]
        start = (expert * FF).astype(jnp.int32)
        gate_cols = lax.dynamic_slice_in_dim(w_gate, start, FF, 1)
        up_cols = lax.dynamic_slice_in_dim(w_up, start, FF, 1)
        down_rows = lax.dynamic_slice_in_dim(w_down, start, FF, 0)
        gate = jnp.dot(slot_rows, gate_cols, preferred_element_type=jnp.float32)
        upward = jnp.dot(slot_rows, up_cols, preferred_element_type=jnp.float32)
        act = ((upward + 1.0) * gate * jax.nn.sigmoid(swish_scale * gate)).astype(jnp.bfloat16)
        return jnp.dot(act, down_rows, preferred_element_type=jnp.float32).astype(jnp.bfloat16)
    outputs = lax.map(run_expert, jnp.arange(EXPERTS, dtype=jnp.int32))
    gathered = outputs.reshape(-1, D)[row_index].reshape(TOKENS, TOP, D).astype(jnp.float32)
    combined = residual
    for member in range(TOP):
        combined = combined + weighing[:, member, None] * gathered[:, member]
    return combined.astype(jnp.bfloat16)

def reference(hidden, norm_gain, w_gate, w_up, w_down, expert_ids, route_weight):
    results = []
    for batch_index in range(MICRO):
        results.append(one_batch(hidden[batch_index], norm_gain, w_gate, w_up, w_down, expert_ids[batch_index], route_weight[batch_index]))
    return jnp.stack(results, axis=0)
```

```python
import functools

import jax
import jax.numpy as jnp
from jax import lax
from jax.experimental import pallas as pl
from jax.experimental.pallas import tpu as pltpu
from jax.sharding import PartitionSpec as P

HSPLIT = 4
LANES = 128

epsilon = 1e-05
swish_scale = 1.702


def split_widths(width):
    first = width // 2 // LANES * LANES
    second = width - first
    held = -(-(second + 32) // LANES) * LANES
    return first, second, held


def moved(block, partner):
    count = lax.axis_size("req")
    return lax.ppermute(block, "req", [(i, partner(i)) for i in range(count)])


def other_core(i):
    return i ^ 1


def first_axis(i):
    return i ^ (2 if i & 1 else 4)


def second_axis(i):
    return i ^ (4 if i & 1 else 2)


def far(step):
    return lambda i: i ^ (step << 3)


def ffn_body(
    width, core_ref, expert_ref, mine_ref, other_ref, gate_hbm, up_hbm, down_hbm,
    keep_ref, send_ref, gate_v, up_v, down_v, swap_v, gate_acc, up_acc, act_v, sems,
):
    first, second, held = split_widths(width)
    quads, rows, _ = mine_ref.shape
    total = quads * rows
    hidden = gate_v.shape[1]
    copies = []
    parts = [(0, first), (first, second)]
    for place, (start, size) in enumerate(parts):
        for index, (source, target) in enumerate(((gate_hbm, gate_v), (up_hbm, up_v))):
            copies.append(
                pltpu.make_async_copy(
                    source.at[pl.ds(start, size)], target.at[pl.ds(start, size)], sems.at[2 * place + index]
                )
            )
    copies.append(pltpu.make_async_copy(down_hbm, down_v, sems.at[4]))

    @pl.when(pl.program_id(0) == 0)
    def _():
        for copy in copies:
            copy.start()

    order = (0, 2, 1, 3)
    for place, source in enumerate(order):
        swap_v[pl.ds(place * rows, rows), :] = other_ref[source]

    tile = mine_ref[:, :, held - LANES :].reshape(total, LANES).astype(jnp.float32)
    lane = lax.broadcasted_iota(jnp.int32, (total, LANES), 1)
    chosen = (lane >= LANES - 32) & (lane < LANES - 16) & (tile == expert_ref[0].astype(jnp.float32))
    weight = jnp.sum(
        jnp.where(chosen, pltpu.roll(tile, LANES - 16, 1), 0.0), axis=1, keepdims=True
    )

    def run(first_rows, second_rows, first_is_mine):
        def ready(index):
            @pl.when(pl.program_id(0) == 0)
            def _():
                copies[index].wait()

        ready(0)
        gate_acc[...] = jnp.dot(first_rows(), gate_v[:first, :], preferred_element_type=jnp.float32)
        ready(1)
        up_acc[...] = jnp.dot(first_rows(), up_v[:first, :], preferred_element_type=jnp.float32)
        ready(2)
        gate_acc[...] += jnp.dot(second_rows(), gate_v[first:, :], preferred_element_type=jnp.float32)
        ready(3)
        up_acc[...] += jnp.dot(second_rows(), up_v[first:, :], preferred_element_type=jnp.float32)
        gate = gate_acc[...]
        act_v[...] = ((up_acc[...] + 1.0) * gate * jax.nn.sigmoid(swish_scale * gate)).astype(jnp.bfloat16)
        ready(4)
        for is_first, (start, size) in zip((True, False), parts):
            result = (
                weight * jnp.dot(act_v[...], down_v[:, start : start + size], preferred_element_type=jnp.float32)
            ).astype(jnp.bfloat16)
            if is_first == first_is_mine:
                keep_ref[:, :, :size] = result.reshape(quads, rows, size)
                if size < held:
                    keep_ref[:, :, size:] = jnp.zeros((quads, rows, held - size), jnp.bfloat16)
            else:
                for place, source in enumerate(order):
                    send_ref[place, :, :size] = result[source * rows : (source + 1) * rows]
                if size < held:
                    send_ref[:, :, size:] = jnp.zeros((quads, rows, held - size), jnp.bfloat16)

    @pl.when(core_ref[0] == 0)
    def _():
        run(
            lambda: mine_ref[:, :, :first].reshape(total, first),
            lambda: swap_v[:, :second],
            True,
        )

    @pl.when(core_ref[0] != 0)
    def _():
        run(
            lambda: swap_v[:, :first],
            lambda: mine_ref[:, :, :second].reshape(total, second),
            False,
        )


def ffn(core, expert, mine, other, w_gate, w_up, w_down):
    quads, rows, held = mine.shape
    width, hidden = w_gate.shape
    block = min(rows, 128)
    total = quads * block
    spec = pl.BlockSpec((quads, block, held), lambda step, *_: (0, step, 0))
    hbm = pl.BlockSpec(memory_space=pl.ANY)
    return pl.pallas_call(
        functools.partial(ffn_body, width),
        out_shape=[jax.ShapeDtypeStruct(mine.shape, jnp.bfloat16)] * 2,
        grid_spec=pltpu.PrefetchScalarGridSpec(
            num_scalar_prefetch=2,
            grid=(rows // block,),
            in_specs=[spec, spec, hbm, hbm, hbm],
            out_specs=[spec, spec],
            scratch_shapes=[
                pltpu.VMEM((width, hidden), jnp.bfloat16),
                pltpu.VMEM((width, hidden), jnp.bfloat16),
                pltpu.VMEM((hidden, width), jnp.bfloat16),
                pltpu.VMEM((total, held), jnp.bfloat16),
                pltpu.VMEM((total, hidden), jnp.float32),
                pltpu.VMEM((total, hidden), jnp.float32),
                pltpu.VMEM((total, hidden), jnp.bfloat16),
                pltpu.SemaphoreType.DMA((5,)),
            ],
        ),
        compiler_params=pltpu.CompilerParams(vmem_limit_bytes=48 * 2**20),
        cost_estimate=pl.CostEstimate(
            flops=6 * quads * rows * width * hidden,
            bytes_accessed=6 * width * hidden + 8 * quads * rows * held,
            transcendentals=quads * rows * hidden,
        ),
    )(core, expert, mine, other, w_gate, w_up, w_down)


def local(hidden, norm_gain, w_gate, w_up, w_down, expert_ids, route_weight):
    micro_count, tokens, width = hidden.shape
    top_count = expert_ids.shape[2]
    devices = lax.axis_size("req")
    distant = devices // 8
    first, second, held = split_widths(width)
    position = lax.axis_index("req")
    core = position & 1
    lower = core == 0
    core_scalar = core.astype(jnp.int32).reshape(1)
    expert_scalar = (position // HSPLIT).astype(jnp.int32).reshape(1)
    gain_f32 = norm_gain.astype(jnp.float32)

    def join(a, b):
        return jnp.concatenate([a, b], axis=0)

    def spread(batch_index):
        residual = hidden[batch_index].astype(jnp.float32)
        normed = (
            residual
            * lax.rsqrt(jnp.mean(residual * residual, axis=-1, keepdims=True) + epsilon)
            * gain_f32
        ).astype(jnp.bfloat16)
        weights = route_weight[batch_index]
        high = lax.reduce_precision(weights, 8, 7)
        middle = lax.reduce_precision(weights - high, 8, 7)
        low = weights - high - middle
        ids = expert_ids[batch_index].astype(jnp.float32)
        gap = jnp.full((tokens, 16 - 3 * top_count), -1.0, jnp.float32)
        routing = jnp.concatenate([ids, ids, ids, gap, high, middle, low, gap], axis=1).astype(jnp.bfloat16)

        def padded(part):
            blank = jnp.zeros((tokens, held - 32 - part.shape[1]), jnp.bfloat16)
            return jnp.concatenate([part, blank, routing], axis=1)

        low_half, high_half = padded(normed[:, :first]), padded(normed[:, first:])
        mine = jnp.where(lower, low_half, high_half)
        theirs = moved(jnp.where(lower, high_half, low_half), other_core)
        pair = join(jnp.where(lower, mine, theirs), jnp.where(lower, theirs, mine))
        column = jnp.concatenate([pair] + [moved(pair, far(j)) for j in range(1, distant)], axis=0)
        half_plane = join(column, moved(column, first_axis))
        plane = join(half_plane, moved(half_plane, second_axis))
        rows = column.shape[0]
        mine = plane.reshape(4, rows, held)
        return residual, mine, moved(plane, other_core).reshape(4, rows, held)

    def add(a, b):
        return (a.astype(jnp.float32) + b.astype(jnp.float32)).astype(jnp.bfloat16)

    def collect(residual, keep, send):
        total = add(keep, moved(send, other_core))
        total = add(total[:2], moved(total[2:], second_axis))
        total = add(total[0], moved(total[1], first_axis))
        total = total.reshape(distant, 2 * tokens, held)
        summed = total[0].astype(jnp.float32)
        for j in range(1, distant):
            summed = summed + moved(total[j], far(j)).astype(jnp.float32)
        own = jnp.where(lower, summed[:tokens], summed[tokens:])
        give = jnp.where(lower, summed[tokens:], summed[:tokens]).astype(jnp.bfloat16)
        taken = moved(give, other_core).astype(jnp.float32)
        mixture = jnp.concatenate(
            [
                jnp.where(lower, own, taken)[:, :first],
                jnp.where(lower, taken, own)[:, :second],
            ],
            axis=1,
        )
        return (residual + mixture).astype(jnp.bfloat16)

    gathered = [spread(b) for b in range(micro_count)]
    results = []
    for residual, mine, other in gathered:
        keep, send = ffn(core_scalar, expert_scalar, mine, other, w_gate, w_up, w_down)
        results.append(collect(residual, keep, send))
    return jnp.stack(results, axis=0)


def solution(mesh):
    return jax.shard_map(
        local,
        mesh=mesh,
        in_specs=(
            P(None, ("groups", "req"), None),
            P(),
            P(None, "req"),
            P(None, "req"),
            P("req", None),
            P(None, ("groups", "req"), None),
            P(None, ("groups", "req"), None),
        ),
        out_specs=P(None, ("groups", "req"), None),
        check_vma=False,
    )
```

```python
import functools

import jax
import jax.numpy as jnp
from jax import lax
from jax.experimental import pallas as pl
from jax.experimental.pallas import tpu as pltpu
from jax.sharding import PartitionSpec as P

HSPLIT = 4
LANES = 128
ROUTING = 32

epsilon = 1e-05
swish_scale = 1.702

across = (((1,), (1,)), ((), ()))
downward = (((0,), (0,)), ((), ()))


def split_widths(width):
    first = width // 2 // LANES * LANES
    second = width - first
    held = -(-(second + ROUTING) // LANES) * LANES
    return first, second, held


def moved(block, partner):
    count = lax.axis_size("req")
    return lax.ppermute(block, "req", [(i, partner(i)) for i in range(count)])


def other_core(i):
    return i ^ 1


def first_axis(i):
    return i ^ (2 if i & 1 else 4)


def second_axis(i):
    return i ^ (4 if i & 1 else 2)


def far(step):
    return lambda i: i ^ (step << 3)


def whole_arrays(count):
    return [pl.BlockSpec(memory_space=pltpu.VMEM)] * count


SCALARS = pl.BlockSpec(memory_space=pltpu.SMEM)


def select_body(tokens, capacity, places_ref, near_ref, next_ref, own_ref, send_ref, slots_ref):
    rows = near_ref.shape[0]
    held = near_ref.shape[1]
    total = 2 * rows
    compact = own_ref.shape[0]
    tile = jnp.concatenate([near_ref[:, held - LANES :], next_ref[:, held - LANES :]], axis=0).astype(jnp.float32)
    lane = lax.broadcasted_iota(jnp.int32, (total, LANES), 1)
    row = lax.broadcasted_iota(jnp.int32, (total, LANES), 0)
    listed = (lane >= LANES - ROUTING) & (lane < LANES - ROUTING // 2)

    def named(expert):
        return jnp.max(jnp.where(listed & (tile == expert.astype(jnp.float32)), 1.0, 0.0), axis=1, keepdims=True)

    mine, theirs = named(places_ref[1]), named(places_ref[2])
    marks = jnp.where(lane == 0, mine, jnp.where(lane == 1, theirs, 0.0))
    left = lax.broadcasted_iota(jnp.int32, (total, total), 0)
    right = lax.broadcasted_iota(jnp.int32, (total, total), 1)
    earlier = ((right < left) & (left // tokens == right // tokens)).astype(jnp.float32).astype(jnp.bfloat16)
    ahead = jnp.dot(earlier, marks.astype(jnp.bfloat16), preferred_element_type=jnp.float32)
    slots = jnp.where(marks > 0.0, ahead + (row // tokens * capacity).astype(jnp.float32), -1.0)
    slots_ref[...] = slots
    column = lax.broadcasted_iota(jnp.int32, (total, compact), 1).astype(jnp.float32)
    for index, target in enumerate((own_ref, send_ref)):
        picks = (slots[:, index : index + 1] == column).astype(jnp.float32).astype(jnp.bfloat16)
        target[...] = (
            lax.dot_general(picks[:rows], near_ref[...], downward, preferred_element_type=jnp.float32)
            + lax.dot_general(picks[rows:], next_ref[...], downward, preferred_element_type=jnp.float32)
        ).astype(jnp.bfloat16)


def select(tokens, capacity, places, near, following):
    rows, held = near.shape
    compact = 2 * rows // tokens * capacity
    block = jax.ShapeDtypeStruct((compact, held), jnp.bfloat16)
    return pl.pallas_call(
        functools.partial(select_body, tokens, capacity),
        out_shape=[block, block, jax.ShapeDtypeStruct((2 * rows, LANES), jnp.float32)],
        in_specs=[SCALARS] + whole_arrays(2),
        out_specs=whole_arrays(3),
        compiler_params=pltpu.CompilerParams(vmem_limit_bytes=40 * 2**20),
        cost_estimate=pl.CostEstimate(flops=8 * rows * compact * held, bytes_accessed=8 * rows * held, transcendentals=0),
    )(places, near, following)


def merge_body(slots_ref, keep_ref, taken_ref, arrived_ref, near_ref, next_ref):
    rows = near_ref.shape[0]
    total = 2 * rows
    compact = keep_ref.shape[0]
    slots = slots_ref[...]
    column = lax.broadcasted_iota(jnp.int32, (total, compact), 1).astype(jnp.float32)
    summed = keep_ref[...] + taken_ref[...].astype(jnp.float32)
    high = summed.astype(jnp.bfloat16)
    result = jnp.zeros((total, keep_ref.shape[1]), jnp.float32)
    for index, source in enumerate((high, arrived_ref[...])):
        picks = (slots[:, index : index + 1] == column).astype(jnp.float32).astype(jnp.bfloat16)
        result += jnp.dot(picks, source, preferred_element_type=jnp.float32)
    near_ref[...] = result[:rows]
    next_ref[...] = result[rows:].astype(jnp.bfloat16)


def merge(slots, keep, taken, arrived):
    rows = slots.shape[0] // 2
    compact, held = keep.shape
    return pl.pallas_call(
        merge_body,
        out_shape=[
            jax.ShapeDtypeStruct((rows, held), jnp.float32),
            jax.ShapeDtypeStruct((rows, held), jnp.bfloat16),
        ],
        in_specs=whole_arrays(4),
        out_specs=whole_arrays(2),
        compiler_params=pltpu.CompilerParams(vmem_limit_bytes=40 * 2**20),
        cost_estimate=pl.CostEstimate(flops=8 * rows * compact * held, bytes_accessed=8 * rows * held, transcendentals=0),
    )(slots, keep, taken, arrived)


def ffn_body(
    places_ref, mine_near_ref, mine_far_ref, other_near_ref, other_far_ref, gate_hbm, up_hbm, down_hbm,
    keep_near_ref, keep_far_ref, send_near_ref, send_far_ref, gate_v, up_v, down_v, rows_v, act_v, sems,
):
    hidden, width = gate_v.shape
    first, second, held = split_widths(width)
    pair = mine_near_ref.shape[0]
    quad = pair // 2
    chunk = hidden // 3
    copies = []
    for part in range(3):
        for place, (source, target) in enumerate(((gate_hbm, gate_v), (up_hbm, up_v))):
            there = pl.ds(part * chunk, chunk)
            copies.append(pltpu.make_async_copy(source.at[there], target.at[there], sems.at[2 * part + place]))
    copies.append(pltpu.make_async_copy(down_hbm, down_v, sems.at[6]))
    for copy in copies:
        copy.start()

    def lay(near, far_ref, swapped, start, size):
        for place in range(4):
            if swapped:
                source, block = (near, far_ref)[place % 2], place // 2
            else:
                source, block = (near, far_ref)[place // 2], place % 2
            rows_v[pl.ds(place * quad, quad), start : start + size] = source[pl.ds(block * quad, quad), :size]

    lower = places_ref[0] == 0

    @pl.when(lower)
    def _():
        lay(mine_near_ref, mine_far_ref, False, 0, first)
        lay(other_near_ref, other_far_ref, True, first, second)

    @pl.when(jnp.logical_not(lower))
    def _():
        lay(other_near_ref, other_far_ref, True, 0, first)
        lay(mine_near_ref, mine_far_ref, False, first, second)

    tile = jnp.concatenate([mine_near_ref[:, held - LANES :], mine_far_ref[:, held - LANES :]], axis=0)
    tile = tile.astype(jnp.float32)
    lane = lax.broadcasted_iota(jnp.int32, (2 * pair, LANES), 1)
    listed = (lane >= LANES - ROUTING) & (lane < LANES - ROUTING // 2)
    chosen = listed & (tile == places_ref[1].astype(jnp.float32))
    weight = jnp.sum(
        jnp.where(chosen, pltpu.roll(tile, LANES - ROUTING // 2, 1), 0.0), axis=1, keepdims=True
    )

    for part in range(3):
        there = slice(part * chunk, (part + 1) * chunk)
        copies[2 * part].wait()
        gate = lax.dot_general(rows_v[...], gate_v[there, :], across, preferred_element_type=jnp.float32)
        copies[2 * part + 1].wait()
        up = lax.dot_general(rows_v[...], up_v[there, :], across, preferred_element_type=jnp.float32)
        act_v[:, there] = ((up + 1.0) * gate * jax.nn.sigmoid(swish_scale * gate)).astype(jnp.bfloat16)
    copies[6].wait()

    def keep_half(result, size):
        keep_near_ref[:, :size] = result[:pair]
        keep_far_ref[:, :size] = result[pair:]
        if size < held:
            keep_near_ref[:, size:] = jnp.zeros((pair, held - size), jnp.float32)
            keep_far_ref[:, size:] = jnp.zeros((pair, held - size), jnp.float32)

    def send_half(result, size):
        result = result.astype(jnp.bfloat16)
        for place in range(4):
            target, block = (send_near_ref, send_far_ref)[place % 2], place // 2
            target[pl.ds(block * quad, quad), :size] = result[place * quad : (place + 1) * quad]
        if size < held:
            send_near_ref[:, size:] = jnp.zeros((pair, held - size), jnp.bfloat16)
            send_far_ref[:, size:] = jnp.zeros((pair, held - size), jnp.bfloat16)

    low = weight * jnp.dot(act_v[...], down_v[:, :first], preferred_element_type=jnp.float32)

    @pl.when(lower)
    def _():
        keep_half(low, first)

    @pl.when(jnp.logical_not(lower))
    def _():
        send_half(low, first)

    high = weight * jnp.dot(act_v[...], down_v[:, first:], preferred_element_type=jnp.float32)

    @pl.when(lower)
    def _():
        send_half(high, second)

    @pl.when(jnp.logical_not(lower))
    def _():
        keep_half(high, second)


def ffn(places, mine_near, mine_far, other_near, other_far, gate_t, up_t, w_down):
    pair, held = mine_near.shape
    hidden, width = gate_t.shape
    total = 2 * pair
    hbm = pl.BlockSpec(memory_space=pl.ANY)
    return pl.pallas_call(
        ffn_body,
        out_shape=[jax.ShapeDtypeStruct((pair, held), jnp.float32)] * 2
        + [jax.ShapeDtypeStruct((pair, held), jnp.bfloat16)] * 2,
        in_specs=[SCALARS] + whole_arrays(4) + [hbm] * 3,
        out_specs=whole_arrays(4),
        scratch_shapes=[
            pltpu.VMEM((hidden, width), jnp.bfloat16),
            pltpu.VMEM((hidden, width), jnp.bfloat16),
            pltpu.VMEM((hidden, width), jnp.bfloat16),
            pltpu.VMEM((total, width), jnp.bfloat16),
            pltpu.VMEM((total, hidden), jnp.bfloat16),
            pltpu.SemaphoreType.DMA((7,)),
        ],
        compiler_params=pltpu.CompilerParams(vmem_limit_bytes=48 * 2**20),
        cost_estimate=pl.CostEstimate(
            flops=6 * total * width * hidden,
            bytes_accessed=6 * width * hidden + 8 * total * held,
            transcendentals=total * hidden,
        ),
    )(places, mine_near, mine_far, other_near, other_far, gate_t, up_t, w_down)


def local(hidden, norm_gain, w_gate, w_up, w_down, expert_ids, route_weight):
    micro_count, tokens, width = hidden.shape
    top_count = expert_ids.shape[2]
    devices = lax.axis_size("req")
    experts = devices // HSPLIT
    rounded = HSPLIT * ((3 * tokens * top_count + 2 * experts * HSPLIT - 1) // (2 * experts * HSPLIT))
    capacity = min(tokens, max(HSPLIT, rounded))
    distant = devices // 8
    first, second, held = split_widths(width)
    position = lax.axis_index("req")
    core = position & 1
    lower = core == 0
    expert = position // HSPLIT
    places = jnp.stack([core, expert, expert ^ core]).astype(jnp.int32)
    gate_t, up_t = w_gate.T, w_up.T

    def join(*blocks):
        return jnp.concatenate(blocks, axis=0)

    residual = hidden.astype(jnp.float32)
    normed = (
        residual
        * lax.rsqrt(jnp.mean(residual * residual, axis=-1, keepdims=True) + epsilon)
        * norm_gain.astype(jnp.float32)
    ).astype(jnp.bfloat16)
    high = lax.reduce_precision(route_weight, 8, 7)
    middle = lax.reduce_precision(route_weight - high, 8, 7)
    low = route_weight - high - middle
    ids = expert_ids.astype(jnp.float32)
    gap = jnp.full((micro_count, tokens, ROUTING // 2 - 3 * top_count), -1.0, jnp.float32)
    routing = jnp.concatenate([ids, ids, ids, gap, high, middle, low, gap], axis=2).astype(jnp.bfloat16)

    def padded(part):
        blank = jnp.zeros((micro_count, tokens, held - ROUTING - part.shape[2]), jnp.bfloat16)
        return jnp.concatenate([part, blank, routing], axis=2)

    low_half, high_half = padded(normed[:, :, :first]), padded(normed[:, :, first:])
    mine = jnp.where(lower, low_half, high_half)
    theirs = moved(jnp.where(lower, high_half, low_half), other_core)
    pairs = [
        join(jnp.where(lower, mine[b], theirs[b]), jnp.where(lower, theirs[b], mine[b]))
        for b in range(micro_count)
    ]

    def column_of(pair):
        return join(pair, *[moved(pair, far(j)) for j in range(1, distant)])

    def tied(*arrays):
        return lax.optimization_barrier(arrays)

    held_state = []
    last = None
    for b in range(micro_count):
        pair = pairs[b]
        if last is not None:
            pair, _ = tied(pair, last["column"])
        column = column_of(pair)
        following = moved(column, first_axis)
        own, send, slots = select(tokens, capacity, places, column, following)
        if last is not None:
            send, last["arrived"] = tied(send, last["arrived"])
        arrived = moved(send, second_axis)
        last = {"column": column, "own": own, "slots": slots, "arrived": arrived}
        held_state.append(last)

    outputs = []
    before = None
    for b in range(micro_count):
        state = held_state[b]
        own, arrived = state["own"], state["arrived"]
        if before is not None:
            arrived, *before = tied(arrived, *before)
            outputs[-1] = before
        before = ffn(
            places, own, arrived, moved(own, other_core), moved(arrived, other_core), gate_t, up_t, w_down
        )
        outputs.append(before)

    def collect(state, keep_near, keep_far, send_near, send_far):
        give = (keep_far + moved(send_far, other_core).astype(jnp.float32)).astype(jnp.bfloat16)
        arrived = moved(give, second_axis)
        near, following = merge(state["slots"], keep_near, moved(send_near, other_core), arrived)
        near = near + moved(following, first_axis).astype(jnp.float32)
        near = near.reshape(distant, 2 * tokens, held)
        summed = near[0]
        for j in range(1, distant):
            summed = summed + moved(near[j].astype(jnp.bfloat16), far(j)).astype(jnp.float32)
        return summed

    sums = jnp.stack([collect(state, *out) for state, out in zip(held_state, outputs)])
    own = jnp.where(lower, sums[:, :tokens], sums[:, tokens:])
    give = jnp.where(lower, sums[:, tokens:], sums[:, :tokens]).astype(jnp.bfloat16)
    taken = moved(give, other_core).astype(jnp.float32)
    mixture = jnp.concatenate(
        [jnp.where(lower, own, taken)[:, :, :first], jnp.where(lower, taken, own)[:, :, :second]], axis=2
    )
    return (residual + mixture).astype(jnp.bfloat16)


def solution(mesh):
    return jax.shard_map(
        local,
        mesh=mesh,
        in_specs=(
            P(None, ("groups", "req"), None),
            P(),
            P(None, "req"),
            P(None, "req"),
            P("req", None),
            P(None, ("groups", "req"), None),
            P(None, ("groups", "req"), None),
        ),
        out_specs=P(None, ("groups", "req"), None),
        check_vma=False,
    )
```

```python
import functools

import jax
import jax.numpy as jnp
from jax import lax
from jax.experimental import pallas as pl
from jax.experimental.pallas import tpu as pltpu
from jax.sharding import PartitionSpec as P

HSPLIT = 4
LANES = 128
ROUTING = 32

epsilon = 1e-05
swish_scale = 1.702

across = (((1,), (1,)), ((), ()))
downward = (((0,), (0,)), ((), ()))


def split_widths(width):
    first = width // 2 // LANES * LANES
    second = width - first
    held = -(-(second + ROUTING) // LANES) * LANES
    return first, second, held


def moved(block, partner):
    count = lax.axis_size("req")
    return lax.ppermute(block, "req", [(i, partner(i)) for i in range(count)])


def other_core(i):
    return i ^ 1


def first_axis(i):
    return i ^ (2 if i & 1 else 4)


def second_axis(i):
    return i ^ (4 if i & 1 else 2)


def far(step):
    return lambda i: i ^ (step << 3)


def whole_arrays(count):
    return [pl.BlockSpec(memory_space=pltpu.VMEM)] * count


SCALARS = pl.BlockSpec(memory_space=pltpu.SMEM)


def select_body(tokens, capacity, index, places_ref, near_ref, next_ref, rows_ref, *slots_refs):
    rows = near_ref.shape[0]
    held = near_ref.shape[1]
    total = 2 * rows
    compact = rows_ref.shape[0]
    tile = jnp.concatenate([near_ref[:, held - LANES :], next_ref[:, held - LANES :]], axis=0).astype(jnp.float32)
    lane = lax.broadcasted_iota(jnp.int32, (total, LANES), 1)
    row = lax.broadcasted_iota(jnp.int32, (total, LANES), 0)
    listed = (lane >= LANES - ROUTING) & (lane < LANES - ROUTING // 2)

    def named(expert):
        return jnp.max(jnp.where(listed & (tile == expert.astype(jnp.float32)), 1.0, 0.0), axis=1, keepdims=True)

    mine, theirs = named(places_ref[1]), named(places_ref[2])
    marks = jnp.where(lane == 0, mine, jnp.where(lane == 1, theirs, 0.0))
    left = lax.broadcasted_iota(jnp.int32, (total, total), 0)
    right = lax.broadcasted_iota(jnp.int32, (total, total), 1)
    earlier = ((right < left) & (left // tokens == right // tokens)).astype(jnp.float32).astype(jnp.bfloat16)
    ahead = jnp.dot(earlier, marks.astype(jnp.bfloat16), preferred_element_type=jnp.float32)
    slots = jnp.where(marks > 0.0, ahead + (row // tokens * capacity).astype(jnp.float32), -1.0)
    for slots_ref in slots_refs:
        slots_ref[...] = slots
    column = lax.broadcasted_iota(jnp.int32, (total, compact), 1).astype(jnp.float32)
    picks = (slots[:, index : index + 1] == column).astype(jnp.float32).astype(jnp.bfloat16)
    rows_ref[...] = (
        lax.dot_general(picks[:rows], near_ref[...], downward, preferred_element_type=jnp.float32)
        + lax.dot_general(picks[rows:], next_ref[...], downward, preferred_element_type=jnp.float32)
    ).astype(jnp.bfloat16)


def select(tokens, capacity, index, places, near, following):
    rows, held = near.shape
    compact = 2 * rows // tokens * capacity
    block = jax.ShapeDtypeStruct((compact, held), jnp.bfloat16)
    return pl.pallas_call(
        functools.partial(select_body, tokens, capacity, index),
        out_shape=[block] + [jax.ShapeDtypeStruct((2 * rows, LANES), jnp.float32)] * (1 - index),
        in_specs=[SCALARS] + whole_arrays(2),
        out_specs=whole_arrays(2 - index),
        compiler_params=pltpu.CompilerParams(vmem_limit_bytes=20 * 2**20),
        cost_estimate=pl.CostEstimate(flops=8 * rows * compact * held, bytes_accessed=8 * rows * held, transcendentals=0),
    )(places, near, following)


def merge_body(slots_ref, keep_ref, taken_ref, arrived_ref, near_ref, next_ref):
    rows = near_ref.shape[0]
    total = 2 * rows
    compact = keep_ref.shape[0]
    slots = slots_ref[...]
    column = lax.broadcasted_iota(jnp.int32, (total, compact), 1).astype(jnp.float32)
    summed = keep_ref[...] + taken_ref[...].astype(jnp.float32)
    high = summed.astype(jnp.bfloat16)
    result = jnp.zeros((total, keep_ref.shape[1]), jnp.float32)
    for index, source in enumerate((high, arrived_ref[...])):
        picks = (slots[:, index : index + 1] == column).astype(jnp.float32).astype(jnp.bfloat16)
        result += jnp.dot(picks, source, preferred_element_type=jnp.float32)
    near_ref[...] = result[:rows]
    next_ref[...] = result[rows:].astype(jnp.bfloat16)


def merge(slots, keep, taken, arrived):
    rows = slots.shape[0] // 2
    compact, held = keep.shape
    return pl.pallas_call(
        merge_body,
        out_shape=[
            jax.ShapeDtypeStruct((rows, held), jnp.float32),
            jax.ShapeDtypeStruct((rows, held), jnp.bfloat16),
        ],
        in_specs=whole_arrays(4),
        out_specs=whole_arrays(2),
        compiler_params=pltpu.CompilerParams(vmem_limit_bytes=20 * 2**20),
        cost_estimate=pl.CostEstimate(flops=8 * rows * compact * held, bytes_accessed=8 * rows * held, transcendentals=0),
    )(slots, keep, taken, arrived)


def ffn_body(
    places_ref, mine_near_ref, mine_far_ref, other_near_ref, other_far_ref, gate_v, up_v, down_v,
    keep_near_ref, keep_far_ref, send_near_ref, send_far_ref, rows_v, act_v,
):
    hidden, width = gate_v.shape
    first, second, held = split_widths(width)
    pair = mine_near_ref.shape[0]
    quad = pair // 2
    chunk = hidden // 3
    def lay(near, far_ref, swapped, start, size):
        for place in range(4):
            if swapped:
                source, block = (near, far_ref)[place % 2], place // 2
            else:
                source, block = (near, far_ref)[place // 2], place % 2
            rows_v[pl.ds(place * quad, quad), start : start + size] = source[pl.ds(block * quad, quad), :size]

    lower = places_ref[0] == 0

    @pl.when(lower)
    def _():
        lay(mine_near_ref, mine_far_ref, False, 0, first)
        lay(other_near_ref, other_far_ref, True, first, second)

    @pl.when(jnp.logical_not(lower))
    def _():
        lay(other_near_ref, other_far_ref, True, 0, first)
        lay(mine_near_ref, mine_far_ref, False, first, second)

    tile = jnp.concatenate([mine_near_ref[:, held - LANES :], mine_far_ref[:, held - LANES :]], axis=0)
    tile = tile.astype(jnp.float32)
    lane = lax.broadcasted_iota(jnp.int32, (2 * pair, LANES), 1)
    listed = (lane >= LANES - ROUTING) & (lane < LANES - ROUTING // 2)
    chosen = listed & (tile == places_ref[1].astype(jnp.float32))
    weight = jnp.sum(
        jnp.where(chosen, pltpu.roll(tile, LANES - ROUTING // 2, 1), 0.0), axis=1, keepdims=True
    )

    for part in range(3):
        there = slice(part * chunk, (part + 1) * chunk)
        gate = lax.dot_general(rows_v[...], gate_v[there, :], across, preferred_element_type=jnp.float32)
        up = lax.dot_general(rows_v[...], up_v[there, :], across, preferred_element_type=jnp.float32)
        act_v[:, there] = ((up + 1.0) * gate * jax.nn.sigmoid(swish_scale * gate)).astype(jnp.bfloat16)

    def keep_half(result, size):
        keep_near_ref[:, :size] = result[:pair]
        keep_far_ref[:, :size] = result[pair:]
        if size < held:
            keep_near_ref[:, size:] = jnp.zeros((pair, held - size), jnp.float32)
            keep_far_ref[:, size:] = jnp.zeros((pair, held - size), jnp.float32)

    def send_half(result, size):
        result = result.astype(jnp.bfloat16)
        for place in range(4):
            target, block = (send_near_ref, send_far_ref)[place % 2], place // 2
            target[pl.ds(block * quad, quad), :size] = result[place * quad : (place + 1) * quad]
        if size < held:
            send_near_ref[:, size:] = jnp.zeros((pair, held - size), jnp.bfloat16)
            send_far_ref[:, size:] = jnp.zeros((pair, held - size), jnp.bfloat16)

    low = weight * jnp.dot(act_v[...], down_v[:, :first], preferred_element_type=jnp.float32)

    @pl.when(lower)
    def _():
        keep_half(low, first)

    @pl.when(jnp.logical_not(lower))
    def _():
        send_half(low, first)

    high = weight * jnp.dot(act_v[...], down_v[:, first:], preferred_element_type=jnp.float32)

    @pl.when(lower)
    def _():
        send_half(high, second)

    @pl.when(jnp.logical_not(lower))
    def _():
        keep_half(high, second)


def ffn(places, mine_near, mine_far, other_near, other_far, gate_t, up_t, w_down):
    pair, held = mine_near.shape
    hidden, width = gate_t.shape
    total = 2 * pair
    return pl.pallas_call(
        ffn_body,
        out_shape=[jax.ShapeDtypeStruct((pair, held), jnp.float32)] * 2
        + [jax.ShapeDtypeStruct((pair, held), jnp.bfloat16)] * 2,
        in_specs=[SCALARS] + whole_arrays(7),
        out_specs=whole_arrays(4),
        scratch_shapes=[
            pltpu.VMEM((total, width), jnp.bfloat16),
            pltpu.VMEM((total, hidden), jnp.bfloat16),
        ],
        compiler_params=pltpu.CompilerParams(vmem_limit_bytes=20 * 2**20),
        cost_estimate=pl.CostEstimate(
            flops=6 * total * width * hidden,
            bytes_accessed=6 * width * hidden + 8 * total * held,
            transcendentals=total * hidden,
        ),
    )(places, mine_near, mine_far, other_near, other_far, gate_t, up_t, w_down)


def preload_body(_, *refs):
    count = (len(refs) - 1) // 2
    sems = refs[-1]
    copies = [pltpu.make_async_copy(refs[i], refs[count + i], sems.at[i]) for i in range(count)]
    for copy in copies:
        copy.start()
    for copy in copies:
        copy.wait()


def preload(token, *arrays):
    return pl.pallas_call(
        preload_body,
        out_shape=[pltpu.VMEM(a.shape, a.dtype) for a in arrays],
        in_specs=[pl.BlockSpec(memory_space=pl.ANY)] + [pl.BlockSpec(memory_space=pltpu.HBM)] * len(arrays),
        out_specs=whole_arrays(len(arrays)),
        scratch_shapes=[pltpu.SemaphoreType.DMA((len(arrays),))],
        compiler_params=pltpu.CompilerParams(vmem_limit_bytes=20 * 2**20),
    )(token, *arrays)


def prologue_body(
    tokens, top_count, places_ref, hidden_ref, gain_ref, ids_ref, weights_ref, mine_ref, give_ref
):
    micro_count, _, width = hidden_ref.shape
    first, second, held = split_widths(width)
    lane = lax.broadcasted_iota(jnp.int32, (tokens, LANES), 1)
    here = lane % (ROUTING // 2)
    on_ids = (lane >= LANES - ROUTING) & (lane < LANES - ROUTING // 2)
    on_weights = lane >= LANES - ROUTING // 2
    diagonal = lax.broadcasted_iota(jnp.int32, (tokens, tokens), 0) == lax.broadcasted_iota(
        jnp.int32, (tokens, tokens), 1
    )

    def upright(line):
        return jnp.sum(jnp.where(diagonal, line, 0.0), axis=1, keepdims=True)

    def store(ref, b, part, tile):
        size = part.shape[1]
        inside = size // LANES * LANES
        ref[b, :, :inside] = part[:, :inside].astype(jnp.bfloat16)
        if inside < size:
            rest = jnp.concatenate([part[:, inside:], jnp.zeros((tokens, LANES - size + inside), jnp.float32)], axis=1)
            tile = jnp.where(lane < size - inside, rest, tile)
        ref[b, :, inside:] = tile.astype(jnp.bfloat16)

    lower = places_ref[0] == 0
    for b in range(micro_count):
        residual = hidden_ref[b].astype(jnp.float32)
        scale = lax.rsqrt(jnp.mean(residual * residual, axis=-1, keepdims=True) + epsilon)
        normed = residual * scale * gain_ref[...].astype(jnp.float32)
        tile = jnp.where(on_ids, -1.0, 0.0)
        for k in range(top_count):
            number = upright(ids_ref[b, k : k + 1, :].astype(jnp.float32))
            weight = upright(weights_ref[b, k : k + 1, :])
            high = weight.astype(jnp.bfloat16).astype(jnp.float32)
            middle = (weight - high).astype(jnp.bfloat16).astype(jnp.float32)
            for place, piece in enumerate((high, middle, weight - high - middle)):
                at = here == place * top_count + k
                tile = jnp.where(at & on_ids, number, jnp.where(at & on_weights, piece, tile))
        parts = normed[:, :first], normed[:, first:]

        @pl.when(lower)
        def _():
            store(mine_ref, b, parts[0], tile)
            store(give_ref, b, parts[1], tile)

        @pl.when(jnp.logical_not(lower))
        def _():
            store(mine_ref, b, parts[1], tile)
            store(give_ref, b, parts[0], tile)


def prologue(places, hidden, gain, ids, weights):
    micro_count, tokens, width = hidden.shape
    held = split_widths(width)[2]
    return pl.pallas_call(
        functools.partial(prologue_body, tokens, ids.shape[1]),
        out_shape=[jax.ShapeDtypeStruct((micro_count, tokens, held), jnp.bfloat16)] * 2,
        in_specs=[SCALARS] + whole_arrays(4),
        out_specs=whole_arrays(2),
        compiler_params=pltpu.CompilerParams(vmem_limit_bytes=20 * 2**20),
    )(places, hidden, gain, ids, weights)


def local(hidden, norm_gain, w_gate, w_up, w_down, expert_ids, route_weight):
    micro_count, tokens, width = hidden.shape
    top_count = expert_ids.shape[2]
    devices = lax.axis_size("req")
    experts = devices // HSPLIT
    rounded = HSPLIT * ((3 * tokens * top_count + 2 * experts * HSPLIT - 1) // (2 * experts * HSPLIT))
    capacity = min(tokens, max(HSPLIT, rounded))
    distant = devices // 8
    first, second, held = split_widths(width)
    position = lax.axis_index("req")
    core = position & 1
    lower = core == 0
    expert = position // HSPLIT
    places = jnp.stack([core, expert, expert ^ core]).astype(jnp.int32)

    def join(*blocks):
        return jnp.concatenate(blocks, axis=0)

    mine, give = prologue(
        places, hidden, norm_gain.reshape(1, width), expert_ids.transpose(0, 2, 1), route_weight.transpose(0, 2, 1)
    )
    theirs = moved(give, other_core)
    pairs = [
        join(jnp.where(lower, mine[b], theirs[b]), jnp.where(lower, theirs[b], mine[b]))
        for b in range(micro_count)
    ]

    def tied(*arrays):
        return lax.optimization_barrier(arrays)

    def far_blocks(pair):
        return [moved(pair, far(j)) for j in range(1, distant)]

    def second_hop(state, earlier):
        following = moved(state["column"], first_axis)
        chosen = tokens, capacity
        (send,) = select(*chosen, 1, places, state["column"], following)
        if earlier is not None:
            send, earlier["arrived"] = tied(send, earlier["arrived"])
        state["arrived"] = moved(send, second_axis)
        state["own"], state["slots"] = select(*chosen, 0, places, state["column"], following)

    states = []
    gate_v, up_v, down_v = preload(pairs[0], w_gate.T, w_up.T, w_down)
    for pair in pairs:
        if states:
            last = states[-1]
            pair, last["column"] = tied(pair, last["column"])
        blocks = far_blocks(pair)
        if states:
            second_hop(last, states[-2] if len(states) > 1 else None)
            *blocks, last["own"] = tied(*blocks, last["own"])
        else:
            blocks[0], gate_v, up_v, down_v = tied(blocks[0], gate_v, up_v, down_v)
        states.append({"column": join(pair, *blocks)})
    second_hop(states[-1], states[-2] if len(states) > 1 else None)
    held_state = states

    outputs = []
    before = None
    for b in range(micro_count):
        state = held_state[b]
        own, arrived = state["own"], state["arrived"]
        if before is not None:
            arrived, *before = tied(arrived, *before)
            outputs[-1] = before
        before = ffn(
            places, own, arrived, moved(own, other_core), moved(arrived, other_core), gate_v, up_v, down_v
        )
        outputs.append(before)

    def collect(state, keep_near, keep_far, send_near, send_far):
        give = (keep_far + moved(send_far, other_core).astype(jnp.float32)).astype(jnp.bfloat16)
        arrived = moved(give, second_axis)
        near, following = merge(state["slots"], keep_near, moved(send_near, other_core), arrived)
        near = near + moved(following, first_axis).astype(jnp.float32)
        near = near.reshape(distant, 2 * tokens, held)
        summed = near[0]
        for j in range(1, distant):
            summed = summed + moved(near[j].astype(jnp.bfloat16), far(j)).astype(jnp.float32)
        return summed

    sums = jnp.stack([collect(state, *out) for state, out in zip(held_state, outputs)])
    own = jnp.where(lower, sums[:, :tokens], sums[:, tokens:])
    give = jnp.where(lower, sums[:, tokens:], sums[:, :tokens]).astype(jnp.bfloat16)
    taken = moved(give, other_core).astype(jnp.float32)
    mixture = jnp.concatenate(
        [jnp.where(lower, own, taken)[:, :, :first], jnp.where(lower, taken, own)[:, :, :second]], axis=2
    )
    return (hidden.astype(jnp.float32) + mixture).astype(jnp.bfloat16)


def solution(mesh):
    return jax.shard_map(
        local,
        mesh=mesh,
        in_specs=(
            P(None, ("groups", "req"), None),
            P(),
            P(None, "req"),
            P(None, "req"),
            P("req", None),
            P(None, ("groups", "req"), None),
            P(None, ("groups", "req"), None),
        ),
        out_specs=P(None, ("groups", "req"), None),
        check_vma=False,
    )
```

```python
import functools

import jax
import jax.numpy as jnp
from jax import lax
from jax.experimental import pallas as pl
from jax.experimental.pallas import tpu as pltpu
from jax.sharding import PartitionSpec as P

HSPLIT = 4
LANES = 128
ROUTING = 32

epsilon = 1e-05
swish_scale = 1.702

across = (((1,), (1,)), ((), ()))
downward = (((0,), (0,)), ((), ()))


def split_widths(width):
    first = width // 2 // LANES * LANES
    second = width - first
    held = -(-(second + ROUTING) // LANES) * LANES
    return first, second, held


def moved(block, partner):
    count = lax.axis_size("req")
    return lax.ppermute(block, "req", [(i, partner(i)) for i in range(count)])


def other_core(i):
    return i ^ 1


def first_axis(i):
    return i ^ (2 if i & 1 else 4)


def second_axis(i):
    return i ^ (4 if i & 1 else 2)


def far(step):
    return lambda i: i ^ (step << 3)


def whole_arrays(count):
    return [pl.BlockSpec(memory_space=pltpu.VMEM)] * count


SCALARS = pl.BlockSpec(memory_space=pltpu.SMEM)


def slots_of(tokens, capacity, base, places_ref, rows_ref):
    total, held = rows_ref.shape
    tile = rows_ref[:, held - LANES :].astype(jnp.float32)
    lane = lax.broadcasted_iota(jnp.int32, (total, LANES), 1)
    row = lax.broadcasted_iota(jnp.int32, (total, LANES), 0)
    listed = (lane >= LANES - ROUTING) & (lane < LANES - ROUTING // 2)

    def named(expert):
        return jnp.max(jnp.where(listed & (tile == expert.astype(jnp.float32)), 1.0, 0.0), axis=1, keepdims=True)

    mine, theirs = named(places_ref[1]), named(places_ref[2])
    marks = jnp.where(lane == 0, mine, jnp.where(lane == 1, theirs, 0.0))
    left = lax.broadcasted_iota(jnp.int32, (total, total), 0)
    right = lax.broadcasted_iota(jnp.int32, (total, total), 1)
    earlier = ((right < left) & (left // tokens == right // tokens)).astype(jnp.float32).astype(jnp.bfloat16)
    ahead = jnp.dot(earlier, marks.astype(jnp.bfloat16), preferred_element_type=jnp.float32)
    return jnp.where(marks > 0.0, ahead + (base + row // tokens * capacity).astype(jnp.float32), -1.0)


def locate_body(tokens, capacity, places_ref, rows_ref, slots_ref):
    slots_ref[...] = slots_of(tokens, capacity, 0, places_ref, rows_ref)


def locate(tokens, capacity, places, rows):
    return pl.pallas_call(
        functools.partial(locate_body, tokens, capacity),
        out_shape=jax.ShapeDtypeStruct((rows.shape[0], LANES), jnp.float32),
        in_specs=[SCALARS] + whole_arrays(1),
        out_specs=pl.BlockSpec(memory_space=pltpu.VMEM),
        compiler_params=pltpu.CompilerParams(vmem_limit_bytes=20 * 2**20),
    )(places, rows)


def select_body(tokens, capacity, wanted, places_ref, slots_ref, near_ref, next_ref, *out_refs):
    rows = near_ref.shape[0]
    compact = out_refs[0].shape[0]
    slots = slots_ref[...]
    next_slots = slots_of(tokens, capacity, rows // tokens * capacity, places_ref, next_ref)
    for next_slots_ref in out_refs[len(wanted) :]:
        next_slots_ref[...] = next_slots
    column = lax.broadcasted_iota(jnp.int32, (rows, compact), 1).astype(jnp.float32)
    for index, rows_ref in zip(wanted, out_refs):
        result = None
        for source, at in ((near_ref, slots), (next_ref, next_slots)):
            picks = (at[:, index : index + 1] == column).astype(jnp.float32).astype(jnp.bfloat16)
            part = lax.dot_general(picks, source[...], downward, preferred_element_type=jnp.float32)
            result = part if result is None else result + part
        rows_ref[...] = result.astype(jnp.bfloat16)


def select(tokens, capacity, wanted, places, slots, near, following):
    with_slots = int(0 in wanted)
    rows, held = near.shape
    compact = 2 * rows // tokens * capacity
    block = jax.ShapeDtypeStruct((compact, held), jnp.bfloat16)
    return pl.pallas_call(
        functools.partial(select_body, tokens, capacity, wanted),
        out_shape=[block] * len(wanted) + [jax.ShapeDtypeStruct((rows, LANES), jnp.float32)] * with_slots,
        in_specs=[SCALARS] + whole_arrays(3),
        out_specs=whole_arrays(len(wanted) + with_slots),
        compiler_params=pltpu.CompilerParams(vmem_limit_bytes=20 * 2**20),
        cost_estimate=pl.CostEstimate(flops=8 * rows * compact * held, bytes_accessed=8 * rows * held, transcendentals=0),
    )(places, slots, near, following)


def merge_body(wanted, near_slots_ref, next_slots_ref, keep_ref, taken_ref, arrived_ref, *out_refs):
    rows = out_refs[0].shape[0]
    compact = keep_ref.shape[0]
    column = lax.broadcasted_iota(jnp.int32, (rows, compact), 1).astype(jnp.float32)
    high = (keep_ref[...] + taken_ref[...].astype(jnp.float32)).astype(jnp.bfloat16)
    for part, out_ref in zip(wanted, out_refs):
        slots = (near_slots_ref, next_slots_ref)[part][...]
        result = jnp.zeros((rows, keep_ref.shape[1]), jnp.float32)
        for index, source in enumerate((high, arrived_ref[...])):
            picks = (slots[:, index : index + 1] == column).astype(jnp.float32).astype(jnp.bfloat16)
            result += jnp.dot(picks, source, preferred_element_type=jnp.float32)
        out_ref[...] = result.astype(out_ref.dtype)


def merge(wanted, types, slots, keep, taken, arrived):
    rows = slots[0].shape[0]
    compact, held = keep.shape
    return pl.pallas_call(
        functools.partial(merge_body, wanted),
        out_shape=[jax.ShapeDtypeStruct((rows, held), kind) for kind in types],
        in_specs=whole_arrays(5),
        out_specs=whole_arrays(len(types)),
        compiler_params=pltpu.CompilerParams(vmem_limit_bytes=20 * 2**20),
        cost_estimate=pl.CostEstimate(flops=8 * rows * compact * held, bytes_accessed=8 * rows * held, transcendentals=0),
    )(*slots, keep, taken, arrived)


def ffn_body(
    places_ref, mine_near_ref, mine_far_ref, other_near_ref, other_far_ref, gate_v, up_v, down_v,
    keep_near_ref, keep_far_ref, send_near_ref, send_far_ref, rows_v, act_v,
):
    hidden, width = gate_v.shape
    first, second, held = split_widths(width)
    pair = mine_near_ref.shape[0]
    quad = pair // 2
    chunk = hidden // 3
    def lay(near, far_ref, swapped, start, size):
        for place in range(4):
            if swapped:
                source, block = (near, far_ref)[place % 2], place // 2
            else:
                source, block = (near, far_ref)[place // 2], place % 2
            rows_v[pl.ds(place * quad, quad), start : start + size] = source[pl.ds(block * quad, quad), :size]

    lower = places_ref[0] == 0

    @pl.when(lower)
    def _():
        lay(mine_near_ref, mine_far_ref, False, 0, first)
        lay(other_near_ref, other_far_ref, True, first, second)

    @pl.when(jnp.logical_not(lower))
    def _():
        lay(other_near_ref, other_far_ref, True, 0, first)
        lay(mine_near_ref, mine_far_ref, False, first, second)

    tile = jnp.concatenate([mine_near_ref[:, held - LANES :], mine_far_ref[:, held - LANES :]], axis=0)
    tile = tile.astype(jnp.float32)
    lane = lax.broadcasted_iota(jnp.int32, (2 * pair, LANES), 1)
    listed = (lane >= LANES - ROUTING) & (lane < LANES - ROUTING // 2)
    chosen = listed & (tile == places_ref[1].astype(jnp.float32))
    weight = jnp.sum(
        jnp.where(chosen, pltpu.roll(tile, LANES - ROUTING // 2, 1), 0.0), axis=1, keepdims=True
    )

    for part in range(3):
        there = slice(part * chunk, (part + 1) * chunk)
        gate = lax.dot_general(rows_v[...], gate_v[there, :], across, preferred_element_type=jnp.float32)
        up = lax.dot_general(rows_v[...], up_v[there, :], across, preferred_element_type=jnp.float32)
        act_v[:, there] = ((up + 1.0) * gate * jax.nn.sigmoid(swish_scale * gate)).astype(jnp.bfloat16)

    def keep_half(result, size):
        keep_near_ref[:, :size] = result[:pair]
        keep_far_ref[:, :size] = result[pair:]
        if size < held:
            keep_near_ref[:, size:] = jnp.zeros((pair, held - size), jnp.float32)
            keep_far_ref[:, size:] = jnp.zeros((pair, held - size), jnp.float32)

    def send_half(result, size):
        result = result.astype(jnp.bfloat16)
        for place in range(4):
            target, block = (send_near_ref, send_far_ref)[place % 2], place // 2
            target[pl.ds(block * quad, quad), :size] = result[place * quad : (place + 1) * quad]
        if size < held:
            send_near_ref[:, size:] = jnp.zeros((pair, held - size), jnp.bfloat16)
            send_far_ref[:, size:] = jnp.zeros((pair, held - size), jnp.bfloat16)

    low = weight * jnp.dot(act_v[...], down_v[:, :first], preferred_element_type=jnp.float32)

    @pl.when(lower)
    def _():
        keep_half(low, first)

    @pl.when(jnp.logical_not(lower))
    def _():
        send_half(low, first)

    high = weight * jnp.dot(act_v[...], down_v[:, first:], preferred_element_type=jnp.float32)

    @pl.when(lower)
    def _():
        send_half(high, second)

    @pl.when(jnp.logical_not(lower))
    def _():
        keep_half(high, second)


def ffn(places, mine_near, mine_far, other_near, other_far, gate_t, up_t, w_down):
    pair, held = mine_near.shape
    hidden, width = gate_t.shape
    total = 2 * pair
    return pl.pallas_call(
        ffn_body,
        out_shape=[jax.ShapeDtypeStruct((pair, held), jnp.float32)] * 2
        + [jax.ShapeDtypeStruct((pair, held), jnp.bfloat16)] * 2,
        in_specs=[SCALARS] + whole_arrays(7),
        out_specs=whole_arrays(4),
        scratch_shapes=[
            pltpu.VMEM((total, width), jnp.bfloat16),
            pltpu.VMEM((total, hidden), jnp.bfloat16),
        ],
        compiler_params=pltpu.CompilerParams(vmem_limit_bytes=20 * 2**20),
        cost_estimate=pl.CostEstimate(
            flops=6 * total * width * hidden,
            bytes_accessed=6 * width * hidden + 8 * total * held,
            transcendentals=total * hidden,
        ),
    )(places, mine_near, mine_far, other_near, other_far, gate_t, up_t, w_down)


def preload_body(_, *refs):
    count = (len(refs) - 1) // 2
    sems = refs[-1]
    copies = [pltpu.make_async_copy(refs[i], refs[count + i], sems.at[i]) for i in range(count)]
    for copy in copies:
        copy.start()
    for copy in copies:
        copy.wait()


def preload(token, *arrays):
    return pl.pallas_call(
        preload_body,
        out_shape=[pltpu.VMEM(a.shape, a.dtype) for a in arrays],
        in_specs=[pl.BlockSpec(memory_space=pl.ANY)] + [pl.BlockSpec(memory_space=pltpu.HBM)] * len(arrays),
        out_specs=whole_arrays(len(arrays)),
        scratch_shapes=[pltpu.SemaphoreType.DMA((len(arrays),))],
        compiler_params=pltpu.CompilerParams(vmem_limit_bytes=20 * 2**20),
    )(token, *arrays)


def prologue_body(
    tokens, top_count, places_ref, hidden_ref, gain_ref, routing_ref, mine_ref, give_ref
):
    micro_count, _, width = hidden_ref.shape
    first, second, held = split_widths(width)
    lane = lax.broadcasted_iota(jnp.int32, (tokens, LANES), 1)
    here = lane % (ROUTING // 2)
    on_ids = (lane >= LANES - ROUTING) & (lane < LANES - ROUTING // 2)
    on_weights = lane >= LANES - ROUTING // 2
    diagonal = lax.broadcasted_iota(jnp.int32, (tokens, tokens), 0) == lax.broadcasted_iota(
        jnp.int32, (tokens, tokens), 1
    )

    def upright(line):
        return jnp.sum(jnp.where(diagonal, line, 0.0), axis=1, keepdims=True)

    def store(ref, b, part, tile):
        size = part.shape[1]
        inside = size // LANES * LANES
        ref[b, :, :inside] = part[:, :inside].astype(jnp.bfloat16)
        if inside < size:
            rest = jnp.concatenate([part[:, inside:], jnp.zeros((tokens, LANES - size + inside), jnp.float32)], axis=1)
            tile = jnp.where(lane < size - inside, rest, tile)
        ref[b, :, inside:] = tile.astype(jnp.bfloat16)

    lower = places_ref[0] == 0
    for b in range(micro_count):
        residual = hidden_ref[b].astype(jnp.float32)
        scale = lax.rsqrt(jnp.mean(residual * residual, axis=-1, keepdims=True) + epsilon)
        normed = residual * scale * gain_ref[...].astype(jnp.float32)
        tile = jnp.where(on_ids, -1.0, 0.0)
        for k in range(top_count):
            number = upright(routing_ref[b, k : k + 1, :])
            weight = upright(routing_ref[b, top_count + k : top_count + k + 1, :])
            high = weight.astype(jnp.bfloat16).astype(jnp.float32)
            middle = (weight - high).astype(jnp.bfloat16).astype(jnp.float32)
            for place, piece in enumerate((high, middle, weight - high - middle)):
                at = here == place * top_count + k
                tile = jnp.where(at & on_ids, number, jnp.where(at & on_weights, piece, tile))
        parts = normed[:, :first], normed[:, first:]

        @pl.when(lower)
        def _():
            store(mine_ref, b, parts[0], tile)
            store(give_ref, b, parts[1], tile)

        @pl.when(jnp.logical_not(lower))
        def _():
            store(mine_ref, b, parts[1], tile)
            store(give_ref, b, parts[0], tile)


def prologue(places, hidden, gain, routing):
    micro_count, tokens, width = hidden.shape
    held = split_widths(width)[2]
    return pl.pallas_call(
        functools.partial(prologue_body, tokens, routing.shape[1] // 2),
        out_shape=[jax.ShapeDtypeStruct((micro_count, tokens, held), jnp.bfloat16)] * 2,
        in_specs=[SCALARS] + whole_arrays(3),
        out_specs=whole_arrays(2),
        compiler_params=pltpu.CompilerParams(vmem_limit_bytes=20 * 2**20),
    )(places, hidden, gain, routing)


def local(hidden, norm_gain, w_gate, w_up, w_down, expert_ids, route_weight):
    micro_count, tokens, width = hidden.shape
    top_count = expert_ids.shape[2]
    devices = lax.axis_size("req")
    experts = devices // HSPLIT
    rounded = HSPLIT * ((3 * tokens * top_count + 2 * experts * HSPLIT - 1) // (2 * experts * HSPLIT))
    capacity = min(tokens, max(HSPLIT, rounded))
    distant = devices // 8
    first, second, held = split_widths(width)
    position = lax.axis_index("req")
    core = position & 1
    lower = core == 0
    expert = position // HSPLIT
    places = jnp.stack([core, expert, expert ^ core]).astype(jnp.int32)

    def join(*blocks):
        return jnp.concatenate(blocks, axis=0)

    routing = jnp.concatenate(
        [expert_ids.transpose(0, 2, 1).astype(jnp.float32), route_weight.transpose(0, 2, 1)], axis=1
    )
    mine, give = prologue(places, hidden, norm_gain.reshape(1, width), routing)
    theirs = moved(give, other_core)
    pairs = [
        join(jnp.where(lower, mine[b], theirs[b]), jnp.where(lower, theirs[b], mine[b]))
        for b in range(micro_count)
    ]

    def tied(*arrays):
        return lax.optimization_barrier(arrays)

    def far_blocks(pair):
        return [moved(pair, far(j)) for j in range(1, distant)]

    def second_hop(state, earlier, apart):
        chosen = tokens, capacity
        near, following = state["near"], state["next"]
        slots = state["slots"]
        if apart:
            (send,) = select(*chosen, (1,), places, slots, near, following)
        else:
            send, state["own"], next_slots = select(*chosen, (1, 0), places, slots, near, following)
        if earlier is not None:
            send, earlier["arrived"] = tied(send, earlier["arrived"])
        state["arrived"] = moved(send, second_axis)
        if apart:
            following, _ = tied(following, send)
            state["own"], next_slots = select(*chosen, (0,), places, state["twin"], near, following)
        state["slots"] = slots, next_slots

    states = []
    gate_v, up_v, down_v = preload(pairs[0], w_gate.T, w_up.T, w_down)
    beside = [moved(pair, first_axis) for pair in pairs[1:]]
    blocks = far_blocks(pairs[0])
    blocks[0], gate_v, up_v, down_v, *beside = tied(blocks[0], gate_v, up_v, down_v, *beside)
    column = join(pairs[0], *blocks)
    states.append(
        {"near": column, "next": moved(column, first_axis), "slots": locate(tokens, capacity, places, column)}
    )
    side = 2 * tokens
    for b in range(1, micro_count):
        last = states[-1]
        both, last["twin"] = tied(join(pairs[b], beside[b - 1]), moved(last["slots"], other_core))
        blocks = far_blocks(both)
        second_hop(last, states[-2] if len(states) > 1 else None, True)
        *blocks, last["own"] = tied(*blocks, last["own"])
        blocks = [both] + blocks
        near, following = join(*[block[:side] for block in blocks]), join(*[block[side:] for block in blocks])
        states.append({"near": near, "next": following, "slots": locate(tokens, capacity, places, near)})
    second_hop(states[-1], states[-2] if len(states) > 1 else None, False)

    hops = []
    for b, state in enumerate(states):
        own, arrived = state["own"], state["arrived"]
        other_far = moved(arrived, other_core)
        if b:
            other_far, hops[-1]["give"] = tied(other_far, hops[-1]["give"])
        keep_near, keep_far, send_near, send_far = ffn(
            places, own, arrived, moved(own, other_core), other_far, gate_v, up_v, down_v
        )
        if b + 1 < micro_count:
            send_far, states[b + 1]["arrived"] = tied(send_far, states[b + 1]["arrived"])
        if b:
            send_far, hops[-1]["arrived"] = tied(send_far, hops[-1]["arrived"])
        give = (keep_far + moved(send_far, other_core).astype(jnp.float32)).astype(jnp.bfloat16)
        hops.append(
            {"keep": keep_near, "taken": moved(send_near, other_core), "give": give, "arrived": moved(give, second_axis)}
        )

    def far_sum(block):
        block = block.reshape(distant, -1, held)
        arrivals = [moved(block[j].astype(jnp.bfloat16), far(j)) for j in range(1, distant)]
        return block[0], arrivals

    def total(kept, arrivals):
        for arrival in arrivals:
            kept = kept + arrival.astype(jnp.float32)
        return kept

    count = len(hops)
    for b in range(1, count):
        hops[b - 1]["taken"], hops[b]["give"] = tied(hops[b - 1]["taken"], hops[b]["give"])
    sums = [None] * count
    waiting = None
    for b, (state, hop) in enumerate(zip(states, hops)):
        final = b == count - 1
        parts = state["slots"], hop["keep"], hop["taken"], hop["arrived"]
        if final:
            (following,) = merge((1,), (jnp.bfloat16,), *parts)
            taken, _ = tied(parts[2], following)
            (near,) = merge((0,), (jnp.float32,), parts[0], parts[1], taken, parts[3])
            if waiting is not None:
                *arrivals, near = tied(*waiting[1], near)
                waiting = waiting[0], arrivals
            near = total(near, [moved(following, first_axis)])
            kept, arrivals = far_sum(near)
            sums[b] = total(kept, arrivals)
        if waiting is not None:
            settled = total(*waiting)
            sums[b - 1] = total(settled[:side], [moved(settled[side:].astype(jnp.bfloat16), first_axis)])
            waiting = None
        if not final:
            near, following = merge((0, 1), (jnp.float32, jnp.float32), *parts)
            waiting = far_sum(
                jnp.concatenate([near.reshape(distant, side, held), following.reshape(distant, side, held)], axis=1)
            )
    sums = jnp.stack(sums)
    own = jnp.where(lower, sums[:, :tokens], sums[:, tokens:])
    give = jnp.where(lower, sums[:, tokens:], sums[:, :tokens]).astype(jnp.bfloat16)
    taken = moved(give, other_core).astype(jnp.float32)
    mixture = jnp.concatenate(
        [jnp.where(lower, own, taken)[:, :, :first], jnp.where(lower, taken, own)[:, :, :second]], axis=2
    )
    return (hidden.astype(jnp.float32) + mixture).astype(jnp.bfloat16)


def solution(mesh):
    return jax.shard_map(
        local,
        mesh=mesh,
        in_specs=(
            P(None, ("groups", "req"), None),
            P(),
            P(None, "req"),
            P(None, "req"),
            P("req", None),
            P(None, ("groups", "req"), None),
            P(None, ("groups", "req"), None),
        ),
        out_specs=P(None, ("groups", "req"), None),
        check_vma=False,
    )
```

```python
import functools

import jax
import jax.numpy as jnp
from jax import lax
from jax.experimental import pallas as pl
from jax.experimental.pallas import tpu as pltpu
from jax.sharding import PartitionSpec as P

HSPLIT = 4
LANES = 128
ROUTING = 32

epsilon = 1e-05
swish_scale = 1.702

across = (((1,), (1,)), ((), ()))
downward = (((0,), (0,)), ((), ()))


def split_widths(width):
    first = width // 2 // LANES * LANES
    second = width - first
    held = -(-(second + ROUTING) // LANES) * LANES
    return first, second, held


def moved(block, partner):
    count = lax.axis_size("req")
    return lax.ppermute(block, "req", [(i, partner(i)) for i in range(count)])


def other_core(i):
    return i ^ 1


def first_axis(i):
    return i ^ (2 if i & 1 else 4)


def second_axis(i):
    return i ^ (4 if i & 1 else 2)


def far(step):
    return lambda i: i ^ (step << 3)


def whole_arrays(count):
    return [pl.BlockSpec(memory_space=pltpu.VMEM)] * count


SCALARS = pl.BlockSpec(memory_space=pltpu.SMEM)


def slots_of(tokens, capacity, base, places_ref, rows_ref):
    total, held = rows_ref.shape
    tile = rows_ref[:, held - LANES :].astype(jnp.float32)
    lane = lax.broadcasted_iota(jnp.int32, (total, LANES), 1)
    row = lax.broadcasted_iota(jnp.int32, (total, LANES), 0)
    listed = (lane >= LANES - ROUTING) & (lane < LANES - ROUTING // 2)

    def named(expert):
        return jnp.max(jnp.where(listed & (tile == expert.astype(jnp.float32)), 1.0, 0.0), axis=1, keepdims=True)

    mine, theirs = named(places_ref[1]), named(places_ref[2])
    marks = jnp.where(lane == 0, mine, jnp.where(lane == 1, theirs, 0.0))
    left = lax.broadcasted_iota(jnp.int32, (total, total), 0)
    right = lax.broadcasted_iota(jnp.int32, (total, total), 1)
    earlier = ((right < left) & (left // tokens == right // tokens)).astype(jnp.float32).astype(jnp.bfloat16)
    ahead = jnp.dot(earlier, marks.astype(jnp.bfloat16), preferred_element_type=jnp.float32)
    return jnp.where(marks > 0.0, ahead + (base + row // tokens * capacity).astype(jnp.float32), -1.0)


def select_body(tokens, capacity, wanted, places_ref, near_ref, next_ref, *out_refs):
    rows = near_ref.shape[0]
    compact = out_refs[0].shape[0]
    slots = [
        slots_of(tokens, capacity, part * (rows // tokens * capacity), places_ref, ref)
        for part, ref in enumerate((near_ref, next_ref))
    ]
    for part, slots_ref in enumerate(out_refs[len(wanted) :]):
        slots_ref[...] = slots[part]
    column = lax.broadcasted_iota(jnp.int32, (rows, compact), 1).astype(jnp.float32)
    for index, rows_ref in zip(wanted, out_refs):
        result = None
        for source, at in zip((near_ref, next_ref), slots):
            picks = (at[:, index : index + 1] == column).astype(jnp.float32).astype(jnp.bfloat16)
            part = lax.dot_general(picks, source[...], downward, preferred_element_type=jnp.float32)
            result = part if result is None else result + part
        rows_ref[...] = result.astype(jnp.bfloat16)


def select(tokens, capacity, wanted, places, near, following):
    located = 2 * int(0 in wanted)
    rows, held = near.shape
    compact = 2 * rows // tokens * capacity
    block = jax.ShapeDtypeStruct((compact, held), jnp.bfloat16)
    return pl.pallas_call(
        functools.partial(select_body, tokens, capacity, wanted),
        out_shape=[block] * len(wanted) + [jax.ShapeDtypeStruct((rows, LANES), jnp.float32)] * located,
        in_specs=[SCALARS] + whole_arrays(2),
        out_specs=whole_arrays(len(wanted) + located),
        compiler_params=pltpu.CompilerParams(vmem_limit_bytes=20 * 2**20),
        cost_estimate=pl.CostEstimate(flops=8 * rows * compact * held, bytes_accessed=8 * rows * held, transcendentals=0),
    )(places, near, following)


def merge_body(wanted, near_slots_ref, next_slots_ref, keep_ref, taken_ref, arrived_ref, *out_refs):
    rows = out_refs[0].shape[0]
    compact = keep_ref.shape[0]
    column = lax.broadcasted_iota(jnp.int32, (rows, compact), 1).astype(jnp.float32)
    high = (keep_ref[...] + taken_ref[...].astype(jnp.float32)).astype(jnp.bfloat16)
    for part, out_ref in zip(wanted, out_refs):
        slots = (near_slots_ref, next_slots_ref)[part][...]
        result = jnp.zeros((rows, keep_ref.shape[1]), jnp.float32)
        for index, source in enumerate((high, arrived_ref[...])):
            picks = (slots[:, index : index + 1] == column).astype(jnp.float32).astype(jnp.bfloat16)
            result += jnp.dot(picks, source, preferred_element_type=jnp.float32)
        out_ref[...] = result.astype(out_ref.dtype)


def merge(wanted, types, slots, keep, taken, arrived):
    rows = slots[0].shape[0]
    compact, held = keep.shape
    return pl.pallas_call(
        functools.partial(merge_body, wanted),
        out_shape=[jax.ShapeDtypeStruct((rows, held), kind) for kind in types],
        in_specs=whole_arrays(5),
        out_specs=whole_arrays(len(types)),
        compiler_params=pltpu.CompilerParams(vmem_limit_bytes=20 * 2**20),
        cost_estimate=pl.CostEstimate(flops=8 * rows * compact * held, bytes_accessed=8 * rows * held, transcendentals=0),
    )(*slots, keep, taken, arrived)


def ffn_body(
    places_ref, mine_near_ref, mine_far_ref, other_near_ref, other_far_ref, gate_v, up_v, down_v,
    keep_near_ref, keep_far_ref, send_near_ref, send_far_ref, rows_v, act_v,
):
    hidden, width = gate_v.shape
    first, second, held = split_widths(width)
    pair = mine_near_ref.shape[0]
    quad = pair // 2
    chunk = hidden // 3
    def lay(near, far_ref, swapped, start, size):
        for place in range(4):
            if swapped:
                source, block = (near, far_ref)[place % 2], place // 2
            else:
                source, block = (near, far_ref)[place // 2], place % 2
            rows_v[pl.ds(place * quad, quad), start : start + size] = source[pl.ds(block * quad, quad), :size]

    lower = places_ref[0] == 0

    @pl.when(lower)
    def _():
        lay(mine_near_ref, mine_far_ref, False, 0, first)
        lay(other_near_ref, other_far_ref, True, first, second)

    @pl.when(jnp.logical_not(lower))
    def _():
        lay(other_near_ref, other_far_ref, True, 0, first)
        lay(mine_near_ref, mine_far_ref, False, first, second)

    tile = jnp.concatenate([mine_near_ref[:, held - LANES :], mine_far_ref[:, held - LANES :]], axis=0)
    tile = tile.astype(jnp.float32)
    lane = lax.broadcasted_iota(jnp.int32, (2 * pair, LANES), 1)
    listed = (lane >= LANES - ROUTING) & (lane < LANES - ROUTING // 2)
    chosen = listed & (tile == places_ref[1].astype(jnp.float32))
    weight = jnp.sum(
        jnp.where(chosen, pltpu.roll(tile, LANES - ROUTING // 2, 1), 0.0), axis=1, keepdims=True
    )

    for part in range(3):
        there = slice(part * chunk, (part + 1) * chunk)
        gate = lax.dot_general(rows_v[...], gate_v[there, :], across, preferred_element_type=jnp.float32)
        up = lax.dot_general(rows_v[...], up_v[there, :], across, preferred_element_type=jnp.float32)
        act_v[:, there] = ((up + 1.0) * gate * jax.nn.sigmoid(swish_scale * gate)).astype(jnp.bfloat16)

    def keep_half(result, size):
        keep_near_ref[:, :size] = result[:pair]
        keep_far_ref[:, :size] = result[pair:]
        if size < held:
            keep_near_ref[:, size:] = jnp.zeros((pair, held - size), jnp.float32)
            keep_far_ref[:, size:] = jnp.zeros((pair, held - size), jnp.float32)

    def send_half(result, size):
        result = result.astype(jnp.bfloat16)
        for place in range(4):
            target, block = (send_near_ref, send_far_ref)[place % 2], place // 2
            target[pl.ds(block * quad, quad), :size] = result[place * quad : (place + 1) * quad]
        if size < held:
            send_near_ref[:, size:] = jnp.zeros((pair, held - size), jnp.bfloat16)
            send_far_ref[:, size:] = jnp.zeros((pair, held - size), jnp.bfloat16)

    low = weight * jnp.dot(act_v[...], down_v[:, :first], preferred_element_type=jnp.float32)

    @pl.when(lower)
    def _():
        keep_half(low, first)

    @pl.when(jnp.logical_not(lower))
    def _():
        send_half(low, first)

    high = weight * jnp.dot(act_v[...], down_v[:, first:], preferred_element_type=jnp.float32)

    @pl.when(lower)
    def _():
        send_half(high, second)

    @pl.when(jnp.logical_not(lower))
    def _():
        keep_half(high, second)


def ffn(places, mine_near, mine_far, other_near, other_far, gate_t, up_t, w_down):
    pair, held = mine_near.shape
    hidden, width = gate_t.shape
    total = 2 * pair
    return pl.pallas_call(
        ffn_body,
        out_shape=[jax.ShapeDtypeStruct((pair, held), jnp.float32)] * 2
        + [jax.ShapeDtypeStruct((pair, held), jnp.bfloat16)] * 2,
        in_specs=[SCALARS] + whole_arrays(7),
        out_specs=whole_arrays(4),
        scratch_shapes=[
            pltpu.VMEM((total, width), jnp.bfloat16),
            pltpu.VMEM((total, hidden), jnp.bfloat16),
        ],
        compiler_params=pltpu.CompilerParams(vmem_limit_bytes=20 * 2**20),
        cost_estimate=pl.CostEstimate(
            flops=6 * total * width * hidden,
            bytes_accessed=6 * width * hidden + 8 * total * held,
            transcendentals=total * hidden,
        ),
    )(places, mine_near, mine_far, other_near, other_far, gate_t, up_t, w_down)


def preload_body(_, *refs):
    count = (len(refs) - 1) // 2
    sems = refs[-1]
    copies = [pltpu.make_async_copy(refs[i], refs[count + i], sems.at[i]) for i in range(count)]
    for copy in copies:
        copy.start()
    for copy in copies:
        copy.wait()


def preload(token, *arrays):
    return pl.pallas_call(
        preload_body,
        out_shape=[pltpu.VMEM(a.shape, a.dtype) for a in arrays],
        in_specs=[pl.BlockSpec(memory_space=pl.ANY)] + [pl.BlockSpec(memory_space=pltpu.HBM)] * len(arrays),
        out_specs=whole_arrays(len(arrays)),
        scratch_shapes=[pltpu.SemaphoreType.DMA((len(arrays),))],
        compiler_params=pltpu.CompilerParams(vmem_limit_bytes=20 * 2**20),
    )(token, *arrays)


def prologue_body(top_count, places_ref, hidden_ref, packed_ref, mine_ref, give_ref):
    micro_count, tokens, width = hidden_ref.shape
    first, second, held = split_widths(width)
    start = -(-width // LANES) * LANES
    lane = lax.broadcasted_iota(jnp.int32, (tokens, LANES), 1)
    row = lax.broadcasted_iota(jnp.int32, (tokens, LANES), 0)
    here = lane % (ROUTING // 2)
    on_ids = (lane >= LANES - ROUTING) & (lane < LANES - ROUTING // 2)
    on_weights = lane >= LANES - ROUTING // 2

    def upright(place):
        at = start + place * tokens
        line = packed_ref[:, at // LANES * LANES : at // LANES * LANES + LANES]
        return jnp.sum(jnp.where(lane == row + at % LANES, line, 0.0), axis=1, keepdims=True)

    def store(ref, b, part, tile):
        size = part.shape[1]
        inside = size // LANES * LANES
        ref[b, :, :inside] = part[:, :inside].astype(jnp.bfloat16)
        if inside < size:
            rest = jnp.concatenate([part[:, inside:], jnp.zeros((tokens, LANES - size + inside), jnp.float32)], axis=1)
            tile = jnp.where(lane < size - inside, rest, tile)
        ref[b, :, inside:] = tile.astype(jnp.bfloat16)

    lower = places_ref[0] == 0
    for b in range(micro_count):
        residual = hidden_ref[b].astype(jnp.float32)
        scale = lax.rsqrt(jnp.mean(residual * residual, axis=-1, keepdims=True) + epsilon)
        normed = residual * scale * packed_ref[:, :width]
        tile = jnp.where(on_ids, -1.0, 0.0)
        for k in range(top_count):
            number = upright(b * top_count + k)
            weight = upright((micro_count + b) * top_count + k)
            high = weight.astype(jnp.bfloat16).astype(jnp.float32)
            middle = (weight - high).astype(jnp.bfloat16).astype(jnp.float32)
            for place, piece in enumerate((high, middle, weight - high - middle)):
                at = here == place * top_count + k
                tile = jnp.where(at & on_ids, number, jnp.where(at & on_weights, piece, tile))
        parts = normed[:, :first], normed[:, first:]

        @pl.when(lower)
        def _():
            store(mine_ref, b, parts[0], tile)
            store(give_ref, b, parts[1], tile)

        @pl.when(jnp.logical_not(lower))
        def _():
            store(mine_ref, b, parts[1], tile)
            store(give_ref, b, parts[0], tile)


def prologue(places, hidden, gain, ids, weights):
    micro_count, tokens, width = hidden.shape
    top_count = ids.shape[2]
    held = split_widths(width)[2]
    packed = jnp.concatenate(
        [
            jnp.pad(gain.astype(jnp.float32), (0, -width % LANES)),
            ids.transpose(0, 2, 1).reshape(-1).astype(jnp.float32),
            weights.transpose(0, 2, 1).reshape(-1),
        ]
    )
    packed = jnp.pad(packed, (0, -packed.shape[0] % LANES)).reshape(1, -1)
    return pl.pallas_call(
        functools.partial(prologue_body, top_count),
        out_shape=[jax.ShapeDtypeStruct((micro_count, tokens, held), jnp.bfloat16)] * 2,
        in_specs=[SCALARS] + whole_arrays(2),
        out_specs=whole_arrays(2),
        compiler_params=pltpu.CompilerParams(vmem_limit_bytes=20 * 2**20),
    )(places, hidden, packed)


def local(hidden, norm_gain, w_gate, w_up, w_down, expert_ids, route_weight):
    micro_count, tokens, width = hidden.shape
    top_count = expert_ids.shape[2]
    devices = lax.axis_size("req")
    experts = devices // HSPLIT
    rounded = HSPLIT * ((3 * tokens * top_count + 2 * experts * HSPLIT - 1) // (2 * experts * HSPLIT))
    capacity = min(tokens, max(HSPLIT, rounded))
    distant = devices // 8
    first, second, held = split_widths(width)
    position = lax.axis_index("req")
    core = position & 1
    lower = core == 0
    expert = position // HSPLIT
    places = jnp.stack([core, expert, expert ^ core]).astype(jnp.int32)

    def join(*blocks):
        return jnp.concatenate(blocks, axis=0)

    mine, give = prologue(places, hidden, norm_gain, expert_ids, route_weight)
    theirs = moved(give, other_core)
    pairs = [
        join(jnp.where(lower, mine[b], theirs[b]), jnp.where(lower, theirs[b], mine[b]))
        for b in range(micro_count)
    ]

    def tied(*arrays):
        return lax.optimization_barrier(arrays)

    def far_blocks(pair):
        return [moved(pair, far(j)) for j in range(1, distant)]

    chosen = tokens, capacity
    states = []

    def second_hop(state, apart):
        near, following = state["near"], state["next"]
        if apart:
            (send,) = select(*chosen, (1,), places, near, following)
        else:
            send, state["own"], *state["slots"] = select(*chosen, (1, 0), places, near, following)
        if len(states) > 1:
            send, states[-2]["arrived"] = tied(send, states[-2]["arrived"])
        state["arrived"] = moved(send, second_axis)
        if apart:
            following, _ = tied(following, send)
            state["own"], *state["slots"] = select(*chosen, (0,), places, near, following)

    pair = pairs[0]
    (gate_v,) = preload(pair, w_gate.T)
    if distant == 4:
        crossed, beside = moved(pair, far(2)), moved(pair, far(1))
        crossed, gate_v = tied(crossed, gate_v)
        (up_v,) = preload(crossed, w_up.T)
        passed = moved(crossed, far(1))
        passed, up_v = tied(passed, up_v)
        blocks = [beside, crossed, passed]
    else:
        (up_v,) = preload(pair, w_up.T)
        blocks = far_blocks(pair)
    column = join(pair, *blocks)
    states.append({"near": column, "next": moved(column, first_axis)})
    down_v = None
    for pair in pairs[1:]:
        last = states[-1]
        pair, last["near"] = tied(pair, last["near"])
        blocks = far_blocks(pair)
        second_hop(last, True)
        *blocks, last["own"] = tied(*blocks, last["own"])
        column = join(pair, *blocks)
        following = moved(column, first_axis)
        if down_v is None:
            (down_v,) = preload(last["own"], w_down)
            following, down_v = tied(following, down_v)
        states.append({"near": column, "next": following})
    second_hop(states[-1], False)
    if down_v is None:
        (down_v,) = preload(states[-1]["own"], w_down)

    hops = []
    before = None
    for state in states:
        own, arrived = state["own"], state["arrived"]
        if before is not None:
            arrived, *before = tied(arrived, *before)
            hops.append(before)
        before = ffn(places, own, arrived, moved(own, other_core), moved(arrived, other_core), gate_v, up_v, down_v)
    hops.append(before)

    def rounded_sum(a, b):
        return (a + b.astype(jnp.float32)).astype(jnp.bfloat16)

    def far_total(block, earlier):
        block = block.reshape(distant, -1, held)
        if distant == 4:
            if earlier:
                block, earlier[-1]["crossing"] = tied(block, earlier[-1]["crossing"])
            through = moved(block[3].astype(jnp.bfloat16), far(1))
            beside = moved(block[1].astype(jnp.bfloat16), far(1))
            return {"kept": block[0], "arrivals": [beside], "crossing": rounded_sum(block[2], through)}
        return {
            "kept": block[0],
            "arrivals": [moved(block[j].astype(jnp.bfloat16), far(j)) for j in range(1, distant)],
            "crossing": None,
        }

    def settled(total):
        kept, arrivals = total["kept"], list(total["arrivals"])
        if total["crossing"] is not None:
            arrivals.append(moved(total["crossing"], far(2)))
        for arrival in arrivals:
            kept = kept + arrival.astype(jnp.float32)
        return kept

    sums = []
    for state, (keep_near, keep_far, send_near, send_far) in zip(states, hops):
        give = rounded_sum(keep_far, moved(send_far, other_core))
        near, following = merge(
            (0, 1), (jnp.float32, jnp.bfloat16), state["slots"], keep_near, moved(send_near, other_core),
            moved(give, second_axis),
        )
        near = near + moved(following, first_axis).astype(jnp.float32)
        sums.append(far_total(near, sums))
    sums = jnp.stack([settled(total) for total in sums])
    own = jnp.where(lower, sums[:, :tokens], sums[:, tokens:])
    give = jnp.where(lower, sums[:, tokens:], sums[:, :tokens]).astype(jnp.bfloat16)
    taken = moved(give, other_core).astype(jnp.float32)
    mixture = jnp.concatenate(
        [jnp.where(lower, own, taken)[:, :, :first], jnp.where(lower, taken, own)[:, :, :second]], axis=2
    )
    return (hidden.astype(jnp.float32) + mixture).astype(jnp.bfloat16)


def solution(mesh):
    return jax.shard_map(
        local,
        mesh=mesh,
        in_specs=(
            P(None, ("groups", "req"), None),
            P(),
            P(None, "req"),
            P(None, "req"),
            P("req", None),
            P(None, ("groups", "req"), None),
            P(None, ("groups", "req"), None),
        ),
        out_specs=P(None, ("groups", "req"), None),
        check_vma=False,
    )
```

```python
import functools

import jax
import jax.numpy as jnp
from jax import lax
from jax.experimental import pallas as pl
from jax.experimental.pallas import tpu as pltpu
from jax.sharding import PartitionSpec as P

HSPLIT = 4
LANES = 128
ROUTING = 32

epsilon = 1e-05
swish_scale = 1.702

across = (((1,), (1,)), ((), ()))
downward = (((0,), (0,)), ((), ()))


def split_widths(width):
    first = width // 2 // LANES * LANES
    second = width - first
    held = -(-(second + ROUTING) // LANES) * LANES
    return first, second, held


def moved(block, partner):
    count = lax.axis_size("req")
    return lax.ppermute(block, "req", [(i, partner(i)) for i in range(count)])


def other_core(i):
    return i ^ 1


def first_axis(i):
    return i ^ (2 if i & 1 else 4)


def second_axis(i):
    return i ^ (4 if i & 1 else 2)


def far(step):
    return lambda i: i ^ (step << 3)


def whole_arrays(count):
    return [pl.BlockSpec(memory_space=pltpu.VMEM)] * count


SCALARS = pl.BlockSpec(memory_space=pltpu.SMEM)


def slots_of(tokens, capacity, base, places_ref, tile):
    total = tile.shape[0]
    tile = tile.astype(jnp.float32)
    lane = lax.broadcasted_iota(jnp.int32, (total, LANES), 1)
    row = lax.broadcasted_iota(jnp.int32, (total, LANES), 0)
    listed = (lane >= LANES - ROUTING) & (lane < LANES - ROUTING // 2)

    def named(expert):
        return jnp.max(jnp.where(listed & (tile == expert.astype(jnp.float32)), 1.0, 0.0), axis=1, keepdims=True)

    mine, theirs = named(places_ref[1]), named(places_ref[2])
    marks = jnp.where(lane == 0, mine, jnp.where(lane == 1, theirs, 0.0))
    left = lax.broadcasted_iota(jnp.int32, (total, total), 0)
    right = lax.broadcasted_iota(jnp.int32, (total, total), 1)
    earlier = ((right < left) & (left // tokens == right // tokens)).astype(jnp.float32).astype(jnp.bfloat16)
    ahead = jnp.dot(earlier, marks.astype(jnp.bfloat16), preferred_element_type=jnp.float32)
    return jnp.where(marks > 0.0, ahead + (base + row // tokens * capacity).astype(jnp.float32), -1.0)


def select_body(tokens, capacity, wanted, places_ref, tile_ref, _, near_ref, next_ref, *out_refs):
    rows, held = near_ref.shape
    compact = out_refs[0].shape[0]
    slots = [
        slots_of(tokens, capacity, part * (rows // tokens * capacity), places_ref, tile)
        for part, tile in enumerate((tile_ref[...], next_ref[:, held - LANES :]))
    ]
    for part, slots_ref in enumerate(out_refs[len(wanted) :]):
        slots_ref[...] = slots[part]
    column = lax.broadcasted_iota(jnp.int32, (rows, compact), 1).astype(jnp.float32)
    for index, rows_ref in zip(wanted, out_refs):
        result = None
        for source, at in zip((near_ref, next_ref), slots):
            picks = (at[:, index : index + 1] == column).astype(jnp.float32).astype(jnp.bfloat16)
            part = lax.dot_general(picks, source[...], downward, preferred_element_type=jnp.float32)
            result = part if result is None else result + part
        rows_ref[...] = result.astype(jnp.bfloat16)


def select(tokens, capacity, wanted, places, near, following, tile=None, token=None):
    tile = near[:, near.shape[1] - LANES :] if tile is None else tile
    token = places if token is None else token
    located = 1 + int(0 in wanted)
    rows, held = near.shape
    compact = 2 * rows // tokens * capacity
    block = jax.ShapeDtypeStruct((compact, held), jnp.bfloat16)
    return pl.pallas_call(
        functools.partial(select_body, tokens, capacity, wanted),
        out_shape=[block] * len(wanted) + [jax.ShapeDtypeStruct((rows, LANES), jnp.float32)] * located,
        in_specs=[SCALARS] + whole_arrays(1) + [pl.BlockSpec(memory_space=pl.ANY)] + whole_arrays(2),
        out_specs=whole_arrays(len(wanted) + located),
        compiler_params=pltpu.CompilerParams(vmem_limit_bytes=20 * 2**20),
        cost_estimate=pl.CostEstimate(flops=8 * rows * compact * held, bytes_accessed=8 * rows * held, transcendentals=0),
    )(places, tile, token, near, following)


def merge_body(wanted, _, near_slots_ref, next_slots_ref, keep_ref, taken_ref, arrived_ref, *out_refs):
    rows = out_refs[0].shape[0]
    compact = keep_ref.shape[0]
    column = lax.broadcasted_iota(jnp.int32, (rows, compact), 1).astype(jnp.float32)
    high = (keep_ref[...] + taken_ref[...].astype(jnp.float32)).astype(jnp.bfloat16)
    for part, out_ref in zip(wanted, out_refs):
        slots = (near_slots_ref, next_slots_ref)[part][...]
        result = jnp.zeros((rows, keep_ref.shape[1]), jnp.float32)
        for index, source in enumerate((high, arrived_ref[...])):
            picks = (slots[:, index : index + 1] == column).astype(jnp.float32).astype(jnp.bfloat16)
            result += jnp.dot(picks, source, preferred_element_type=jnp.float32)
        out_ref[...] = result.astype(out_ref.dtype)


def merge(wanted, types, slots, keep, taken, arrived, token=None):
    token = slots[0] if token is None else token
    rows = slots[0].shape[0]
    compact, held = keep.shape
    return pl.pallas_call(
        functools.partial(merge_body, wanted),
        out_shape=[jax.ShapeDtypeStruct((rows, held), kind) for kind in types],
        in_specs=[pl.BlockSpec(memory_space=pl.ANY)] + whole_arrays(5),
        out_specs=whole_arrays(len(types)),
        compiler_params=pltpu.CompilerParams(vmem_limit_bytes=20 * 2**20),
        cost_estimate=pl.CostEstimate(flops=8 * rows * compact * held, bytes_accessed=8 * rows * held, transcendentals=0),
    )(token, *slots, keep, taken, arrived)


def ffn_body(
    places_ref, mine_near_ref, mine_far_ref, other_near_ref, other_far_ref, gate_v, up_v, down_v,
    keep_near_ref, keep_far_ref, send_near_ref, send_far_ref, rows_v, act_v,
):
    hidden, width = gate_v.shape
    first, second, held = split_widths(width)
    pair = mine_near_ref.shape[0]
    quad = pair // 2
    chunk = hidden // 3
    def lay(near, far_ref, swapped, start, size):
        for place in range(4):
            if swapped:
                source, block = (near, far_ref)[place % 2], place // 2
            else:
                source, block = (near, far_ref)[place // 2], place % 2
            rows_v[pl.ds(place * quad, quad), start : start + size] = source[pl.ds(block * quad, quad), :size]

    lower = places_ref[0] == 0

    @pl.when(lower)
    def _():
        lay(mine_near_ref, mine_far_ref, False, 0, first)
        lay(other_near_ref, other_far_ref, True, first, second)

    @pl.when(jnp.logical_not(lower))
    def _():
        lay(other_near_ref, other_far_ref, True, 0, first)
        lay(mine_near_ref, mine_far_ref, False, first, second)

    tile = jnp.concatenate([mine_near_ref[:, held - LANES :], mine_far_ref[:, held - LANES :]], axis=0)
    tile = tile.astype(jnp.float32)
    lane = lax.broadcasted_iota(jnp.int32, (2 * pair, LANES), 1)
    listed = (lane >= LANES - ROUTING) & (lane < LANES - ROUTING // 2)
    chosen = listed & (tile == places_ref[1].astype(jnp.float32))
    weight = jnp.sum(
        jnp.where(chosen, pltpu.roll(tile, LANES - ROUTING // 2, 1), 0.0), axis=1, keepdims=True
    )

    for part in range(3):
        there = slice(part * chunk, (part + 1) * chunk)
        gate = lax.dot_general(rows_v[...], gate_v[there, :], across, preferred_element_type=jnp.float32)
        up = lax.dot_general(rows_v[...], up_v[there, :], across, preferred_element_type=jnp.float32)
        act_v[:, there] = ((up + 1.0) * gate * jax.nn.sigmoid(swish_scale * gate)).astype(jnp.bfloat16)

    def keep_half(result, size):
        keep_near_ref[:, :size] = result[:pair]
        keep_far_ref[:, :size] = result[pair:]
        if size < held:
            keep_near_ref[:, size:] = jnp.zeros((pair, held - size), jnp.float32)
            keep_far_ref[:, size:] = jnp.zeros((pair, held - size), jnp.float32)

    def send_half(result, size):
        result = result.astype(jnp.bfloat16)
        for place in range(4):
            target, block = (send_near_ref, send_far_ref)[place % 2], place // 2
            target[pl.ds(block * quad, quad), :size] = result[place * quad : (place + 1) * quad]
        if size < held:
            send_near_ref[:, size:] = jnp.zeros((pair, held - size), jnp.bfloat16)
            send_far_ref[:, size:] = jnp.zeros((pair, held - size), jnp.bfloat16)

    low = weight * jnp.dot(act_v[...], down_v[:, :first], preferred_element_type=jnp.float32)

    @pl.when(lower)
    def _():
        keep_half(low, first)

    @pl.when(jnp.logical_not(lower))
    def _():
        send_half(low, first)

    high = weight * jnp.dot(act_v[...], down_v[:, first:], preferred_element_type=jnp.float32)

    @pl.when(lower)
    def _():
        send_half(high, second)

    @pl.when(jnp.logical_not(lower))
    def _():
        keep_half(high, second)


def ffn(places, mine_near, mine_far, other_near, other_far, gate_t, up_t, w_down):
    pair, held = mine_near.shape
    hidden, width = gate_t.shape
    total = 2 * pair
    return pl.pallas_call(
        ffn_body,
        out_shape=[jax.ShapeDtypeStruct((pair, held), jnp.float32)] * 2
        + [jax.ShapeDtypeStruct((pair, held), jnp.bfloat16)] * 2,
        in_specs=[SCALARS] + whole_arrays(7),
        out_specs=whole_arrays(4),
        scratch_shapes=[
            pltpu.VMEM((total, width), jnp.bfloat16),
            pltpu.VMEM((total, hidden), jnp.bfloat16),
        ],
        compiler_params=pltpu.CompilerParams(vmem_limit_bytes=20 * 2**20),
        cost_estimate=pl.CostEstimate(
            flops=6 * total * width * hidden,
            bytes_accessed=6 * width * hidden + 8 * total * held,
            transcendentals=total * hidden,
        ),
    )(places, mine_near, mine_far, other_near, other_far, gate_t, up_t, w_down)


def preload_body(_, *refs):
    count = (len(refs) - 1) // 2
    sems = refs[-1]
    copies = [pltpu.make_async_copy(refs[i], refs[count + i], sems.at[i]) for i in range(count)]
    for copy in copies:
        copy.start()
    for copy in copies:
        copy.wait()


def preload(token, *arrays):
    return pl.pallas_call(
        preload_body,
        out_shape=[pltpu.VMEM(a.shape, a.dtype) for a in arrays],
        in_specs=[pl.BlockSpec(memory_space=pl.ANY)] + [pl.BlockSpec(memory_space=pltpu.HBM)] * len(arrays),
        out_specs=whole_arrays(len(arrays)),
        scratch_shapes=[pltpu.SemaphoreType.DMA((len(arrays),))],
        compiler_params=pltpu.CompilerParams(vmem_limit_bytes=20 * 2**20),
    )(token, *arrays)


def prologue_body(top_count, places_ref, hidden_ref, packed_ref, mine_ref, give_ref):
    micro_count, tokens, width = hidden_ref.shape
    first, second, held = split_widths(width)
    start = -(-width // LANES) * LANES
    lane = lax.broadcasted_iota(jnp.int32, (tokens, LANES), 1)
    row = lax.broadcasted_iota(jnp.int32, (tokens, LANES), 0)
    here = lane % (ROUTING // 2)
    on_ids = (lane >= LANES - ROUTING) & (lane < LANES - ROUTING // 2)
    on_weights = lane >= LANES - ROUTING // 2

    def upright(place):
        at = start + place * tokens
        line = packed_ref[:, at // LANES * LANES : at // LANES * LANES + LANES]
        return jnp.sum(jnp.where(lane == row + at % LANES, line, 0.0), axis=1, keepdims=True)

    def store(ref, b, part, tile):
        size = part.shape[1]
        inside = size // LANES * LANES
        ref[b, :, :inside] = part[:, :inside].astype(jnp.bfloat16)
        if inside < size:
            rest = jnp.concatenate([part[:, inside:], jnp.zeros((tokens, LANES - size + inside), jnp.float32)], axis=1)
            tile = jnp.where(lane < size - inside, rest, tile)
        ref[b, :, inside:] = tile.astype(jnp.bfloat16)

    lower = places_ref[0] == 0
    for b in range(micro_count):
        residual = hidden_ref[b].astype(jnp.float32)
        scale = lax.rsqrt(jnp.mean(residual * residual, axis=-1, keepdims=True) + epsilon)
        normed = residual * scale * packed_ref[:, :width]
        tile = jnp.where(on_ids, -1.0, 0.0)
        for k in range(top_count):
            number = upright(b * top_count + k)
            weight = upright((micro_count + b) * top_count + k)
            high = weight.astype(jnp.bfloat16).astype(jnp.float32)
            middle = (weight - high).astype(jnp.bfloat16).astype(jnp.float32)
            for place, piece in enumerate((high, middle, weight - high - middle)):
                at = here == place * top_count + k
                tile = jnp.where(at & on_ids, number, jnp.where(at & on_weights, piece, tile))
        parts = normed[:, :first], normed[:, first:]

        @pl.when(lower)
        def _():
            store(mine_ref, b, parts[0], tile)
            store(give_ref, b, parts[1], tile)

        @pl.when(jnp.logical_not(lower))
        def _():
            store(mine_ref, b, parts[1], tile)
            store(give_ref, b, parts[0], tile)


def prologue(places, hidden, gain, ids, weights):
    micro_count, tokens, width = hidden.shape
    top_count = ids.shape[2]
    held = split_widths(width)[2]
    packed = jnp.concatenate(
        [
            jnp.pad(gain.astype(jnp.float32), (0, -width % LANES)),
            ids.transpose(0, 2, 1).reshape(-1).astype(jnp.float32),
            weights.transpose(0, 2, 1).reshape(-1),
        ]
    )
    packed = jnp.pad(packed, (0, -packed.shape[0] % LANES)).reshape(1, -1)
    return pl.pallas_call(
        functools.partial(prologue_body, top_count),
        out_shape=[jax.ShapeDtypeStruct((micro_count, tokens, held), jnp.bfloat16)] * 2,
        in_specs=[SCALARS] + whole_arrays(2),
        out_specs=whole_arrays(2),
        compiler_params=pltpu.CompilerParams(vmem_limit_bytes=20 * 2**20),
    )(places, hidden, packed)


def local(hidden, norm_gain, w_gate, w_up, w_down, expert_ids, route_weight):
    micro_count, tokens, width = hidden.shape
    top_count = expert_ids.shape[2]
    devices = lax.axis_size("req")
    experts = devices // HSPLIT
    rounded = HSPLIT * ((3 * tokens * top_count + 2 * experts * HSPLIT - 1) // (2 * experts * HSPLIT))
    capacity = min(tokens, max(HSPLIT, rounded))
    distant = devices // 8
    first, second, held = split_widths(width)
    position = lax.axis_index("req")
    core = position & 1
    lower = core == 0
    expert = position // HSPLIT
    places = jnp.stack([core, expert, expert ^ core]).astype(jnp.int32)

    def join(*blocks):
        return jnp.concatenate(blocks, axis=0)

    mine, give = prologue(places, hidden, norm_gain, expert_ids, route_weight)
    theirs = moved(give, other_core)
    pairs = [
        join(jnp.where(lower, mine[b], theirs[b]), jnp.where(lower, theirs[b], mine[b]))
        for b in range(micro_count)
    ]

    def tied(*arrays):
        return lax.optimization_barrier(arrays)

    def far_blocks(pair):
        return [moved(pair, far(j)) for j in range(1, distant)]

    chosen = tokens, capacity
    states = []

    side = 2 * tokens

    def second_hop(state, apart):
        near, following = state["near"], state["next"]
        if apart:
            send, state["places"] = select(*chosen, (1,), places, near, following)
        else:
            send, state["own"], *state["slots"] = select(*chosen, (1, 0), places, near, following)
        if len(states) > 1:
            send, states[-2]["arrived"] = tied(send, states[-2]["arrived"])
        state["arrived"] = moved(send, second_axis)
        if apart:
            tile = state["twin"]
            state["own"], near_slots, next_slots = select(*chosen, (0,), places, near, following, tile, send)
            state["slots"] = state["places"], next_slots

    def staged(block, load):
        crossed, beside = moved(block, far(2)), moved(block, far(1))
        crossed, first_loaded = tied(crossed, load(0, block))
        passed = moved(crossed, far(1))
        passed, second_loaded = tied(passed, load(1, crossed))
        return [beside, crossed, passed], first_loaded, second_loaded

    pair = pairs[0]
    asides = [moved(other, first_axis) for other in pairs[1:]]
    weights_t = w_gate.T, w_up.T
    if distant == 4:
        blocks, gate_v, up_v = staged(pair, lambda index, token: preload(token, weights_t[index])[0])
    else:
        blocks = far_blocks(pair)
        gate_v, up_v = preload(pair, *weights_t)
    blocks[0], *asides = tied(blocks[0], *asides)
    column = join(pair, *blocks)
    states.append({"near": column, "next": moved(column, first_axis)})
    down_v = None
    for pair, aside in zip(pairs[1:], asides):
        last = states[-1]
        both, last["twin"] = tied(join(pair, aside), moved(last["near"][:, held - LANES :], other_core))
        if distant == 4:
            crossed, beside = moved(both, far(2)), moved(both, far(1))
            second_hop(last, True)
            crossed, beside, last["own"] = tied(crossed, beside, last["own"])
            blocks = [beside, crossed, moved(crossed, far(1))]
        else:
            blocks = far_blocks(both)
            second_hop(last, True)
        if down_v is None:
            (down_v,) = preload(last["own"], w_down)
            blocks[-1], down_v = tied(blocks[-1], down_v)
        blocks = [both] + blocks
        states.append(
            {"near": join(*[block[:side] for block in blocks]), "next": join(*[block[side:] for block in blocks])}
        )
    second_hop(states[-1], False)
    if down_v is None:
        (down_v,) = preload(states[-1]["own"], w_down)

    def rounded_sum(a, b):
        return (a + b.astype(jnp.float32)).astype(jnp.bfloat16)

    hops = []
    for b, state in enumerate(states):
        own, arrived = state["own"], state["arrived"]
        other_far = moved(arrived, other_core)
        if b:
            other_far, hops[-1]["give"] = tied(other_far, hops[-1]["give"])
        keep_near, keep_far, send_near, send_far = ffn(
            places, own, arrived, moved(own, other_core), other_far, gate_v, up_v, down_v
        )
        if b + 1 < micro_count:
            send_far, states[b + 1]["arrived"] = tied(send_far, states[b + 1]["arrived"])
        if b:
            send_far, hops[-1]["arrived"] = tied(send_far, hops[-1]["arrived"])
        give = rounded_sum(keep_far, moved(send_far, other_core))
        hops.append(
            {"keep": keep_near, "taken": moved(send_near, other_core), "give": give, "arrived": moved(give, second_axis)}
        )
    for b in range(1, micro_count):
        hops[b - 1]["taken"], hops[b]["give"] = tied(hops[b - 1]["taken"], hops[b]["give"])

    def far_hop(block):
        block = block.reshape(distant, -1, held)
        if distant == 4:
            through = moved(block[3].astype(jnp.bfloat16), far(1))
            beside = moved(block[1].astype(jnp.bfloat16), far(1))
            return block[0], [beside], rounded_sum(block[2], through)
        return block[0], [moved(block[j].astype(jnp.bfloat16), far(j)) for j in range(1, distant)], None

    def crossing(total):
        kept, arrivals, cross = total
        return kept, arrivals + ([] if cross is None else [moved(cross, far(2))])

    def settled(kept, arrivals):
        for arrival in arrivals:
            kept = kept + arrival.astype(jnp.float32)
        return kept

    sums = []
    waiting = None
    for b, (state, hop) in enumerate(zip(states, hops)):
        final = b == micro_count - 1
        parts = state["slots"], hop["keep"], hop["taken"], hop["arrived"]
        if not final:
            near, following = merge((0, 1), (jnp.float32, jnp.float32), *parts)
            both = jnp.concatenate([near.reshape(distant, side, held), following.reshape(distant, side, held)], axis=1)
            total = far_hop(both)
            if total[2] is not None and b + 1 < micro_count:
                cross, hops[b + 1]["arrived"] = tied(total[2], hops[b + 1]["arrived"])
                total = total[0], total[1], cross
            waiting = crossing(total)
            continue
        (following,) = merge((1,), (jnp.bfloat16,), *parts)
        (near,) = merge((0,), (jnp.float32,), *parts, following)
        if waiting is not None:
            *earlier, near = tied(*waiting[1], near)
        near = near + moved(following, first_axis).astype(jnp.float32)
        kept, arrivals = crossing(far_hop(near))
        if waiting is not None:
            before = settled(waiting[0], earlier)
            sums.append(before[:side] + moved(before[side:].astype(jnp.bfloat16), first_axis).astype(jnp.float32))
        sums.append(settled(kept, arrivals))
    sums = jnp.stack(sums)
    own = jnp.where(lower, sums[:, :tokens], sums[:, tokens:])
    give = jnp.where(lower, sums[:, tokens:], sums[:, :tokens]).astype(jnp.bfloat16)
    taken = moved(give, other_core).astype(jnp.float32)
    mixture = jnp.concatenate(
        [jnp.where(lower, own, taken)[:, :, :first], jnp.where(lower, taken, own)[:, :, :second]], axis=2
    )
    return (hidden.astype(jnp.float32) + mixture).astype(jnp.bfloat16)


def solution(mesh):
    return jax.shard_map(
        local,
        mesh=mesh,
        in_specs=(
            P(None, ("groups", "req"), None),
            P(),
            P(None, "req"),
            P(None, "req"),
            P("req", None),
            P(None, ("groups", "req"), None),
            P(None, ("groups", "req"), None),
        ),
        out_specs=P(None, ("groups", "req"), None),
        check_vma=False,
    )
```

```python
import functools

import jax
import jax.numpy as jnp
from jax import lax
from jax.experimental import pallas as pl
from jax.experimental.pallas import tpu as pltpu
from jax.sharding import PartitionSpec as P

HSPLIT = 4
LANES = 128
ROUTING = 32

epsilon = 1e-05
swish_scale = 1.702

across = (((1,), (1,)), ((), ()))
downward = (((0,), (0,)), ((), ()))


def split_widths(width):
    first = width // 2 // LANES * LANES
    second = width - first
    held = -(-(second + ROUTING) // LANES) * LANES
    return first, second, held


def moved(block, partner):
    count = lax.axis_size("req")
    return lax.ppermute(block, "req", [(i, partner(i)) for i in range(count)])


def other_core(i):
    return i ^ 1


def first_axis(i):
    return i ^ (2 if i & 1 else 4)


def second_axis(i):
    return i ^ (4 if i & 1 else 2)


def far(step):
    return lambda i: i ^ (step << 3)


def whole_arrays(count):
    return [pl.BlockSpec(memory_space=pltpu.VMEM)] * count


SCALARS = pl.BlockSpec(memory_space=pltpu.SMEM)


def slots_of(tokens, capacity, base, places_ref, tile):
    total = tile.shape[0]
    tile = tile.astype(jnp.float32)
    lane = lax.broadcasted_iota(jnp.int32, (total, LANES), 1)
    row = lax.broadcasted_iota(jnp.int32, (total, LANES), 0)
    listed = (lane >= LANES - ROUTING) & (lane < LANES - ROUTING // 2)

    def named(expert):
        return jnp.max(jnp.where(listed & (tile == expert.astype(jnp.float32)), 1.0, 0.0), axis=1, keepdims=True)

    mine, theirs = named(places_ref[1]), named(places_ref[2])
    marks = jnp.where(lane == 0, mine, jnp.where(lane == 1, theirs, 0.0))
    left = lax.broadcasted_iota(jnp.int32, (total, total), 0)
    right = lax.broadcasted_iota(jnp.int32, (total, total), 1)
    earlier = ((right < left) & (left // tokens == right // tokens)).astype(jnp.float32).astype(jnp.bfloat16)
    ahead = jnp.dot(earlier, marks.astype(jnp.bfloat16), preferred_element_type=jnp.float32)
    return jnp.where(marks > 0.0, ahead + (base + row // tokens * capacity).astype(jnp.float32), -1.0)


def select_body(tokens, capacity, wanted, places_ref, tile_ref, _, near_ref, next_ref, *out_refs):
    rows, held = near_ref.shape
    compact = out_refs[0].shape[0]
    slots = [
        slots_of(tokens, capacity, part * (rows // tokens * capacity), places_ref, tile)
        for part, tile in enumerate((tile_ref[...], next_ref[:, held - LANES :]))
    ]
    for part, slots_ref in enumerate(out_refs[len(wanted) :]):
        slots_ref[...] = slots[part]
    column = lax.broadcasted_iota(jnp.int32, (rows, compact), 1).astype(jnp.float32)
    for index, rows_ref in zip(wanted, out_refs):
        result = None
        for source, at in zip((near_ref, next_ref), slots):
            picks = (at[:, index : index + 1] == column).astype(jnp.float32).astype(jnp.bfloat16)
            part = lax.dot_general(picks, source[...], downward, preferred_element_type=jnp.float32)
            result = part if result is None else result + part
        rows_ref[...] = result.astype(jnp.bfloat16)


def select(tokens, capacity, wanted, places, near, following, tile=None, token=None):
    tile = near[:, near.shape[1] - LANES :] if tile is None else tile
    token = places if token is None else token
    located = 1 + int(0 in wanted)
    rows, held = near.shape
    compact = 2 * rows // tokens * capacity
    block = jax.ShapeDtypeStruct((compact, held), jnp.bfloat16)
    return pl.pallas_call(
        functools.partial(select_body, tokens, capacity, wanted),
        out_shape=[block] * len(wanted) + [jax.ShapeDtypeStruct((rows, LANES), jnp.float32)] * located,
        in_specs=[SCALARS] + whole_arrays(1) + [pl.BlockSpec(memory_space=pl.ANY)] + whole_arrays(2),
        out_specs=whole_arrays(len(wanted) + located),
        compiler_params=pltpu.CompilerParams(vmem_limit_bytes=20 * 2**20),
        cost_estimate=pl.CostEstimate(flops=8 * rows * compact * held, bytes_accessed=8 * rows * held, transcendentals=0),
    )(places, tile, token, near, following)


def merge_body(wanted, _, near_slots_ref, next_slots_ref, keep_ref, taken_ref, arrived_ref, *out_refs):
    rows = out_refs[0].shape[0]
    compact = keep_ref.shape[0]
    column = lax.broadcasted_iota(jnp.int32, (rows, compact), 1).astype(jnp.float32)
    high = (keep_ref[...] + taken_ref[...].astype(jnp.float32)).astype(jnp.bfloat16)
    for part, out_ref in zip(wanted, out_refs):
        slots = (near_slots_ref, next_slots_ref)[part][...]
        result = jnp.zeros((rows, keep_ref.shape[1]), jnp.float32)
        for index, source in enumerate((high, arrived_ref[...])):
            picks = (slots[:, index : index + 1] == column).astype(jnp.float32).astype(jnp.bfloat16)
            result += jnp.dot(picks, source, preferred_element_type=jnp.float32)
        out_ref[...] = result.astype(out_ref.dtype)


def merge(wanted, types, slots, keep, taken, arrived, token=None):
    token = slots[0] if token is None else token
    rows = slots[0].shape[0]
    compact, held = keep.shape
    return pl.pallas_call(
        functools.partial(merge_body, wanted),
        out_shape=[jax.ShapeDtypeStruct((rows, held), kind) for kind in types],
        in_specs=[pl.BlockSpec(memory_space=pl.ANY)] + whole_arrays(5),
        out_specs=whole_arrays(len(types)),
        compiler_params=pltpu.CompilerParams(vmem_limit_bytes=20 * 2**20),
        cost_estimate=pl.CostEstimate(flops=8 * rows * compact * held, bytes_accessed=8 * rows * held, transcendentals=0),
    )(token, *slots, keep, taken, arrived)


def ffn_body(
    places_ref, mine_near_ref, mine_far_ref, other_near_ref, other_far_ref, gate_v, up_v, down_v,
    keep_near_ref, keep_far_ref, send_near_ref, send_far_ref, rows_v, act_v,
):
    hidden, width = gate_v.shape
    first, second, held = split_widths(width)
    pair = mine_near_ref.shape[0]
    quad = pair // 2
    chunk = hidden // 3
    def lay(near, far_ref, swapped, start, size):
        for place in range(4):
            if swapped:
                source, block = (near, far_ref)[place % 2], place // 2
            else:
                source, block = (near, far_ref)[place // 2], place % 2
            rows_v[pl.ds(place * quad, quad), start : start + size] = source[pl.ds(block * quad, quad), :size]

    lower = places_ref[0] == 0

    @pl.when(lower)
    def _():
        lay(mine_near_ref, mine_far_ref, False, 0, first)
        lay(other_near_ref, other_far_ref, True, first, second)

    @pl.when(jnp.logical_not(lower))
    def _():
        lay(other_near_ref, other_far_ref, True, 0, first)
        lay(mine_near_ref, mine_far_ref, False, first, second)

    tile = jnp.concatenate([mine_near_ref[:, held - LANES :], mine_far_ref[:, held - LANES :]], axis=0)
    tile = tile.astype(jnp.float32)
    lane = lax.broadcasted_iota(jnp.int32, (2 * pair, LANES), 1)
    listed = (lane >= LANES - ROUTING) & (lane < LANES - ROUTING // 2)
    chosen = listed & (tile == places_ref[1].astype(jnp.float32))
    weight = jnp.sum(
        jnp.where(chosen, pltpu.roll(tile, LANES - ROUTING // 2, 1), 0.0), axis=1, keepdims=True
    )

    for part in range(3):
        there = slice(part * chunk, (part + 1) * chunk)
        gate = lax.dot_general(rows_v[...], gate_v[there, :], across, preferred_element_type=jnp.float32)
        up = lax.dot_general(rows_v[...], up_v[there, :], across, preferred_element_type=jnp.float32)
        act_v[:, there] = ((up + 1.0) * gate * jax.nn.sigmoid(swish_scale * gate)).astype(jnp.bfloat16)

    def keep_half(result, size):
        keep_near_ref[:, :size] = result[:pair]
        keep_far_ref[:, :size] = result[pair:]
        if size < held:
            keep_near_ref[:, size:] = jnp.zeros((pair, held - size), jnp.float32)
            keep_far_ref[:, size:] = jnp.zeros((pair, held - size), jnp.float32)

    def send_half(result, size):
        result = result.astype(jnp.bfloat16)
        for place in range(4):
            target, block = (send_near_ref, send_far_ref)[place % 2], place // 2
            target[pl.ds(block * quad, quad), :size] = result[place * quad : (place + 1) * quad]
        if size < held:
            send_near_ref[:, size:] = jnp.zeros((pair, held - size), jnp.bfloat16)
            send_far_ref[:, size:] = jnp.zeros((pair, held - size), jnp.bfloat16)

    low = weight * jnp.dot(act_v[...], down_v[:, :first], preferred_element_type=jnp.float32)

    @pl.when(lower)
    def _():
        keep_half(low, first)

    @pl.when(jnp.logical_not(lower))
    def _():
        send_half(low, first)

    high = weight * jnp.dot(act_v[...], down_v[:, first:], preferred_element_type=jnp.float32)

    @pl.when(lower)
    def _():
        send_half(high, second)

    @pl.when(jnp.logical_not(lower))
    def _():
        keep_half(high, second)


def ffn(places, mine_near, mine_far, other_near, other_far, gate_t, up_t, w_down):
    pair, held = mine_near.shape
    hidden, width = gate_t.shape
    total = 2 * pair
    return pl.pallas_call(
        ffn_body,
        out_shape=[jax.ShapeDtypeStruct((pair, held), jnp.float32)] * 2
        + [jax.ShapeDtypeStruct((pair, held), jnp.bfloat16)] * 2,
        in_specs=[SCALARS] + whole_arrays(7),
        out_specs=whole_arrays(4),
        scratch_shapes=[
            pltpu.VMEM((total, width), jnp.bfloat16),
            pltpu.VMEM((total, hidden), jnp.bfloat16),
        ],
        compiler_params=pltpu.CompilerParams(vmem_limit_bytes=20 * 2**20),
        cost_estimate=pl.CostEstimate(
            flops=6 * total * width * hidden,
            bytes_accessed=6 * width * hidden + 8 * total * held,
            transcendentals=total * hidden,
        ),
    )(places, mine_near, mine_far, other_near, other_far, gate_t, up_t, w_down)


def preload_body(_, *refs):
    count = (len(refs) - 1) // 2
    sems = refs[-1]
    copies = [pltpu.make_async_copy(refs[i], refs[count + i], sems.at[i]) for i in range(count)]
    for copy in copies:
        copy.start()
    for copy in copies:
        copy.wait()


def preload(token, *arrays):
    return pl.pallas_call(
        preload_body,
        out_shape=[pltpu.VMEM(a.shape, a.dtype) for a in arrays],
        in_specs=[pl.BlockSpec(memory_space=pl.ANY)] + [pl.BlockSpec(memory_space=pltpu.HBM)] * len(arrays),
        out_specs=whole_arrays(len(arrays)),
        scratch_shapes=[pltpu.SemaphoreType.DMA((len(arrays),))],
        compiler_params=pltpu.CompilerParams(vmem_limit_bytes=20 * 2**20),
    )(token, *arrays)


def prologue_body(top_count, places_ref, hidden_ref, packed_ref, mine_ref, give_ref):
    micro_count, tokens, width = hidden_ref.shape
    first, second, held = split_widths(width)
    start = -(-width // LANES) * LANES
    lane = lax.broadcasted_iota(jnp.int32, (tokens, LANES), 1)
    row = lax.broadcasted_iota(jnp.int32, (tokens, LANES), 0)
    here = lane % (ROUTING // 2)
    on_ids = (lane >= LANES - ROUTING) & (lane < LANES - ROUTING // 2)
    on_weights = lane >= LANES - ROUTING // 2

    def upright(place):
        at = start + place * tokens
        line = packed_ref[:, at // LANES * LANES : at // LANES * LANES + LANES]
        return jnp.sum(jnp.where(lane == row + at % LANES, line, 0.0), axis=1, keepdims=True)

    def store(ref, b, part, tile):
        size = part.shape[1]
        inside = size // LANES * LANES
        ref[b, :, :inside] = part[:, :inside].astype(jnp.bfloat16)
        if inside < size:
            rest = jnp.concatenate([part[:, inside:], jnp.zeros((tokens, LANES - size + inside), jnp.float32)], axis=1)
            tile = jnp.where(lane < size - inside, rest, tile)
        ref[b, :, inside:] = tile.astype(jnp.bfloat16)

    lower = places_ref[0] == 0
    for b in range(micro_count):
        residual = hidden_ref[b].astype(jnp.float32)
        scale = lax.rsqrt(jnp.mean(residual * residual, axis=-1, keepdims=True) + epsilon)
        normed = residual * scale * packed_ref[:, :width]
        tile = jnp.where(on_ids, -1.0, 0.0)
        for k in range(top_count):
            number = upright(b * top_count + k)
            weight = upright((micro_count + b) * top_count + k)
            high = weight.astype(jnp.bfloat16).astype(jnp.float32)
            middle = (weight - high).astype(jnp.bfloat16).astype(jnp.float32)
            for place, piece in enumerate((high, middle, weight - high - middle)):
                at = here == place * top_count + k
                tile = jnp.where(at & on_ids, number, jnp.where(at & on_weights, piece, tile))
        parts = normed[:, :first], normed[:, first:]

        @pl.when(lower)
        def _():
            store(mine_ref, b, parts[0], tile)
            store(give_ref, b, parts[1], tile)

        @pl.when(jnp.logical_not(lower))
        def _():
            store(mine_ref, b, parts[1], tile)
            store(give_ref, b, parts[0], tile)


def prologue(places, hidden, gain, ids, weights):
    micro_count, tokens, width = hidden.shape
    top_count = ids.shape[2]
    held = split_widths(width)[2]
    packed = jnp.concatenate(
        [
            jnp.pad(gain.astype(jnp.float32), (0, -width % LANES)),
            ids.transpose(0, 2, 1).reshape(-1).astype(jnp.float32),
            weights.transpose(0, 2, 1).reshape(-1),
        ]
    )
    packed = jnp.pad(packed, (0, -packed.shape[0] % LANES)).reshape(1, -1)
    return pl.pallas_call(
        functools.partial(prologue_body, top_count),
        out_shape=[jax.ShapeDtypeStruct((micro_count, tokens, held), jnp.bfloat16)] * 2,
        in_specs=[SCALARS] + whole_arrays(2),
        out_specs=whole_arrays(2),
        compiler_params=pltpu.CompilerParams(vmem_limit_bytes=20 * 2**20),
    )(places, hidden, packed)


def local(hidden, norm_gain, w_gate, w_up, w_down, expert_ids, route_weight):
    micro_count, tokens, width = hidden.shape
    top_count = expert_ids.shape[2]
    devices = lax.axis_size("req")
    experts = devices // HSPLIT
    rounded = HSPLIT * ((3 * tokens * top_count + 2 * experts * HSPLIT - 1) // (2 * experts * HSPLIT))
    capacity = min(tokens, max(HSPLIT, rounded))
    distant = devices // 8
    first, second, held = split_widths(width)
    position = lax.axis_index("req")
    core = position & 1
    lower = core == 0
    expert = position // HSPLIT
    places = jnp.stack([core, expert, expert ^ core]).astype(jnp.int32)

    def join(*blocks):
        return jnp.concatenate(blocks, axis=0)

    mine, give = prologue(places, hidden, norm_gain, expert_ids, route_weight)
    theirs = moved(give, other_core)
    pairs = [
        join(jnp.where(lower, mine[b], theirs[b]), jnp.where(lower, theirs[b], mine[b]))
        for b in range(micro_count)
    ]

    def tied(*arrays):
        return lax.optimization_barrier(arrays)

    def far_blocks(pair):
        return [moved(pair, far(j)) for j in range(1, distant)]

    chosen = tokens, capacity
    states = []

    side = 2 * tokens

    def second_hop(state, apart):
        near, following = state["near"], state["next"]
        if apart:
            send, state["places"] = select(*chosen, (1,), places, near, following)
        else:
            send, state["own"], *state["slots"] = select(*chosen, (1, 0), places, near, following)
        if len(states) > 1:
            send, states[-2]["arrived"] = tied(send, states[-2]["arrived"])
        state["arrived"] = moved(send, second_axis)
        if apart:
            tile = state["twin"]
            state["own"], near_slots, next_slots = select(*chosen, (0,), places, near, following, tile, send)
            state["slots"] = state["places"], next_slots

    pair = pairs[0]
    weights_t = w_gate.T, w_up.T
    if distant == 4:
        (gate_v,) = preload(pair, weights_t[0])
        crossed = moved(pair, far(2))
        again, pairs[-1] = tied(pair, pairs[-1])
        beside = moved(again, far(1))
        crossed, gate_v = tied(crossed, gate_v)
        (up_v,) = preload(crossed, weights_t[1])
        passed = moved(crossed, far(1))
        passed, up_v = tied(passed, up_v)
        blocks = [beside, crossed, passed]
        *rest, gate_v = tied(*pairs[1:], gate_v)
    else:
        blocks = far_blocks(pair)
        gate_v, up_v = preload(pair, *weights_t)
        rest = pairs[1:]
    asides = [moved(other, first_axis) for other in rest]
    blocks[-1], *asides = tied(blocks[-1], *asides)
    column = join(pair, *blocks)
    states.append({"near": column, "next": moved(column, first_axis)})
    down_v = None
    for pair, aside in zip(pairs[1:], asides):
        last = states[-1]
        both, last["twin"] = tied(join(pair, aside), moved(last["near"][:, held - LANES :], other_core))
        if distant == 4:
            crossed, beside = moved(both, far(2)), moved(both, far(1))
            second_hop(last, True)
            crossed, beside, last["own"] = tied(crossed, beside, last["own"])
            blocks = [beside, crossed, moved(crossed, far(1))]
        else:
            blocks = far_blocks(both)
            second_hop(last, True)
        if down_v is None:
            (down_v,) = preload(last["own"], w_down)
            blocks[-1], down_v, last["arrived"] = tied(blocks[-1], down_v, last["arrived"])
        blocks = [both] + blocks
        states.append(
            {"near": join(*[block[:side] for block in blocks]), "next": join(*[block[side:] for block in blocks])}
        )
    second_hop(states[-1], False)
    if down_v is None:
        (down_v,) = preload(states[-1]["own"], w_down)

    def rounded_sum(a, b):
        return (a + b.astype(jnp.float32)).astype(jnp.bfloat16)

    hops = []
    for b, state in enumerate(states):
        own, arrived = state["own"], state["arrived"]
        other_far = moved(arrived, other_core)
        if b:
            other_far, hops[-1]["give"] = tied(other_far, hops[-1]["give"])
        keep_near, keep_far, send_near, send_far = ffn(
            places, own, arrived, moved(own, other_core), other_far, gate_v, up_v, down_v
        )
        if b + 1 < micro_count:
            send_far, states[b + 1]["arrived"] = tied(send_far, states[b + 1]["arrived"])
        if b:
            send_far, hops[-1]["arrived"] = tied(send_far, hops[-1]["arrived"])
        give = rounded_sum(keep_far, moved(send_far, other_core))
        hops.append(
            {"keep": keep_near, "taken": moved(send_near, other_core), "give": give, "arrived": moved(give, second_axis)}
        )
    def far_hop(block):
        block = block.reshape(distant, -1, held)
        if distant == 4:
            through = moved(block[3].astype(jnp.bfloat16), far(1))
            beside = moved(block[1].astype(jnp.bfloat16), far(1))
            return [block[0], [beside], rounded_sum(block[2], through)]
        return [block[0], [moved(block[j].astype(jnp.bfloat16), far(j)) for j in range(1, distant)], None]

    def settled(kept, arrivals, cross):
        for arrival in arrivals if cross is None else arrivals + [moved(cross, far(2))]:
            kept = kept + arrival.astype(jnp.float32)
        return kept

    totals = []
    near = None
    for b, (state, hop) in enumerate(zip(states, hops)):
        token = hops[b + 1]["give"] if b + 1 < micro_count else None
        parts = state["slots"], hop["keep"], hop["taken"], hop["arrived"]
        if near is None:
            kept, following = merge((0, 1), (jnp.float32, jnp.bfloat16), *parts, token)
        else:
            (following,) = merge((1,), (jnp.bfloat16,), *parts, token)
            (kept,) = merge((0,), (jnp.float32,), *parts, following)
            near, kept = tied(near, kept)
            totals.append(far_hop(near))
        near = kept + moved(following, first_axis).astype(jnp.float32)
    totals.append(far_hop(near))
    sums = jnp.stack([settled(*total) for total in totals])
    own = jnp.where(lower, sums[:, :tokens], sums[:, tokens:])
    give = jnp.where(lower, sums[:, tokens:], sums[:, :tokens]).astype(jnp.bfloat16)
    taken = moved(give, other_core).astype(jnp.float32)
    mixture = jnp.concatenate(
        [jnp.where(lower, own, taken)[:, :, :first], jnp.where(lower, taken, own)[:, :, :second]], axis=2
    )
    return (hidden.astype(jnp.float32) + mixture).astype(jnp.bfloat16)


def solution(mesh):
    return jax.shard_map(
        local,
        mesh=mesh,
        in_specs=(
            P(None, ("groups", "req"), None),
            P(),
            P(None, "req"),
            P(None, "req"),
            P("req", None),
            P(None, ("groups", "req"), None),
            P(None, ("groups", "req"), None),
        ),
        out_specs=P(None, ("groups", "req"), None),
        check_vma=False,
    )
```

```python
import functools

import jax
import jax.numpy as jnp
from jax import lax
from jax.experimental import pallas as pl
from jax.experimental.pallas import tpu as pltpu
from jax.sharding import PartitionSpec as P

HSPLIT = 4
LANES = 128
ROUTING = 32

epsilon = 1e-05
swish_scale = 1.702

across = (((1,), (1,)), ((), ()))
downward = (((0,), (0,)), ((), ()))


def split_widths(width):
    first = width // 2 // LANES * LANES
    second = width - first
    held = -(-(second + ROUTING) // LANES) * LANES
    return first, second, held


def moved(block, partner):
    count = lax.axis_size("req")
    return lax.ppermute(block, "req", [(i, partner(i)) for i in range(count)])


def other_core(i):
    return i ^ 1


def first_axis(i):
    return i ^ (2 if i & 1 else 4)


def second_axis(i):
    return i ^ (4 if i & 1 else 2)


def far(step):
    return lambda i: i ^ (step << 3)


def whole_arrays(count):
    return [pl.BlockSpec(memory_space=pltpu.VMEM)] * count


SCALARS = pl.BlockSpec(memory_space=pltpu.SMEM)


def slots_of(tokens, capacity, base, places_ref, rows_ref):
    total, held = rows_ref.shape
    tile = rows_ref[:, held - LANES :].astype(jnp.float32)
    lane = lax.broadcasted_iota(jnp.int32, (total, LANES), 1)
    row = lax.broadcasted_iota(jnp.int32, (total, LANES), 0)
    listed = (lane >= LANES - ROUTING) & (lane < LANES - ROUTING // 2)

    def named(expert):
        return jnp.max(jnp.where(listed & (tile == expert.astype(jnp.float32)), 1.0, 0.0), axis=1, keepdims=True)

    mine, theirs = named(places_ref[1]), named(places_ref[2])
    marks = jnp.where(lane == 0, mine, jnp.where(lane == 1, theirs, 0.0))
    left = lax.broadcasted_iota(jnp.int32, (total, total), 0)
    right = lax.broadcasted_iota(jnp.int32, (total, total), 1)
    earlier = ((right < left) & (left // tokens == right // tokens)).astype(jnp.float32).astype(jnp.bfloat16)
    ahead = jnp.dot(earlier, marks.astype(jnp.bfloat16), preferred_element_type=jnp.float32)
    return jnp.where(marks > 0.0, ahead + (base + row // tokens * capacity).astype(jnp.float32), -1.0)


def select_body(tokens, capacity, wanted, places_ref, near_ref, next_ref, *out_refs):
    rows = near_ref.shape[0]
    compact = out_refs[0].shape[0]
    slots = [
        slots_of(tokens, capacity, part * (rows // tokens * capacity), places_ref, ref)
        for part, ref in enumerate((near_ref, next_ref))
    ]
    for part, slots_ref in enumerate(out_refs[len(wanted) :]):
        slots_ref[...] = slots[part]
    column = lax.broadcasted_iota(jnp.int32, (rows, compact), 1).astype(jnp.float32)
    for index, rows_ref in zip(wanted, out_refs):
        result = None
        for source, at in zip((near_ref, next_ref), slots):
            picks = (at[:, index : index + 1] == column).astype(jnp.float32).astype(jnp.bfloat16)
            part = lax.dot_general(picks, source[...], downward, preferred_element_type=jnp.float32)
            result = part if result is None else result + part
        rows_ref[...] = result.astype(jnp.bfloat16)


def select(tokens, capacity, wanted, places, near, following):
    located = 2 * int(0 in wanted)
    rows, held = near.shape
    compact = 2 * rows // tokens * capacity
    block = jax.ShapeDtypeStruct((compact, held), jnp.bfloat16)
    return pl.pallas_call(
        functools.partial(select_body, tokens, capacity, wanted),
        out_shape=[block] * len(wanted) + [jax.ShapeDtypeStruct((rows, LANES), jnp.float32)] * located,
        in_specs=[SCALARS] + whole_arrays(2),
        out_specs=whole_arrays(len(wanted) + located),
        compiler_params=pltpu.CompilerParams(vmem_limit_bytes=20 * 2**20),
        cost_estimate=pl.CostEstimate(flops=8 * rows * compact * held, bytes_accessed=8 * rows * held, transcendentals=0),
    )(places, near, following)


def merge_body(wanted, _, near_slots_ref, next_slots_ref, keep_ref, taken_ref, arrived_ref, *out_refs):
    rows = out_refs[0].shape[0]
    compact = keep_ref.shape[0]
    column = lax.broadcasted_iota(jnp.int32, (rows, compact), 1).astype(jnp.float32)
    high = (keep_ref[...] + taken_ref[...].astype(jnp.float32)).astype(jnp.bfloat16)
    for part, out_ref in zip(wanted, out_refs):
        slots = (near_slots_ref, next_slots_ref)[part][...]
        result = jnp.zeros((rows, keep_ref.shape[1]), jnp.float32)
        for index, source in enumerate((high, arrived_ref[...])):
            picks = (slots[:, index : index + 1] == column).astype(jnp.float32).astype(jnp.bfloat16)
            result += jnp.dot(picks, source, preferred_element_type=jnp.float32)
        out_ref[...] = result.astype(out_ref.dtype)


def merge(wanted, types, slots, keep, taken, arrived, token=None):
    token = slots[0] if token is None else token
    rows = slots[0].shape[0]
    compact, held = keep.shape
    return pl.pallas_call(
        functools.partial(merge_body, wanted),
        out_shape=[jax.ShapeDtypeStruct((rows, held), kind) for kind in types],
        in_specs=[pl.BlockSpec(memory_space=pl.ANY)] + whole_arrays(5),
        out_specs=whole_arrays(len(types)),
        compiler_params=pltpu.CompilerParams(vmem_limit_bytes=20 * 2**20),
        cost_estimate=pl.CostEstimate(flops=8 * rows * compact * held, bytes_accessed=8 * rows * held, transcendentals=0),
    )(token, *slots, keep, taken, arrived)


def add_products(places_ref, mine_ref, other_ref, weights_ref, mine_to, other_to, total_ref, fresh):
    width = weights_ref.shape[1]
    first, second, _ = split_widths(width)
    quad = mine_ref.shape[0] // 2

    def add(mine_columns, other_columns):
        pieces = []
        for ref, (start, size), places in (
            (mine_ref, mine_columns, mine_to), (other_ref, other_columns, other_to)
        ):
            product = lax.dot_general(
                ref[:, :size], weights_ref[:, start : start + size], across, preferred_element_type=jnp.float32
            )
            pieces += [(place, product[block * quad : (block + 1) * quad]) for block, place in enumerate(places)]
        seen = set()
        for place, piece in pieces:
            there = pl.ds(place * quad, quad)
            if place in fresh and place not in seen:
                total_ref[there, :] = piece
            else:
                total_ref[there, :] += piece
            seen.add(place)

    lower = places_ref[0] == 0

    @pl.when(lower)
    def _():
        add((0, first), (first, second))

    @pl.when(jnp.logical_not(lower))
    def _():
        add((first, second), (0, first))


def start_body(places_ref, _, mine_ref, other_ref, gate_v, up_v, gate_ref, up_ref):
    for weights_ref, total_ref in ((gate_v, gate_ref), (up_v, up_ref)):
        add_products(places_ref, mine_ref, other_ref, weights_ref, (0, 1), (0, 2), total_ref, (0, 1, 2))


def ffn_start(places, mine, other, gate_v, up_v, token=None):
    pair = mine.shape[0]
    hidden, width = gate_v.shape
    return pl.pallas_call(
        start_body,
        out_shape=[jax.ShapeDtypeStruct((pair // 2 * 3, hidden), jnp.float32)] * 2,
        in_specs=[SCALARS, pl.BlockSpec(memory_space=pl.ANY)] + whole_arrays(4),
        out_specs=whole_arrays(2),
        compiler_params=pltpu.CompilerParams(vmem_limit_bytes=20 * 2**20),
        cost_estimate=pl.CostEstimate(flops=4 * pair * width * hidden, bytes_accessed=4 * width * hidden, transcendentals=0),
    )(places, places if token is None else token, mine, other, gate_v, up_v)


def ffn_body(
    places_ref, gate_part_ref, up_part_ref, mine_near_ref, mine_far_ref, other_far_ref, gate_v, up_v, down_v,
    keep_near_ref, keep_far_ref, send_near_ref, send_far_ref, gate_acc, up_acc, act_v,
):
    hidden, width = gate_v.shape
    first, second, held = split_widths(width)
    pair = mine_near_ref.shape[0]
    quad = pair // 2
    lower = places_ref[0] == 0

    tile = jnp.concatenate([mine_near_ref[:, held - LANES :], mine_far_ref[:, held - LANES :]], axis=0)
    tile = tile.astype(jnp.float32)
    lane = lax.broadcasted_iota(jnp.int32, (2 * pair, LANES), 1)
    listed = (lane >= LANES - ROUTING) & (lane < LANES - ROUTING // 2)
    chosen = listed & (tile == places_ref[1].astype(jnp.float32))
    weight = jnp.sum(
        jnp.where(chosen, pltpu.roll(tile, LANES - ROUTING // 2, 1), 0.0), axis=1, keepdims=True
    )

    for part_ref, weights_ref, total_ref in ((gate_part_ref, gate_v, gate_acc), (up_part_ref, up_v, up_acc)):
        total_ref[pl.ds(0, 3 * quad), :] = part_ref[...]
        add_products(places_ref, mine_far_ref, other_far_ref, weights_ref, (2, 3), (1, 3), total_ref, (3,))
    gate = gate_acc[...]
    act_v[...] = ((up_acc[...] + 1.0) * gate * jax.nn.sigmoid(swish_scale * gate)).astype(jnp.bfloat16)

    def keep_half(result, size):
        keep_near_ref[:, :size] = result[:pair]
        keep_far_ref[:, :size] = result[pair:]
        if size < held:
            keep_near_ref[:, size:] = jnp.zeros((pair, held - size), jnp.float32)
            keep_far_ref[:, size:] = jnp.zeros((pair, held - size), jnp.float32)

    def send_half(result, size):
        result = result.astype(jnp.bfloat16)
        for place in range(4):
            target, block = (send_near_ref, send_far_ref)[place % 2], place // 2
            target[pl.ds(block * quad, quad), :size] = result[place * quad : (place + 1) * quad]
        if size < held:
            send_near_ref[:, size:] = jnp.zeros((pair, held - size), jnp.bfloat16)
            send_far_ref[:, size:] = jnp.zeros((pair, held - size), jnp.bfloat16)

    low = weight * jnp.dot(act_v[...], down_v[:, :first], preferred_element_type=jnp.float32)

    @pl.when(lower)
    def _():
        keep_half(low, first)

    @pl.when(jnp.logical_not(lower))
    def _():
        send_half(low, first)

    high = weight * jnp.dot(act_v[...], down_v[:, first:], preferred_element_type=jnp.float32)

    @pl.when(lower)
    def _():
        send_half(high, second)

    @pl.when(jnp.logical_not(lower))
    def _():
        keep_half(high, second)


def ffn(places, parts, mine_near, mine_far, other_far, gate_v, up_v, down_v):
    pair, held = mine_near.shape
    hidden, width = gate_v.shape
    total = 2 * pair
    return pl.pallas_call(
        ffn_body,
        out_shape=[jax.ShapeDtypeStruct((pair, held), jnp.float32)] * 2
        + [jax.ShapeDtypeStruct((pair, held), jnp.bfloat16)] * 2,
        in_specs=[SCALARS] + whole_arrays(8),
        out_specs=whole_arrays(4),
        scratch_shapes=[
            pltpu.VMEM((total, hidden), jnp.float32),
            pltpu.VMEM((total, hidden), jnp.float32),
            pltpu.VMEM((total, hidden), jnp.bfloat16),
        ],
        compiler_params=pltpu.CompilerParams(vmem_limit_bytes=20 * 2**20),
        cost_estimate=pl.CostEstimate(
            flops=4 * total * width * hidden,
            bytes_accessed=6 * width * hidden + 8 * total * held,
            transcendentals=total * hidden,
        ),
    )(places, *parts, mine_near, mine_far, other_far, gate_v, up_v, down_v)


def preload_body(_, *refs):
    count = (len(refs) - 1) // 2
    sems = refs[-1]
    copies = [pltpu.make_async_copy(refs[i], refs[count + i], sems.at[i]) for i in range(count)]
    for copy in copies:
        copy.start()
    for copy in copies:
        copy.wait()


def preload(token, *arrays):
    return pl.pallas_call(
        preload_body,
        out_shape=[pltpu.VMEM(a.shape, a.dtype) for a in arrays],
        in_specs=[pl.BlockSpec(memory_space=pl.ANY)] + [pl.BlockSpec(memory_space=pltpu.HBM)] * len(arrays),
        out_specs=whole_arrays(len(arrays)),
        scratch_shapes=[pltpu.SemaphoreType.DMA((len(arrays),))],
        compiler_params=pltpu.CompilerParams(vmem_limit_bytes=20 * 2**20),
    )(token, *arrays)


def prologue_body(top_count, places_ref, hidden_ref, packed_ref, mine_ref, give_ref):
    micro_count, tokens, width = hidden_ref.shape
    first, second, held = split_widths(width)
    start = -(-width // LANES) * LANES
    lane = lax.broadcasted_iota(jnp.int32, (tokens, LANES), 1)
    row = lax.broadcasted_iota(jnp.int32, (tokens, LANES), 0)
    here = lane % (ROUTING // 2)
    on_ids = (lane >= LANES - ROUTING) & (lane < LANES - ROUTING // 2)
    on_weights = lane >= LANES - ROUTING // 2

    def upright(place):
        at = start + place * tokens
        line = packed_ref[:, at // LANES * LANES : at // LANES * LANES + LANES]
        return jnp.sum(jnp.where(lane == row + at % LANES, line, 0.0), axis=1, keepdims=True)

    def store(ref, b, part, tile):
        size = part.shape[1]
        inside = size // LANES * LANES
        ref[b, :, :inside] = part[:, :inside].astype(jnp.bfloat16)
        if inside < size:
            rest = jnp.concatenate([part[:, inside:], jnp.zeros((tokens, LANES - size + inside), jnp.float32)], axis=1)
            tile = jnp.where(lane < size - inside, rest, tile)
        ref[b, :, inside:] = tile.astype(jnp.bfloat16)

    lower = places_ref[0] == 0
    for b in range(micro_count):
        residual = hidden_ref[b].astype(jnp.float32)
        scale = lax.rsqrt(jnp.mean(residual * residual, axis=-1, keepdims=True) + epsilon)
        normed = residual * scale * packed_ref[:, :width]
        tile = jnp.where(on_ids, -1.0, 0.0)
        for k in range(top_count):
            number = upright(b * top_count + k)
            weight = upright((micro_count + b) * top_count + k)
            high = weight.astype(jnp.bfloat16).astype(jnp.float32)
            middle = (weight - high).astype(jnp.bfloat16).astype(jnp.float32)
            for place, piece in enumerate((high, middle, weight - high - middle)):
                at = here == place * top_count + k
                tile = jnp.where(at & on_ids, number, jnp.where(at & on_weights, piece, tile))
        parts = normed[:, :first], normed[:, first:]

        @pl.when(lower)
        def _():
            store(mine_ref, b, parts[0], tile)
            store(give_ref, b, parts[1], tile)

        @pl.when(jnp.logical_not(lower))
        def _():
            store(mine_ref, b, parts[1], tile)
            store(give_ref, b, parts[0], tile)


def prologue(places, hidden, gain, ids, weights):
    micro_count, tokens, width = hidden.shape
    top_count = ids.shape[2]
    held = split_widths(width)[2]
    packed = jnp.concatenate(
        [
            jnp.pad(gain.astype(jnp.float32), (0, -width % LANES)),
            ids.transpose(0, 2, 1).reshape(-1).astype(jnp.float32),
            weights.transpose(0, 2, 1).reshape(-1),
        ]
    )
    packed = jnp.pad(packed, (0, -packed.shape[0] % LANES)).reshape(1, -1)
    return pl.pallas_call(
        functools.partial(prologue_body, top_count),
        out_shape=[jax.ShapeDtypeStruct((micro_count, tokens, held), jnp.bfloat16)] * 2,
        in_specs=[SCALARS] + whole_arrays(2),
        out_specs=whole_arrays(2),
        compiler_params=pltpu.CompilerParams(vmem_limit_bytes=20 * 2**20),
    )(places, hidden, packed)


def local(hidden, norm_gain, w_gate, w_up, w_down, expert_ids, route_weight):
    micro_count, tokens, width = hidden.shape
    top_count = expert_ids.shape[2]
    devices = lax.axis_size("req")
    experts = devices // HSPLIT
    rounded = HSPLIT * ((3 * tokens * top_count + 2 * experts * HSPLIT - 1) // (2 * experts * HSPLIT))
    capacity = min(tokens, max(HSPLIT, rounded))
    distant = devices // 8
    first, second, held = split_widths(width)
    position = lax.axis_index("req")
    core = position & 1
    lower = core == 0
    expert = position // HSPLIT
    places = jnp.stack([core, expert, expert ^ core]).astype(jnp.int32)

    def join(*blocks):
        return jnp.concatenate(blocks, axis=0)

    mine, give = prologue(places, hidden, norm_gain, expert_ids, route_weight)
    theirs = moved(give, other_core)
    pairs = [
        join(jnp.where(lower, mine[b], theirs[b]), jnp.where(lower, theirs[b], mine[b]))
        for b in range(micro_count)
    ]

    def tied(*arrays):
        return lax.optimization_barrier(arrays)

    def far_blocks(pair):
        return [moved(pair, far(j)) for j in range(1, distant)]

    chosen = tokens, capacity
    states = []

    def second_hop(state, apart):
        near, following = state["near"], state["next"]
        if apart:
            (send,) = select(*chosen, (1,), places, near, following)
        else:
            send, state["own"], *state["slots"] = select(*chosen, (1, 0), places, near, following)
        if len(states) > 1:
            send, states[-2]["arrived"] = tied(send, states[-2]["arrived"])
        state["arrived"] = moved(send, second_axis)
        if apart:
            following, _ = tied(following, send)
            state["own"], *state["slots"] = select(*chosen, (0,), places, near, following)

    pair = pairs[0]
    (gate_v,) = preload(pair, w_gate.T)
    if distant == 4:
        crossed, beside = moved(pair, far(2)), moved(pair, far(1))
        crossed, gate_v = tied(crossed, gate_v)
        (up_v,) = preload(crossed, w_up.T)
        passed = moved(crossed, far(1))
        passed, up_v = tied(passed, up_v)
        blocks = [beside, crossed, passed]
    else:
        (up_v,) = preload(pair, w_up.T)
        blocks = far_blocks(pair)
    column = join(pair, *blocks)
    states.append({"near": column, "next": moved(column, first_axis)})
    down_v = None
    for pair in pairs[1:]:
        last = states[-1]
        pair, last["near"] = tied(pair, last["near"])
        blocks = far_blocks(pair)
        second_hop(last, True)
        *blocks, last["own"] = tied(*blocks, last["own"])
        column = join(pair, *blocks)
        following = moved(column, first_axis)
        last["parts"] = ffn_start(places, last["own"], moved(last["own"], other_core), gate_v, up_v)
        if down_v is None:
            (down_v,) = preload(last["parts"][0], w_down)
            following, down_v = tied(following, down_v)
        states.append({"near": column, "next": following})
    second_hop(states[-1], False)
    if down_v is None:
        (down_v,) = preload(states[-1]["own"], w_down)

    hops = []
    for state in states:
        own, arrived = state["own"], state["arrived"]
        if "parts" not in state:
            token = hops[-1][1] if hops else None
            state["parts"] = ffn_start(places, own, moved(own, other_core), gate_v, up_v, token)
        if hops:
            arrived, *state["parts"] = tied(arrived, *state["parts"])
        hops.append(
            ffn(places, state["parts"], own, arrived, moved(arrived, other_core), gate_v, up_v, down_v)
        )

    def rounded_sum(a, b):
        return (a + b.astype(jnp.float32)).astype(jnp.bfloat16)

    def far_hop(block):
        block = block.reshape(distant, -1, held)
        if distant == 4:
            through = moved(block[3].astype(jnp.bfloat16), far(1))
            beside = moved(block[1].astype(jnp.bfloat16), far(1))
            return [block[0], [beside], rounded_sum(block[2], through)]
        return [block[0], [moved(block[j].astype(jnp.bfloat16), far(j)) for j in range(1, distant)], None]

    def settled(kept, arrivals, cross):
        for arrival in arrivals if cross is None else arrivals + [moved(cross, far(2))]:
            kept = kept + arrival.astype(jnp.float32)
        return kept

    totals = []
    near = None
    for state, (keep_near, keep_far, send_near, send_far) in zip(states, hops):
        give = rounded_sum(keep_far, moved(send_far, other_core))
        parts = state["slots"], keep_near, moved(send_near, other_core), moved(give, second_axis)
        if near is None:
            kept, following = merge((0, 1), (jnp.float32, jnp.bfloat16), *parts)
        else:
            (following,) = merge((1,), (jnp.bfloat16,), *parts)
            (kept,) = merge((0,), (jnp.float32,), *parts, following)
            near, kept = tied(near, kept)
            totals.append(far_hop(near))
        near = kept + moved(following, first_axis).astype(jnp.float32)
    totals.append(far_hop(near))
    sums = jnp.stack([settled(*total) for total in totals])
    own = jnp.where(lower, sums[:, :tokens], sums[:, tokens:])
    give = jnp.where(lower, sums[:, tokens:], sums[:, :tokens]).astype(jnp.bfloat16)
    taken = moved(give, other_core).astype(jnp.float32)
    mixture = jnp.concatenate(
        [jnp.where(lower, own, taken)[:, :, :first], jnp.where(lower, taken, own)[:, :, :second]], axis=2
    )
    return (hidden.astype(jnp.float32) + mixture).astype(jnp.bfloat16)


def solution(mesh):
    return jax.shard_map(
        local,
        mesh=mesh,
        in_specs=(
            P(None, ("groups", "req"), None),
            P(),
            P(None, "req"),
            P(None, "req"),
            P("req", None),
            P(None, ("groups", "req"), None),
            P(None, ("groups", "req"), None),
        ),
        out_specs=P(None, ("groups", "req"), None),
        check_vma=False,
    )
```

```python
import functools

import jax
import jax.numpy as jnp
from jax import lax
from jax.experimental import pallas as pl
from jax.experimental.pallas import tpu as pltpu
from jax.sharding import PartitionSpec as P

HSPLIT = 4
LANES = 128
ROUTING = 32

epsilon = 1e-05
swish_scale = 1.702

across = (((1,), (1,)), ((), ()))
downward = (((0,), (0,)), ((), ()))


def split_widths(width):
    first = width // 2 // LANES * LANES
    second = width - first
    held = -(-(second + ROUTING) // LANES) * LANES
    return first, second, held


def moved(block, partner):
    count = lax.axis_size("req")
    return lax.ppermute(block, "req", [(i, partner(i)) for i in range(count)])


def other_core(i):
    return i ^ 1


def first_axis(i):
    return i ^ (2 if i & 1 else 4)


def second_axis(i):
    return i ^ (4 if i & 1 else 2)


def far(step):
    return lambda i: i ^ (step << 3)


def whole_arrays(count):
    return [pl.BlockSpec(memory_space=pltpu.VMEM)] * count


SCALARS = pl.BlockSpec(memory_space=pltpu.SMEM)


def slots_of(tokens, capacity, base, places_ref, rows_ref):
    total, held = rows_ref.shape
    tile = rows_ref[:, held - LANES :].astype(jnp.float32)
    lane = lax.broadcasted_iota(jnp.int32, (total, LANES), 1)
    row = lax.broadcasted_iota(jnp.int32, (total, LANES), 0)
    listed = (lane >= LANES - ROUTING) & (lane < LANES - ROUTING // 2)

    def named(expert):
        return jnp.max(jnp.where(listed & (tile == expert.astype(jnp.float32)), 1.0, 0.0), axis=1, keepdims=True)

    mine, theirs = named(places_ref[1]), named(places_ref[2])
    marks = jnp.where(lane == 0, mine, jnp.where(lane == 1, theirs, 0.0))
    left = lax.broadcasted_iota(jnp.int32, (total, total), 0)
    right = lax.broadcasted_iota(jnp.int32, (total, total), 1)
    earlier = ((right < left) & (left // tokens == right // tokens)).astype(jnp.float32).astype(jnp.bfloat16)
    ahead = jnp.dot(earlier, marks.astype(jnp.bfloat16), preferred_element_type=jnp.float32)
    return jnp.where(marks > 0.0, ahead + (base + row // tokens * capacity).astype(jnp.float32), -1.0)


def select_body(tokens, capacity, wanted, places_ref, near_ref, next_ref, *out_refs):
    rows = near_ref.shape[0]
    compact = out_refs[0].shape[0]
    slots = [
        slots_of(tokens, capacity, part * (rows // tokens * capacity), places_ref, ref)
        for part, ref in enumerate((near_ref, next_ref))
    ]
    for part, slots_ref in enumerate(out_refs[len(wanted) :]):
        slots_ref[...] = slots[part]
    column = lax.broadcasted_iota(jnp.int32, (rows, compact), 1).astype(jnp.float32)
    for index, rows_ref in zip(wanted, out_refs):
        result = None
        for source, at in zip((near_ref, next_ref), slots):
            picks = (at[:, index : index + 1] == column).astype(jnp.float32).astype(jnp.bfloat16)
            part = lax.dot_general(picks, source[...], downward, preferred_element_type=jnp.float32)
            result = part if result is None else result + part
        rows_ref[...] = result.astype(jnp.bfloat16)


def select(tokens, capacity, wanted, places, near, following):
    located = 2 * int(0 in wanted)
    rows, held = near.shape
    compact = 2 * rows // tokens * capacity
    block = jax.ShapeDtypeStruct((compact, held), jnp.bfloat16)
    return pl.pallas_call(
        functools.partial(select_body, tokens, capacity, wanted),
        out_shape=[block] * len(wanted) + [jax.ShapeDtypeStruct((rows, LANES), jnp.float32)] * located,
        in_specs=[SCALARS] + whole_arrays(2),
        out_specs=whole_arrays(len(wanted) + located),
        compiler_params=pltpu.CompilerParams(vmem_limit_bytes=20 * 2**20),
        cost_estimate=pl.CostEstimate(flops=8 * rows * compact * held, bytes_accessed=8 * rows * held, transcendentals=0),
    )(places, near, following)


def merge_body(wanted, _, near_slots_ref, next_slots_ref, keep_ref, taken_ref, arrived_ref, *out_refs):
    rows = out_refs[0].shape[0]
    compact = keep_ref.shape[0]
    column = lax.broadcasted_iota(jnp.int32, (rows, compact), 1).astype(jnp.float32)
    high = (keep_ref[...] + taken_ref[...].astype(jnp.float32)).astype(jnp.bfloat16)
    for part, out_ref in zip(wanted, out_refs):
        slots = (near_slots_ref, next_slots_ref)[part][...]
        result = jnp.zeros((rows, keep_ref.shape[1]), jnp.float32)
        for index, source in enumerate((high, arrived_ref[...])):
            picks = (slots[:, index : index + 1] == column).astype(jnp.float32).astype(jnp.bfloat16)
            result += jnp.dot(picks, source, preferred_element_type=jnp.float32)
        out_ref[...] = result.astype(out_ref.dtype)


def merge(wanted, types, slots, keep, taken, arrived, token=None):
    token = slots[0] if token is None else token
    rows = slots[0].shape[0]
    compact, held = keep.shape
    return pl.pallas_call(
        functools.partial(merge_body, wanted),
        out_shape=[jax.ShapeDtypeStruct((rows, held), kind) for kind in types],
        in_specs=[pl.BlockSpec(memory_space=pl.ANY)] + whole_arrays(5),
        out_specs=whole_arrays(len(types)),
        compiler_params=pltpu.CompilerParams(vmem_limit_bytes=20 * 2**20),
        cost_estimate=pl.CostEstimate(flops=8 * rows * compact * held, bytes_accessed=8 * rows * held, transcendentals=0),
    )(token, *slots, keep, taken, arrived)


def ffn_body(
    places_ref, mine_near_ref, mine_far_ref, other_near_ref, other_far_ref, gate_v, up_v, down_v,
    keep_near_ref, keep_far_ref, send_near_ref, send_far_ref, rows_v, act_v,
):
    hidden, width = gate_v.shape
    first, second, held = split_widths(width)
    pair = mine_near_ref.shape[0]
    quad = pair // 2
    chunk = hidden // 3
    def lay(near, far_ref, swapped, start, size):
        for place in range(4):
            if swapped:
                source, block = (near, far_ref)[place % 2], place // 2
            else:
                source, block = (near, far_ref)[place // 2], place % 2
            rows_v[pl.ds(place * quad, quad), start : start + size] = source[pl.ds(block * quad, quad), :size]

    lower = places_ref[0] == 0

    @pl.when(lower)
    def _():
        lay(mine_near_ref, mine_far_ref, False, 0, first)
        lay(other_near_ref, other_far_ref, True, first, second)

    @pl.when(jnp.logical_not(lower))
    def _():
        lay(other_near_ref, other_far_ref, True, 0, first)
        lay(mine_near_ref, mine_far_ref, False, first, second)

    tile = jnp.concatenate([mine_near_ref[:, held - LANES :], mine_far_ref[:, held - LANES :]], axis=0)
    tile = tile.astype(jnp.float32)
    lane = lax.broadcasted_iota(jnp.int32, (2 * pair, LANES), 1)
    listed = (lane >= LANES - ROUTING) & (lane < LANES - ROUTING // 2)
    chosen = listed & (tile == places_ref[1].astype(jnp.float32))
    weight = jnp.sum(
        jnp.where(chosen, pltpu.roll(tile, LANES - ROUTING // 2, 1), 0.0), axis=1, keepdims=True
    )

    for part in range(3):
        there = slice(part * chunk, (part + 1) * chunk)
        gate = lax.dot_general(rows_v[...], gate_v[there, :], across, preferred_element_type=jnp.float32)
        up = lax.dot_general(rows_v[...], up_v[there, :], across, preferred_element_type=jnp.float32)
        act_v[:, there] = ((up + 1.0) * gate * jax.nn.sigmoid(swish_scale * gate)).astype(jnp.bfloat16)

    def keep_half(result, size):
        keep_near_ref[:, :size] = result[:pair]
        keep_far_ref[:, :size] = result[pair:]
        if size < held:
            keep_near_ref[:, size:] = jnp.zeros((pair, held - size), jnp.float32)
            keep_far_ref[:, size:] = jnp.zeros((pair, held - size), jnp.float32)

    def send_half(result, size):
        result = result.astype(jnp.bfloat16)
        for place in range(4):
            target, block = (send_near_ref, send_far_ref)[place % 2], place // 2
            target[pl.ds(block * quad, quad), :size] = result[place * quad : (place + 1) * quad]
        if size < held:
            send_near_ref[:, size:] = jnp.zeros((pair, held - size), jnp.bfloat16)
            send_far_ref[:, size:] = jnp.zeros((pair, held - size), jnp.bfloat16)

    def product(start, size):
        return weight * jnp.dot(act_v[...], down_v[:, start : start + size], preferred_element_type=jnp.float32)

    @pl.when(lower)
    def _():
        send_half(product(first, second), second)
        keep_half(product(0, first), first)

    @pl.when(jnp.logical_not(lower))
    def _():
        send_half(product(0, first), first)
        keep_half(product(first, second), second)


def ffn(places, mine_near, mine_far, other_near, other_far, gate_t, up_t, w_down):
    pair, held = mine_near.shape
    hidden, width = gate_t.shape
    total = 2 * pair
    return pl.pallas_call(
        ffn_body,
        out_shape=[jax.ShapeDtypeStruct((pair, held), jnp.float32)] * 2
        + [jax.ShapeDtypeStruct((pair, held), jnp.bfloat16)] * 2,
        in_specs=[SCALARS] + whole_arrays(7),
        out_specs=whole_arrays(4),
        scratch_shapes=[
            pltpu.VMEM((total, width), jnp.bfloat16),
            pltpu.VMEM((total, hidden), jnp.bfloat16),
        ],
        compiler_params=pltpu.CompilerParams(vmem_limit_bytes=20 * 2**20),
        cost_estimate=pl.CostEstimate(
            flops=6 * total * width * hidden,
            bytes_accessed=6 * width * hidden + 8 * total * held,
            transcendentals=total * hidden,
        ),
    )(places, mine_near, mine_far, other_near, other_far, gate_t, up_t, w_down)


def preload_body(_, *refs):
    count = (len(refs) - 1) // 2
    sems = refs[-1]
    copies = [pltpu.make_async_copy(refs[i], refs[count + i], sems.at[i]) for i in range(count)]
    for copy in copies:
        copy.start()
    for copy in copies:
        copy.wait()


def preload(token, *arrays):
    return pl.pallas_call(
        preload_body,
        out_shape=[pltpu.VMEM(a.shape, a.dtype) for a in arrays],
        in_specs=[pl.BlockSpec(memory_space=pl.ANY)] + [pl.BlockSpec(memory_space=pltpu.HBM)] * len(arrays),
        out_specs=whole_arrays(len(arrays)),
        scratch_shapes=[pltpu.SemaphoreType.DMA((len(arrays),))],
        compiler_params=pltpu.CompilerParams(vmem_limit_bytes=20 * 2**20),
    )(token, *arrays)


def prologue_body(top_count, places_ref, hidden_ref, packed_ref, mine_ref, give_ref):
    micro_count, tokens, width = hidden_ref.shape
    first, second, held = split_widths(width)
    start = -(-width // LANES) * LANES
    lane = lax.broadcasted_iota(jnp.int32, (tokens, LANES), 1)
    row = lax.broadcasted_iota(jnp.int32, (tokens, LANES), 0)
    here = lane % (ROUTING // 2)
    on_ids = (lane >= LANES - ROUTING) & (lane < LANES - ROUTING // 2)
    on_weights = lane >= LANES - ROUTING // 2

    def upright(place):
        at = start + place * tokens
        line = packed_ref[:, at // LANES * LANES : at // LANES * LANES + LANES]
        return jnp.sum(jnp.where(lane == row + at % LANES, line, 0.0), axis=1, keepdims=True)

    def store(ref, b, part, tile):
        size = part.shape[1]
        inside = size // LANES * LANES
        ref[b, :, :inside] = part[:, :inside].astype(jnp.bfloat16)
        if inside < size:
            rest = jnp.concatenate([part[:, inside:], jnp.zeros((tokens, LANES - size + inside), jnp.float32)], axis=1)
            tile = jnp.where(lane < size - inside, rest, tile)
        ref[b, :, inside:] = tile.astype(jnp.bfloat16)

    lower = places_ref[0] == 0
    for b in range(micro_count):
        residual = hidden_ref[b].astype(jnp.float32)
        scale = lax.rsqrt(jnp.mean(residual * residual, axis=-1, keepdims=True) + epsilon)
        normed = residual * scale * packed_ref[:, :width]
        tile = jnp.where(on_ids, -1.0, 0.0)
        for k in range(top_count):
            number = upright(b * top_count + k)
            weight = upright((micro_count + b) * top_count + k)
            high = weight.astype(jnp.bfloat16).astype(jnp.float32)
            middle = (weight - high).astype(jnp.bfloat16).astype(jnp.float32)
            for place, piece in enumerate((high, middle, weight - high - middle)):
                at = here == place * top_count + k
                tile = jnp.where(at & on_ids, number, jnp.where(at & on_weights, piece, tile))
        parts = normed[:, :first], normed[:, first:]

        @pl.when(lower)
        def _():
            store(mine_ref, b, parts[0], tile)
            store(give_ref, b, parts[1], tile)

        @pl.when(jnp.logical_not(lower))
        def _():
            store(mine_ref, b, parts[1], tile)
            store(give_ref, b, parts[0], tile)


def prologue(places, hidden, gain, ids, weights):
    micro_count, tokens, width = hidden.shape
    top_count = ids.shape[2]
    held = split_widths(width)[2]
    packed = jnp.concatenate(
        [
            jnp.pad(gain.astype(jnp.float32), (0, -width % LANES)),
            ids.transpose(0, 2, 1).reshape(-1).astype(jnp.float32),
            weights.transpose(0, 2, 1).reshape(-1),
        ]
    )
    packed = jnp.pad(packed, (0, -packed.shape[0] % LANES)).reshape(1, -1)
    return pl.pallas_call(
        functools.partial(prologue_body, top_count),
        out_shape=[jax.ShapeDtypeStruct((micro_count, tokens, held), jnp.bfloat16)] * 2,
        in_specs=[SCALARS] + whole_arrays(2),
        out_specs=whole_arrays(2),
        compiler_params=pltpu.CompilerParams(vmem_limit_bytes=20 * 2**20),
    )(places, hidden, packed)


def finish_body(places_ref, hidden_ref, own_ref, taken_ref, mixed_ref):
    first, second, _ = split_widths(hidden_ref.shape[2])
    lower = places_ref[0] == 0

    def add(low_ref, high_ref):
        for ref, (start, size) in ((low_ref, (0, first)), (high_ref, (first, second))):
            columns = slice(start, start + size)
            total = hidden_ref[:, :, columns].astype(jnp.float32) + ref[:, :, :size].astype(jnp.float32)
            mixed_ref[:, :, columns] = total.astype(jnp.bfloat16)

    @pl.when(lower)
    def _():
        add(own_ref, taken_ref)

    @pl.when(jnp.logical_not(lower))
    def _():
        add(taken_ref, own_ref)


def finish(places, hidden, own, taken):
    return pl.pallas_call(
        finish_body,
        out_shape=jax.ShapeDtypeStruct(hidden.shape, jnp.bfloat16),
        in_specs=[SCALARS] + whole_arrays(3),
        out_specs=pl.BlockSpec(memory_space=pltpu.VMEM),
        compiler_params=pltpu.CompilerParams(vmem_limit_bytes=20 * 2**20),
    )(places, hidden, own, taken)


def local(hidden, norm_gain, w_gate, w_up, w_down, expert_ids, route_weight):
    micro_count, tokens, width = hidden.shape
    top_count = expert_ids.shape[2]
    devices = lax.axis_size("req")
    experts = devices // HSPLIT
    rounded = HSPLIT * ((3 * tokens * top_count + 2 * experts * HSPLIT - 1) // (2 * experts * HSPLIT))
    capacity = min(tokens, max(HSPLIT, rounded))
    distant = devices // 8
    first, second, held = split_widths(width)
    position = lax.axis_index("req")
    core = position & 1
    lower = core == 0
    expert = position // HSPLIT
    places = jnp.stack([core, expert, expert ^ core]).astype(jnp.int32)

    def join(*blocks):
        return jnp.concatenate(blocks, axis=0)

    mine, give = prologue(places, hidden, norm_gain, expert_ids, route_weight)
    theirs = moved(give, other_core)
    pairs = [
        join(jnp.where(lower, mine[b], theirs[b]), jnp.where(lower, theirs[b], mine[b]))
        for b in range(micro_count)
    ]

    def tied(*arrays):
        return lax.optimization_barrier(arrays)

    def far_blocks(pair):
        return [moved(pair, far(j)) for j in range(1, distant)]

    chosen = tokens, capacity
    states = []

    def second_hop(state, apart):
        near, following = state["near"], state["next"]
        if apart:
            (send,) = select(*chosen, (1,), places, near, following)
        else:
            send, state["own"], *state["slots"] = select(*chosen, (1, 0), places, near, following)
        if len(states) > 1:
            send, states[-2]["arrived"] = tied(send, states[-2]["arrived"])
        state["arrived"] = moved(send, second_axis)
        if apart:
            following, _ = tied(following, send)
            state["own"], *state["slots"] = select(*chosen, (0,), places, near, following)

    pair = pairs[0]
    (gate_v,) = preload(pair, w_gate.T)
    if distant == 4:
        crossed, beside = moved(pair, far(2)), moved(pair, far(1))
        crossed, gate_v = tied(crossed, gate_v)
        (up_v,) = preload(crossed, w_up.T)
        passed = moved(crossed, far(1))
        passed, up_v = tied(passed, up_v)
        blocks = [beside, crossed, passed]
    else:
        (up_v,) = preload(pair, w_up.T)
        blocks = far_blocks(pair)
    column = join(pair, *blocks)
    states.append({"near": column, "next": moved(column, first_axis)})
    down_v = None
    for pair in pairs[1:]:
        last = states[-1]
        pair, last["near"] = tied(pair, last["near"])
        blocks = far_blocks(pair)
        second_hop(last, True)
        *blocks, last["own"] = tied(*blocks, last["own"])
        column = join(pair, *blocks)
        following = moved(column, first_axis)
        if down_v is None:
            (down_v,) = preload(last["own"], w_down)
            following, down_v = tied(following, down_v)
        states.append({"near": column, "next": following})
    second_hop(states[-1], False)
    if down_v is None:
        (down_v,) = preload(states[-1]["own"], w_down)

    hops = []
    before = None
    for state in states:
        own, arrived = state["own"], state["arrived"]
        if before is not None:
            arrived, *before = tied(arrived, *before)
            hops.append(before)
        before = ffn(places, own, arrived, moved(own, other_core), moved(arrived, other_core), gate_v, up_v, down_v)
    hops.append(before)

    def rounded_sum(a, b):
        return (a + b.astype(jnp.float32)).astype(jnp.bfloat16)

    def far_hop(block):
        block = block.reshape(distant, -1, held)
        if distant == 4:
            through = moved(block[3].astype(jnp.bfloat16), far(1))
            beside = moved(block[1].astype(jnp.bfloat16), far(1))
            return [block[0], [beside], rounded_sum(block[2], through)]
        return [block[0], [moved(block[j].astype(jnp.bfloat16), far(j)) for j in range(1, distant)], None]

    def settled(kept, arrivals, cross):
        for arrival in arrivals if cross is None else arrivals + [moved(cross, far(2))]:
            kept = kept + arrival.astype(jnp.float32)
        return kept

    totals = []
    near = None
    for state, (keep_near, keep_far, send_near, send_far) in zip(states, hops):
        give = rounded_sum(keep_far, moved(send_far, other_core))
        parts = state["slots"], keep_near, moved(send_near, other_core), moved(give, second_axis)
        if near is None:
            kept, following = merge((0, 1), (jnp.float32, jnp.bfloat16), *parts)
        else:
            (following,) = merge((1,), (jnp.bfloat16,), *parts)
            (kept,) = merge((0,), (jnp.float32,), *parts, following)
            near, kept = tied(near, kept)
            totals.append(far_hop(near))
        near = kept + moved(following, first_axis).astype(jnp.float32)
    totals.append(far_hop(near))
    sums = jnp.stack([settled(*total) for total in totals])
    own = jnp.where(lower, sums[:, :tokens], sums[:, tokens:])
    give = jnp.where(lower, sums[:, tokens:], sums[:, :tokens]).astype(jnp.bfloat16)
    taken = moved(give, other_core)
    return finish(places, hidden, own, taken)


def solution(mesh):
    return jax.shard_map(
        local,
        mesh=mesh,
        in_specs=(
            P(None, ("groups", "req"), None),
            P(),
            P(None, "req"),
            P(None, "req"),
            P("req", None),
            P(None, ("groups", "req"), None),
            P(None, ("groups", "req"), None),
        ),
        out_specs=P(None, ("groups", "req"), None),
        check_vma=False,
    )
```

```python
import functools

import jax
import jax.numpy as jnp
from jax import lax
from jax.experimental import pallas as pl
from jax.experimental.pallas import tpu as pltpu
from jax.sharding import PartitionSpec as P

HSPLIT = 4
LANES = 128
ROUTING = 32

epsilon = 1e-05
swish_scale = 1.702

across = (((1,), (1,)), ((), ()))
downward = (((0,), (0,)), ((), ()))


def split_widths(width):
    first = width // 2 // LANES * LANES
    second = width - first
    held = -(-(second + ROUTING) // LANES) * LANES
    return first, second, held


def moved(block, partner):
    count = lax.axis_size("req")
    return lax.ppermute(block, "req", [(i, partner(i)) for i in range(count)])


def other_core(i):
    return i ^ 1


def first_axis(i):
    return i ^ (2 if i & 1 else 4)


def second_axis(i):
    return i ^ (4 if i & 1 else 2)


def far(step):
    return lambda i: i ^ (step << 3)


def whole_arrays(count):
    return [pl.BlockSpec(memory_space=pltpu.VMEM)] * count


SCALARS = pl.BlockSpec(memory_space=pltpu.SMEM)


def slots_of(tokens, capacity, base, places_ref, rows_ref):
    total, held = rows_ref.shape
    tile = rows_ref[:, held - LANES :].astype(jnp.float32)
    lane = lax.broadcasted_iota(jnp.int32, (total, LANES), 1)
    row = lax.broadcasted_iota(jnp.int32, (total, LANES), 0)
    listed = (lane >= LANES - ROUTING) & (lane < LANES - ROUTING // 2)

    def named(expert):
        return jnp.max(jnp.where(listed & (tile == expert.astype(jnp.float32)), 1.0, 0.0), axis=1, keepdims=True)

    mine, theirs = named(places_ref[1]), named(places_ref[2])
    marks = jnp.where(lane == 0, mine, jnp.where(lane == 1, theirs, 0.0))
    left = lax.broadcasted_iota(jnp.int32, (total, total), 0)
    right = lax.broadcasted_iota(jnp.int32, (total, total), 1)
    earlier = ((right < left) & (left // tokens == right // tokens)).astype(jnp.float32).astype(jnp.bfloat16)
    ahead = jnp.dot(earlier, marks.astype(jnp.bfloat16), preferred_element_type=jnp.float32)
    return jnp.where(marks > 0.0, ahead + (base + row // tokens * capacity).astype(jnp.float32), -1.0)


def select_body(tokens, capacity, wanted, places_ref, near_ref, next_ref, *out_refs):
    rows = near_ref.shape[0]
    compact = out_refs[0].shape[0]
    slots = [
        slots_of(tokens, capacity, part * (rows // tokens * capacity), places_ref, ref)
        for part, ref in enumerate((near_ref, next_ref))
    ]
    for part, slots_ref in enumerate(out_refs[len(wanted) :]):
        slots_ref[...] = slots[part]
    column = lax.broadcasted_iota(jnp.int32, (rows, compact), 1).astype(jnp.float32)
    for index, rows_ref in zip(wanted, out_refs):
        result = None
        for source, at in zip((near_ref, next_ref), slots):
            picks = (at[:, index : index + 1] == column).astype(jnp.float32).astype(jnp.bfloat16)
            part = lax.dot_general(picks, source[...], downward, preferred_element_type=jnp.float32)
            result = part if result is None else result + part
        rows_ref[...] = result.astype(jnp.bfloat16)


def select(tokens, capacity, wanted, places, near, following):
    located = 2 * int(0 in wanted)
    rows, held = near.shape
    compact = 2 * rows // tokens * capacity
    block = jax.ShapeDtypeStruct((compact, held), jnp.bfloat16)
    return pl.pallas_call(
        functools.partial(select_body, tokens, capacity, wanted),
        out_shape=[block] * len(wanted) + [jax.ShapeDtypeStruct((rows, LANES), jnp.float32)] * located,
        in_specs=[SCALARS] + whole_arrays(2),
        out_specs=whole_arrays(len(wanted) + located),
        compiler_params=pltpu.CompilerParams(vmem_limit_bytes=20 * 2**20),
        cost_estimate=pl.CostEstimate(flops=8 * rows * compact * held, bytes_accessed=8 * rows * held, transcendentals=0),
    )(places, near, following)


def merge_body(wanted, _, near_slots_ref, next_slots_ref, keep_ref, taken_ref, arrived_ref, *out_refs):
    rows = out_refs[0].shape[0]
    compact = keep_ref.shape[0]
    column = lax.broadcasted_iota(jnp.int32, (rows, compact), 1).astype(jnp.float32)
    high = (keep_ref[...] + taken_ref[...].astype(jnp.float32)).astype(jnp.bfloat16)
    for part, out_ref in zip(wanted, out_refs):
        slots = (near_slots_ref, next_slots_ref)[part][...]
        result = jnp.zeros((rows, keep_ref.shape[1]), jnp.float32)
        for index, source in enumerate((high, arrived_ref[...])):
            picks = (slots[:, index : index + 1] == column).astype(jnp.float32).astype(jnp.bfloat16)
            result += jnp.dot(picks, source, preferred_element_type=jnp.float32)
        out_ref[...] = result.astype(out_ref.dtype)


def merge(wanted, types, slots, keep, taken, arrived, token=None):
    token = slots[0] if token is None else token
    rows = slots[0].shape[0]
    compact, held = keep.shape
    return pl.pallas_call(
        functools.partial(merge_body, wanted),
        out_shape=[jax.ShapeDtypeStruct((rows, held), kind) for kind in types],
        in_specs=[pl.BlockSpec(memory_space=pl.ANY)] + whole_arrays(5),
        out_specs=whole_arrays(len(types)),
        compiler_params=pltpu.CompilerParams(vmem_limit_bytes=20 * 2**20),
        cost_estimate=pl.CostEstimate(flops=8 * rows * compact * held, bytes_accessed=8 * rows * held, transcendentals=0),
    )(token, *slots, keep, taken, arrived)


def ffn_body(
    places_ref, mine_near_ref, mine_far_ref, other_near_ref, other_far_ref, gate_v, up_v, down_v,
    keep_near_ref, keep_far_ref, send_near_ref, send_far_ref, rows_v, act_v,
):
    hidden, width = gate_v.shape
    first, second, held = split_widths(width)
    pair = mine_near_ref.shape[0]
    quad = pair // 2
    chunk = hidden // 3
    def lay(near, far_ref, swapped, start, size):
        for place in range(4):
            if swapped:
                source, block = (near, far_ref)[place % 2], place // 2
            else:
                source, block = (near, far_ref)[place // 2], place % 2
            rows_v[pl.ds(place * quad, quad), start : start + size] = source[pl.ds(block * quad, quad), :size]

    lower = places_ref[0] == 0

    @pl.when(lower)
    def _():
        lay(mine_near_ref, mine_far_ref, False, 0, first)
        lay(other_near_ref, other_far_ref, True, first, second)

    @pl.when(jnp.logical_not(lower))
    def _():
        lay(other_near_ref, other_far_ref, True, 0, first)
        lay(mine_near_ref, mine_far_ref, False, first, second)

    tile = jnp.concatenate([mine_near_ref[:, held - LANES :], mine_far_ref[:, held - LANES :]], axis=0)
    tile = tile.astype(jnp.float32)
    lane = lax.broadcasted_iota(jnp.int32, (2 * pair, LANES), 1)
    listed = (lane >= LANES - ROUTING) & (lane < LANES - ROUTING // 2)
    chosen = listed & (tile == places_ref[1].astype(jnp.float32))
    weight = jnp.sum(
        jnp.where(chosen, pltpu.roll(tile, LANES - ROUTING // 2, 1), 0.0), axis=1, keepdims=True
    )

    for part in range(3):
        there = slice(part * chunk, (part + 1) * chunk)
        gate = lax.dot_general(rows_v[...], gate_v[there, :], across, preferred_element_type=jnp.float32)
        up = lax.dot_general(rows_v[...], up_v[there, :], across, preferred_element_type=jnp.float32)
        act_v[:, there] = ((up + 1.0) * gate * jax.nn.sigmoid(swish_scale * gate)).astype(jnp.bfloat16)

    def keep_half(result, size):
        keep_near_ref[:, :size] = result[:pair]
        keep_far_ref[:, :size] = result[pair:]
        if size < held:
            keep_near_ref[:, size:] = jnp.zeros((pair, held - size), jnp.float32)
            keep_far_ref[:, size:] = jnp.zeros((pair, held - size), jnp.float32)

    def send_half(result, size):
        result = result.astype(jnp.bfloat16)
        for place in range(4):
            target, block = (send_near_ref, send_far_ref)[place % 2], place // 2
            target[pl.ds(block * quad, quad), :size] = result[place * quad : (place + 1) * quad]
        if size < held:
            send_near_ref[:, size:] = jnp.zeros((pair, held - size), jnp.bfloat16)
            send_far_ref[:, size:] = jnp.zeros((pair, held - size), jnp.bfloat16)

    def product(start, size):
        return weight * jnp.dot(act_v[...], down_v[:, start : start + size], preferred_element_type=jnp.float32)

    @pl.when(lower)
    def _():
        send_half(product(first, second), second)
        keep_half(product(0, first), first)

    @pl.when(jnp.logical_not(lower))
    def _():
        send_half(product(0, first), first)
        keep_half(product(first, second), second)


def ffn(places, mine_near, mine_far, other_near, other_far, gate_t, up_t, w_down):
    pair, held = mine_near.shape
    hidden, width = gate_t.shape
    total = 2 * pair
    return pl.pallas_call(
        ffn_body,
        out_shape=[jax.ShapeDtypeStruct((pair, held), jnp.float32)] * 2
        + [jax.ShapeDtypeStruct((pair, held), jnp.bfloat16)] * 2,
        in_specs=[SCALARS] + whole_arrays(7),
        out_specs=whole_arrays(4),
        scratch_shapes=[
            pltpu.VMEM((total, width), jnp.bfloat16),
            pltpu.VMEM((total, hidden), jnp.bfloat16),
        ],
        compiler_params=pltpu.CompilerParams(vmem_limit_bytes=20 * 2**20),
        cost_estimate=pl.CostEstimate(
            flops=6 * total * width * hidden,
            bytes_accessed=6 * width * hidden + 8 * total * held,
            transcendentals=total * hidden,
        ),
    )(places, mine_near, mine_far, other_near, other_far, gate_t, up_t, w_down)


def preload_body(_, *refs):
    count = (len(refs) - 1) // 2
    sems = refs[-1]
    copies = [pltpu.make_async_copy(refs[i], refs[count + i], sems.at[i]) for i in range(count)]
    for copy in copies:
        copy.start()
    for copy in copies:
        copy.wait()


def preload(token, *arrays):
    return pl.pallas_call(
        preload_body,
        out_shape=[pltpu.VMEM(a.shape, a.dtype) for a in arrays],
        in_specs=[pl.BlockSpec(memory_space=pl.ANY)] + [pl.BlockSpec(memory_space=pltpu.HBM)] * len(arrays),
        out_specs=whole_arrays(len(arrays)),
        scratch_shapes=[pltpu.SemaphoreType.DMA((len(arrays),))],
        compiler_params=pltpu.CompilerParams(vmem_limit_bytes=20 * 2**20),
    )(token, *arrays)


def prologue_body(top_count, places_ref, hidden_ref, packed_ref, mine_ref, give_ref):
    micro_count, tokens, width = hidden_ref.shape
    first, second, held = split_widths(width)
    start = -(-width // LANES) * LANES
    lane = lax.broadcasted_iota(jnp.int32, (tokens, LANES), 1)
    row = lax.broadcasted_iota(jnp.int32, (tokens, LANES), 0)
    here = lane % (ROUTING // 2)
    on_ids = (lane >= LANES - ROUTING) & (lane < LANES - ROUTING // 2)
    on_weights = lane >= LANES - ROUTING // 2

    def upright(place):
        at = start + place * tokens
        line = packed_ref[:, at // LANES * LANES : at // LANES * LANES + LANES]
        return jnp.sum(jnp.where(lane == row + at % LANES, line, 0.0), axis=1, keepdims=True)

    def store(ref, b, part, tile):
        size = part.shape[1]
        inside = size // LANES * LANES
        ref[b, :, :inside] = part[:, :inside].astype(jnp.bfloat16)
        if inside < size:
            rest = jnp.concatenate([part[:, inside:], jnp.zeros((tokens, LANES - size + inside), jnp.float32)], axis=1)
            tile = jnp.where(lane < size - inside, rest, tile)
        ref[b, :, inside:] = tile.astype(jnp.bfloat16)

    lower = places_ref[0] == 0
    for b in range(micro_count):
        residual = hidden_ref[b].astype(jnp.float32)
        scale = lax.rsqrt(jnp.mean(residual * residual, axis=-1, keepdims=True) + epsilon)
        normed = residual * scale * packed_ref[:, :width]
        tile = jnp.where(on_ids, -1.0, 0.0)
        for k in range(top_count):
            number = upright(b * top_count + k)
            weight = upright((micro_count + b) * top_count + k)
            high = weight.astype(jnp.bfloat16).astype(jnp.float32)
            middle = (weight - high).astype(jnp.bfloat16).astype(jnp.float32)
            for place, piece in enumerate((high, middle, weight - high - middle)):
                at = here == place * top_count + k
                tile = jnp.where(at & on_ids, number, jnp.where(at & on_weights, piece, tile))
        parts = normed[:, :first], normed[:, first:]

        @pl.when(lower)
        def _():
            store(mine_ref, b, parts[0], tile)
            store(give_ref, b, parts[1], tile)

        @pl.when(jnp.logical_not(lower))
        def _():
            store(mine_ref, b, parts[1], tile)
            store(give_ref, b, parts[0], tile)


def prologue(places, hidden, gain, ids, weights):
    micro_count, tokens, width = hidden.shape
    top_count = ids.shape[2]
    held = split_widths(width)[2]
    packed = jnp.concatenate(
        [
            jnp.pad(gain.astype(jnp.float32), (0, -width % LANES)),
            ids.transpose(0, 2, 1).reshape(-1).astype(jnp.float32),
            weights.transpose(0, 2, 1).reshape(-1),
        ]
    )
    packed = jnp.pad(packed, (0, -packed.shape[0] % LANES)).reshape(1, -1)
    return pl.pallas_call(
        functools.partial(prologue_body, top_count),
        out_shape=[jax.ShapeDtypeStruct((micro_count, tokens, held), jnp.bfloat16)] * 2,
        in_specs=[SCALARS] + whole_arrays(2),
        out_specs=whole_arrays(2),
        compiler_params=pltpu.CompilerParams(vmem_limit_bytes=20 * 2**20),
    )(places, hidden, packed)


def finish_body(places_ref, hidden_ref, own_ref, taken_ref, mixed_ref):
    first, second, _ = split_widths(hidden_ref.shape[2])
    lower = places_ref[0] == 0

    def add(low_ref, high_ref):
        for ref, (start, size) in ((low_ref, (0, first)), (high_ref, (first, second))):
            columns = slice(start, start + size)
            total = hidden_ref[:, :, columns].astype(jnp.float32) + ref[:, :, :size].astype(jnp.float32)
            mixed_ref[:, :, columns] = total.astype(jnp.bfloat16)

    @pl.when(lower)
    def _():
        add(own_ref, taken_ref)

    @pl.when(jnp.logical_not(lower))
    def _():
        add(taken_ref, own_ref)


def finish(places, hidden, own, taken):
    return pl.pallas_call(
        finish_body,
        out_shape=jax.ShapeDtypeStruct(hidden.shape, jnp.bfloat16),
        in_specs=[SCALARS] + whole_arrays(3),
        out_specs=pl.BlockSpec(memory_space=pltpu.VMEM),
        compiler_params=pltpu.CompilerParams(vmem_limit_bytes=20 * 2**20),
    )(places, hidden, own, taken)


def local(hidden, norm_gain, w_gate, w_up, w_down, expert_ids, route_weight):
    micro_count, tokens, width = hidden.shape
    top_count = expert_ids.shape[2]
    devices = lax.axis_size("req")
    experts = devices // HSPLIT
    rounded = HSPLIT * ((3 * tokens * top_count + 2 * experts * HSPLIT - 1) // (2 * experts * HSPLIT))
    capacity = min(tokens, max(HSPLIT, rounded))
    distant = devices // 8
    first, second, held = split_widths(width)
    position = lax.axis_index("req")
    core = position & 1
    lower = core == 0
    expert = position // HSPLIT
    places = jnp.stack([core, expert, expert ^ core]).astype(jnp.int32)

    def join(*blocks):
        return jnp.concatenate(blocks, axis=0)

    mine, give = prologue(places, hidden, norm_gain, expert_ids, route_weight)
    theirs = moved(give, other_core)
    pairs = [
        join(jnp.where(lower, mine[b], theirs[b]), jnp.where(lower, theirs[b], mine[b]))
        for b in range(micro_count)
    ]

    def tied(*arrays):
        return lax.optimization_barrier(arrays)

    def far_blocks(pair):
        return [moved(pair, far(j)) for j in range(1, distant)]

    chosen = tokens, capacity
    states = []

    def second_hop(state, apart):
        near, following = state["near"], state["next"]
        if apart:
            (send,) = select(*chosen, (1,), places, near, following)
        else:
            send, state["own"], *state["slots"] = select(*chosen, (1, 0), places, near, following)
        if len(states) > 1:
            send, states[-2]["arrived"] = tied(send, states[-2]["arrived"])
        state["arrived"] = moved(send, second_axis)
        if apart:
            following, _ = tied(following, send)
            state["own"], *state["slots"] = select(*chosen, (0,), places, near, following)

    pair = pairs[0]
    (gate_v,) = preload(pair, w_gate.T)
    if distant == 4:
        crossed = moved(pair, far(2))
        again, pairs[-1] = tied(pair, pairs[-1])
        beside = moved(again, far(1))
        crossed, gate_v = tied(crossed, gate_v)
        (up_v,) = preload(crossed, w_up.T)
        passed = moved(crossed, far(1))
        passed, up_v = tied(passed, up_v)
        blocks = [beside, crossed, passed]
    else:
        (up_v,) = preload(pair, w_up.T)
        blocks = far_blocks(pair)
    column = join(pair, *blocks)
    states.append({"near": column, "next": moved(column, first_axis)})
    down_v = None
    for pair in pairs[1:]:
        last = states[-1]
        pair, last["near"] = tied(pair, last["near"])
        blocks = far_blocks(pair)
        second_hop(last, True)
        *blocks, last["own"] = tied(*blocks, last["own"])
        column = join(pair, *blocks)
        following = moved(column, first_axis)
        if down_v is None:
            (down_v,) = preload(last["own"], w_down)
            following, down_v = tied(following, down_v)
        states.append({"near": column, "next": following})
    second_hop(states[-1], False)
    if down_v is None:
        (down_v,) = preload(states[-1]["own"], w_down)

    hops = []
    before = None
    for state in states:
        own, arrived = state["own"], state["arrived"]
        if before is not None:
            arrived, *before = tied(arrived, *before)
            hops.append(before)
        before = ffn(places, own, arrived, moved(own, other_core), moved(arrived, other_core), gate_v, up_v, down_v)
    hops.append(before)

    def rounded_sum(a, b):
        return (a + b.astype(jnp.float32)).astype(jnp.bfloat16)

    def far_hop(block):
        block = block.reshape(distant, -1, held)
        if distant == 4:
            odd = moved(jnp.stack([block[1], block[3]]).astype(jnp.bfloat16), far(1))
            return [block[0], [odd[0]], rounded_sum(block[2], odd[1])]
        return [block[0], [moved(block[j].astype(jnp.bfloat16), far(j)) for j in range(1, distant)], None]

    def settled(kept, arrivals, cross):
        for arrival in arrivals if cross is None else arrivals + [moved(cross, far(2))]:
            kept = kept + arrival.astype(jnp.float32)
        return kept

    totals = []
    near = None
    for state, (keep_near, keep_far, send_near, send_far) in zip(states, hops):
        give = rounded_sum(keep_far, moved(send_far, other_core))
        parts = state["slots"], keep_near, moved(send_near, other_core), moved(give, second_axis)
        if near is None:
            kept, following = merge((0, 1), (jnp.float32, jnp.bfloat16), *parts)
        else:
            (following,) = merge((1,), (jnp.bfloat16,), *parts)
            (kept,) = merge((0,), (jnp.float32,), *parts, following)
            near, kept = tied(near, kept)
            totals.append(far_hop(near))
        near = kept + moved(following, first_axis).astype(jnp.float32)
    totals.append(far_hop(near))
    sums = jnp.stack([settled(*total) for total in totals])
    own = jnp.where(lower, sums[:, :tokens], sums[:, tokens:])
    give = jnp.where(lower, sums[:, tokens:], sums[:, :tokens]).astype(jnp.bfloat16)
    taken = moved(give, other_core)
    return finish(places, hidden, own, taken)


def solution(mesh):
    return jax.shard_map(
        local,
        mesh=mesh,
        in_specs=(
            P(None, ("groups", "req"), None),
            P(),
            P(None, "req"),
            P(None, "req"),
            P("req", None),
            P(None, ("groups", "req"), None),
            P(None, ("groups", "req"), None),
        ),
        out_specs=P(None, ("groups", "req"), None),
        check_vma=False,
    )
```

```python
import functools

import jax
import jax.numpy as jnp
from jax import lax
from jax.experimental import pallas as pl
from jax.experimental.pallas import tpu as pltpu
from jax.sharding import PartitionSpec as P

HSPLIT = 4
LANES = 128
ROUTING = 32

epsilon = 1e-05
swish_scale = 1.702

across = (((1,), (1,)), ((), ()))
downward = (((0,), (0,)), ((), ()))


def split_widths(width):
    first = width // 2 // LANES * LANES
    second = width - first
    held = -(-(second + ROUTING) // LANES) * LANES
    return first, second, held


def moved(block, partner):
    count = lax.axis_size("req")
    return lax.ppermute(block, "req", [(i, partner(i)) for i in range(count)])


def other_core(i):
    return i ^ 1


def first_axis(i):
    return i ^ (2 if i & 1 else 4)


def second_axis(i):
    return i ^ (4 if i & 1 else 2)


def far(step):
    return lambda i: i ^ (step << 3)


def whole_arrays(count):
    return [pl.BlockSpec(memory_space=pltpu.VMEM)] * count


SCALARS = pl.BlockSpec(memory_space=pltpu.SMEM)


def slots_of(tokens, capacity, base, places_ref, rows_ref):
    total, held = rows_ref.shape
    tile = rows_ref[:, held - LANES :].astype(jnp.float32)
    lane = lax.broadcasted_iota(jnp.int32, (total, LANES), 1)
    row = lax.broadcasted_iota(jnp.int32, (total, LANES), 0)
    listed = (lane >= LANES - ROUTING) & (lane < LANES - ROUTING // 2)

    def named(expert):
        return jnp.max(jnp.where(listed & (tile == expert.astype(jnp.float32)), 1.0, 0.0), axis=1, keepdims=True)

    mine, theirs = named(places_ref[1]), named(places_ref[2])
    marks = jnp.where(lane == 0, mine, jnp.where(lane == 1, theirs, 0.0))
    left = lax.broadcasted_iota(jnp.int32, (total, total), 0)
    right = lax.broadcasted_iota(jnp.int32, (total, total), 1)
    earlier = ((right < left) & (left // tokens == right // tokens)).astype(jnp.float32).astype(jnp.bfloat16)
    ahead = jnp.dot(earlier, marks.astype(jnp.bfloat16), preferred_element_type=jnp.float32)
    return jnp.where(marks > 0.0, ahead + (base + row // tokens * capacity).astype(jnp.float32), -1.0)


def select_body(tokens, capacity, wanted, places_ref, near_ref, next_ref, *out_refs):
    rows = near_ref.shape[0]
    compact = out_refs[0].shape[0]
    slots = [
        slots_of(tokens, capacity, part * (rows // tokens * capacity), places_ref, ref)
        for part, ref in enumerate((near_ref, next_ref))
    ]
    for part, slots_ref in enumerate(out_refs[len(wanted) :]):
        slots_ref[...] = slots[part]
    column = lax.broadcasted_iota(jnp.int32, (rows, compact), 1).astype(jnp.float32)
    for index, rows_ref in zip(wanted, out_refs):
        result = None
        for source, at in zip((near_ref, next_ref), slots):
            picks = (at[:, index : index + 1] == column).astype(jnp.float32).astype(jnp.bfloat16)
            part = lax.dot_general(picks, source[...], downward, preferred_element_type=jnp.float32)
            result = part if result is None else result + part
        rows_ref[...] = result.astype(jnp.bfloat16)


def select(tokens, capacity, wanted, places, near, following):
    located = 2 * int(0 in wanted)
    rows, held = near.shape
    compact = 2 * rows // tokens * capacity
    block = jax.ShapeDtypeStruct((compact, held), jnp.bfloat16)
    return pl.pallas_call(
        functools.partial(select_body, tokens, capacity, wanted),
        out_shape=[block] * len(wanted) + [jax.ShapeDtypeStruct((rows, LANES), jnp.float32)] * located,
        in_specs=[SCALARS] + whole_arrays(2),
        out_specs=whole_arrays(len(wanted) + located),
        compiler_params=pltpu.CompilerParams(vmem_limit_bytes=20 * 2**20),
        cost_estimate=pl.CostEstimate(flops=8 * rows * compact * held, bytes_accessed=8 * rows * held, transcendentals=0),
    )(places, near, following)


def merge_body(wanted, _, near_slots_ref, next_slots_ref, keep_ref, taken_ref, arrived_ref, *out_refs):
    rows = out_refs[0].shape[0]
    compact = keep_ref.shape[0]
    column = lax.broadcasted_iota(jnp.int32, (rows, compact), 1).astype(jnp.float32)
    high = (keep_ref[...] + taken_ref[...].astype(jnp.float32)).astype(jnp.bfloat16)
    for part, out_ref in zip(wanted, out_refs):
        slots = (near_slots_ref, next_slots_ref)[part][...]
        result = jnp.zeros((rows, keep_ref.shape[1]), jnp.float32)
        for index, source in enumerate((high, arrived_ref[...])):
            picks = (slots[:, index : index + 1] == column).astype(jnp.float32).astype(jnp.bfloat16)
            result += jnp.dot(picks, source, preferred_element_type=jnp.float32)
        out_ref[...] = result.astype(out_ref.dtype)


def merge(wanted, types, slots, keep, taken, arrived, token=None):
    token = slots[0] if token is None else token
    rows = slots[0].shape[0]
    compact, held = keep.shape
    return pl.pallas_call(
        functools.partial(merge_body, wanted),
        out_shape=[jax.ShapeDtypeStruct((rows, held), kind) for kind in types],
        in_specs=[pl.BlockSpec(memory_space=pl.ANY)] + whole_arrays(5),
        out_specs=whole_arrays(len(types)),
        compiler_params=pltpu.CompilerParams(vmem_limit_bytes=20 * 2**20),
        cost_estimate=pl.CostEstimate(flops=8 * rows * compact * held, bytes_accessed=8 * rows * held, transcendentals=0),
    )(token, *slots, keep, taken, arrived)


def ffn_body(
    places_ref, mine_near_ref, mine_far_ref, other_near_ref, other_far_ref, gate_v, up_v, down_v,
    keep_near_ref, keep_far_ref, send_near_ref, send_far_ref, rows_v, act_v,
):
    hidden, width = gate_v.shape
    first, second, held = split_widths(width)
    pair = mine_near_ref.shape[0]
    quad = pair // 2
    chunk = hidden // 3
    def lay(near, far_ref, swapped, start, size):
        for place in range(4):
            if swapped:
                source, block = (near, far_ref)[place % 2], place // 2
            else:
                source, block = (near, far_ref)[place // 2], place % 2
            rows_v[pl.ds(place * quad, quad), start : start + size] = source[pl.ds(block * quad, quad), :size]

    lower = places_ref[0] == 0

    @pl.when(lower)
    def _():
        lay(mine_near_ref, mine_far_ref, False, 0, first)
        lay(other_near_ref, other_far_ref, True, first, second)

    @pl.when(jnp.logical_not(lower))
    def _():
        lay(other_near_ref, other_far_ref, True, 0, first)
        lay(mine_near_ref, mine_far_ref, False, first, second)

    tile = jnp.concatenate([mine_near_ref[:, held - LANES :], mine_far_ref[:, held - LANES :]], axis=0)
    tile = tile.astype(jnp.float32)
    lane = lax.broadcasted_iota(jnp.int32, (2 * pair, LANES), 1)
    listed = (lane >= LANES - ROUTING) & (lane < LANES - ROUTING // 2)
    chosen = listed & (tile == places_ref[1].astype(jnp.float32))
    weight = jnp.sum(
        jnp.where(chosen, pltpu.roll(tile, LANES - ROUTING // 2, 1), 0.0), axis=1, keepdims=True
    )

    for part in range(3):
        there = slice(part * chunk, (part + 1) * chunk)
        gate = lax.dot_general(rows_v[...], gate_v[there, :], across, preferred_element_type=jnp.float32)
        up = lax.dot_general(rows_v[...], up_v[there, :], across, preferred_element_type=jnp.float32)
        act_v[:, there] = ((up + 1.0) * gate * jax.nn.sigmoid(swish_scale * gate)).astype(jnp.bfloat16)

    def keep_half(result, size):
        keep_near_ref[:, :size] = result[:pair]
        keep_far_ref[:, :size] = result[pair:]
        if size < held:
            keep_near_ref[:, size:] = jnp.zeros((pair, held - size), jnp.float32)
            keep_far_ref[:, size:] = jnp.zeros((pair, held - size), jnp.float32)

    def send_half(result, size):
        result = result.astype(jnp.bfloat16)
        for place in range(4):
            target, block = (send_near_ref, send_far_ref)[place % 2], place // 2
            target[pl.ds(block * quad, quad), :size] = result[place * quad : (place + 1) * quad]
        if size < held:
            send_near_ref[:, size:] = jnp.zeros((pair, held - size), jnp.bfloat16)
            send_far_ref[:, size:] = jnp.zeros((pair, held - size), jnp.bfloat16)

    def product(start, size):
        return weight * jnp.dot(act_v[...], down_v[:, start : start + size], preferred_element_type=jnp.float32)

    @pl.when(lower)
    def _():
        send_half(product(first, second), second)
        keep_half(product(0, first), first)

    @pl.when(jnp.logical_not(lower))
    def _():
        send_half(product(0, first), first)
        keep_half(product(first, second), second)


def ffn(places, mine_near, mine_far, other_near, other_far, gate_t, up_t, w_down):
    pair, held = mine_near.shape
    hidden, width = gate_t.shape
    total = 2 * pair
    return pl.pallas_call(
        ffn_body,
        out_shape=[jax.ShapeDtypeStruct((pair, held), jnp.float32)] * 2
        + [jax.ShapeDtypeStruct((pair, held), jnp.bfloat16)] * 2,
        in_specs=[SCALARS] + whole_arrays(7),
        out_specs=whole_arrays(4),
        scratch_shapes=[
            pltpu.VMEM((total, width), jnp.bfloat16),
            pltpu.VMEM((total, hidden), jnp.bfloat16),
        ],
        compiler_params=pltpu.CompilerParams(vmem_limit_bytes=20 * 2**20),
        cost_estimate=pl.CostEstimate(
            flops=6 * total * width * hidden,
            bytes_accessed=6 * width * hidden + 8 * total * held,
            transcendentals=total * hidden,
        ),
    )(places, mine_near, mine_far, other_near, other_far, gate_t, up_t, w_down)


def preload_body(_, *refs):
    count = (len(refs) - 1) // 2
    sems = refs[-1]
    copies = [pltpu.make_async_copy(refs[i], refs[count + i], sems.at[i]) for i in range(count)]
    for copy in copies:
        copy.start()
    for copy in copies:
        copy.wait()


def preload(token, *arrays):
    return pl.pallas_call(
        preload_body,
        out_shape=[pltpu.VMEM(a.shape, a.dtype) for a in arrays],
        in_specs=[pl.BlockSpec(memory_space=pl.ANY)] + [pl.BlockSpec(memory_space=pltpu.HBM)] * len(arrays),
        out_specs=whole_arrays(len(arrays)),
        scratch_shapes=[pltpu.SemaphoreType.DMA((len(arrays),))],
        compiler_params=pltpu.CompilerParams(vmem_limit_bytes=20 * 2**20),
    )(token, *arrays)


def prologue_body(top_count, places_ref, hidden_ref, packed_ref, mine_ref, give_ref):
    micro_count, tokens, width = hidden_ref.shape
    first, second, held = split_widths(width)
    start = -(-width // LANES) * LANES
    lane = lax.broadcasted_iota(jnp.int32, (tokens, LANES), 1)
    row = lax.broadcasted_iota(jnp.int32, (tokens, LANES), 0)
    here = lane % (ROUTING // 2)
    on_ids = (lane >= LANES - ROUTING) & (lane < LANES - ROUTING // 2)
    on_weights = lane >= LANES - ROUTING // 2

    def upright(place):
        at = start + place * tokens
        line = packed_ref[:, at // LANES * LANES : at // LANES * LANES + LANES]
        return jnp.sum(jnp.where(lane == row + at % LANES, line, 0.0), axis=1, keepdims=True)

    def store(ref, b, part, tile):
        size = part.shape[1]
        inside = size // LANES * LANES
        ref[b, :, :inside] = part[:, :inside].astype(jnp.bfloat16)
        if inside < size:
            rest = jnp.concatenate([part[:, inside:], jnp.zeros((tokens, LANES - size + inside), jnp.float32)], axis=1)
            tile = jnp.where(lane < size - inside, rest, tile)
        ref[b, :, inside:] = tile.astype(jnp.bfloat16)

    lower = places_ref[0] == 0
    for b in range(micro_count):
        residual = hidden_ref[b].astype(jnp.float32)
        scale = lax.rsqrt(jnp.mean(residual * residual, axis=-1, keepdims=True) + epsilon)
        normed = residual * scale * packed_ref[:, :width]
        tile = jnp.where(on_ids, -1.0, 0.0)
        for k in range(top_count):
            number = upright(b * top_count + k)
            weight = upright((micro_count + b) * top_count + k)
            high = weight.astype(jnp.bfloat16).astype(jnp.float32)
            middle = (weight - high).astype(jnp.bfloat16).astype(jnp.float32)
            for place, piece in enumerate((high, middle, weight - high - middle)):
                at = here == place * top_count + k
                tile = jnp.where(at & on_ids, number, jnp.where(at & on_weights, piece, tile))
        parts = normed[:, :first], normed[:, first:]

        @pl.when(lower)
        def _():
            store(mine_ref, b, parts[0], tile)
            store(give_ref, b, parts[1], tile)

        @pl.when(jnp.logical_not(lower))
        def _():
            store(mine_ref, b, parts[1], tile)
            store(give_ref, b, parts[0], tile)


def prologue(places, hidden, gain, ids, weights):
    micro_count, tokens, width = hidden.shape
    top_count = ids.shape[2]
    held = split_widths(width)[2]
    packed = jnp.concatenate(
        [
            jnp.pad(gain.astype(jnp.float32), (0, -width % LANES)),
            ids.transpose(0, 2, 1).reshape(-1).astype(jnp.float32),
            weights.transpose(0, 2, 1).reshape(-1),
        ]
    )
    packed = jnp.pad(packed, (0, -packed.shape[0] % LANES)).reshape(1, -1)
    return pl.pallas_call(
        functools.partial(prologue_body, top_count),
        out_shape=[jax.ShapeDtypeStruct((micro_count, tokens, held), jnp.bfloat16)] * 2,
        in_specs=[SCALARS] + whole_arrays(2),
        out_specs=whole_arrays(2),
        compiler_params=pltpu.CompilerParams(vmem_limit_bytes=20 * 2**20),
    )(places, hidden, packed)


def local(hidden, norm_gain, w_gate, w_up, w_down, expert_ids, route_weight):
    micro_count, tokens, width = hidden.shape
    top_count = expert_ids.shape[2]
    devices = lax.axis_size("req")
    experts = devices // HSPLIT
    rounded = HSPLIT * ((3 * tokens * top_count + 2 * experts * HSPLIT - 1) // (2 * experts * HSPLIT))
    capacity = min(tokens, max(HSPLIT, rounded))
    distant = devices // 8
    first, second, held = split_widths(width)
    position = lax.axis_index("req")
    core = position & 1
    lower = core == 0
    expert = position // HSPLIT
    places = jnp.stack([core, expert, expert ^ core]).astype(jnp.int32)

    def join(*blocks):
        return jnp.concatenate(blocks, axis=0)

    mine, give = prologue(places, hidden, norm_gain, expert_ids, route_weight)
    theirs = moved(give, other_core)
    pairs = [
        join(jnp.where(lower, mine[b], theirs[b]), jnp.where(lower, theirs[b], mine[b]))
        for b in range(micro_count)
    ]

    def tied(*arrays):
        return lax.optimization_barrier(arrays)

    def far_blocks(pair):
        return [moved(pair, far(j)) for j in range(1, distant)]

    chosen = tokens, capacity
    states = []

    def second_hop(state, apart):
        near, following = state["near"], state["next"]
        if apart:
            (send,) = select(*chosen, (1,), places, near, following)
        else:
            send, state["own"], *state["slots"] = select(*chosen, (1, 0), places, near, following)
        if len(states) > 1:
            send, states[-2]["arrived"] = tied(send, states[-2]["arrived"])
        state["arrived"] = moved(send, second_axis)
        if apart:
            following, _ = tied(following, send)
            state["own"], *state["slots"] = select(*chosen, (0,), places, near, following)

    pair = pairs[0]
    (gate_v,) = preload(pair, w_gate.T)
    if distant == 4:
        crossed = moved(pair, far(2))
        again, pairs[-1] = tied(pair, pairs[-1])
        beside = moved(again, far(1))
        crossed, gate_v = tied(crossed, gate_v)
        (up_v,) = preload(crossed, w_up.T)
        passed = moved(crossed, far(1))
        passed, up_v = tied(passed, up_v)
        blocks = [beside, crossed, passed]
    else:
        (up_v,) = preload(pair, w_up.T)
        blocks = far_blocks(pair)
    column = join(pair, *blocks)
    states.append({"near": column, "next": moved(column, first_axis)})
    down_v = None
    for pair in pairs[1:]:
        last = states[-1]
        pair, last["near"] = tied(pair, last["near"])
        blocks = far_blocks(pair)
        second_hop(last, True)
        *blocks, last["own"] = tied(*blocks, last["own"])
        column = join(pair, *blocks)
        following = moved(column, first_axis)
        if down_v is None:
            (down_v,) = preload(last["own"], w_down)
            following, down_v = tied(following, down_v)
        states.append({"near": column, "next": following})
    second_hop(states[-1], False)
    if down_v is None:
        (down_v,) = preload(states[-1]["own"], w_down)

    hops = []
    before = None
    for state in states:
        own, arrived = state["own"], state["arrived"]
        if before is not None:
            arrived, *before = tied(arrived, *before)
            hops.append(before)
        before = ffn(places, own, arrived, moved(own, other_core), moved(arrived, other_core), gate_v, up_v, down_v)
    hops.append(before)

    def rounded_sum(a, b):
        return (a + b.astype(jnp.float32)).astype(jnp.bfloat16)

    def far_hop(block):
        block = block.reshape(distant, -1, held)
        if distant == 4:
            through = moved(block[3].astype(jnp.bfloat16), far(1))
            beside = moved(block[1].astype(jnp.bfloat16), far(1))
            return [block[0], [beside], rounded_sum(block[2], through)]
        return [block[0], [moved(block[j].astype(jnp.bfloat16), far(j)) for j in range(1, distant)], None]

    def settled(kept, arrivals, cross):
        for arrival in arrivals if cross is None else arrivals + [moved(cross, far(2))]:
            kept = kept + arrival.astype(jnp.float32)
        return kept

    totals = []
    near = None
    for state, (keep_near, keep_far, send_near, send_far) in zip(states, hops):
        give = rounded_sum(keep_far, moved(send_far, other_core))
        parts = state["slots"], keep_near, moved(send_near, other_core), moved(give, second_axis)
        if near is None:
            kept, following = merge((0, 1), (jnp.float32, jnp.bfloat16), *parts)
        else:
            (following,) = merge((1,), (jnp.bfloat16,), *parts)
            (kept,) = merge((0,), (jnp.float32,), *parts, following)
            near, kept = tied(near, kept)
            totals.append(far_hop(near))
        near = kept + moved(following, first_axis).astype(jnp.float32)
    totals.append(far_hop(near))
    sums = jnp.stack([settled(*total) for total in totals])
    own = jnp.where(lower, sums[:, :tokens], sums[:, tokens:])
    give = jnp.where(lower, sums[:, tokens:], sums[:, :tokens]).astype(jnp.bfloat16)
    taken = moved(give, other_core).astype(jnp.float32)
    mixture = jnp.concatenate(
        [jnp.where(lower, own, taken)[:, :, :first], jnp.where(lower, taken, own)[:, :, :second]], axis=2
    )
    return (hidden.astype(jnp.float32) + mixture).astype(jnp.bfloat16)


def solution(mesh):
    return jax.shard_map(
        local,
        mesh=mesh,
        in_specs=(
            P(None, ("groups", "req"), None),
            P(),
            P(None, "req"),
            P(None, "req"),
            P("req", None),
            P(None, ("groups", "req"), None),
            P(None, ("groups", "req"), None),
        ),
        out_specs=P(None, ("groups", "req"), None),
        check_vma=False,
    )
```

```python
import functools

import jax
import jax.numpy as jnp
from jax import lax
from jax.experimental import pallas as pl
from jax.experimental.pallas import tpu as pltpu
from jax.sharding import PartitionSpec as P

HSPLIT = 4
LANES = 128
ROUTING = 32

epsilon = 1e-05
swish_scale = 1.702

across = (((1,), (1,)), ((), ()))
downward = (((0,), (0,)), ((), ()))


def split_widths(width):
    first = width // 2 // LANES * LANES
    second = width - first
    held = -(-(second + ROUTING) // LANES) * LANES
    return first, second, held


def moved(block, partner):
    count = lax.axis_size("req")
    return lax.ppermute(block, "req", [(i, partner(i)) for i in range(count)])


def other_core(i):
    return i ^ 1


def first_axis(i):
    return i ^ (2 if i & 1 else 4)


def second_axis(i):
    return i ^ (4 if i & 1 else 2)


def far(step):
    return lambda i: i ^ (step << 3)


def whole_arrays(count):
    return [pl.BlockSpec(memory_space=pltpu.VMEM)] * count


SCALARS = pl.BlockSpec(memory_space=pltpu.SMEM)


def slots_of(tokens, capacity, base, places_ref, rows_ref):
    total, held = rows_ref.shape
    tile = rows_ref[:, held - LANES :].astype(jnp.float32)
    lane = lax.broadcasted_iota(jnp.int32, (total, LANES), 1)
    row = lax.broadcasted_iota(jnp.int32, (total, LANES), 0)
    listed = (lane >= LANES - ROUTING) & (lane < LANES - ROUTING // 2)

    def named(expert):
        return jnp.max(jnp.where(listed & (tile == expert.astype(jnp.float32)), 1.0, 0.0), axis=1, keepdims=True)

    mine, theirs = named(places_ref[1]), named(places_ref[2])
    marks = jnp.where(lane == 0, mine, jnp.where(lane == 1, theirs, 0.0))
    left = lax.broadcasted_iota(jnp.int32, (total, total), 0)
    right = lax.broadcasted_iota(jnp.int32, (total, total), 1)
    earlier = ((right < left) & (left // tokens == right // tokens)).astype(jnp.float32).astype(jnp.bfloat16)
    ahead = jnp.dot(earlier, marks.astype(jnp.bfloat16), preferred_element_type=jnp.float32)
    return jnp.where(marks > 0.0, ahead + (base + row // tokens * capacity).astype(jnp.float32), -1.0)


def select_body(tokens, capacity, wanted, places_ref, near_ref, next_ref, *out_refs):
    rows = near_ref.shape[0]
    compact = out_refs[0].shape[0]
    slots = [
        slots_of(tokens, capacity, part * (rows // tokens * capacity), places_ref, ref)
        for part, ref in enumerate((near_ref, next_ref))
    ]
    for part, slots_ref in enumerate(out_refs[len(wanted) :]):
        slots_ref[...] = slots[part]
    column = lax.broadcasted_iota(jnp.int32, (rows, compact), 1).astype(jnp.float32)
    for index, rows_ref in zip(wanted, out_refs):
        result = None
        for source, at in zip((near_ref, next_ref), slots):
            picks = (at[:, index : index + 1] == column).astype(jnp.float32).astype(jnp.bfloat16)
            part = lax.dot_general(picks, source[...], downward, preferred_element_type=jnp.float32)
            result = part if result is None else result + part
        rows_ref[...] = result.astype(jnp.bfloat16)


def select(tokens, capacity, wanted, places, near, following):
    located = 2 * int(0 in wanted)
    rows, held = near.shape
    compact = 2 * rows // tokens * capacity
    block = jax.ShapeDtypeStruct((compact, held), jnp.bfloat16)
    return pl.pallas_call(
        functools.partial(select_body, tokens, capacity, wanted),
        out_shape=[block] * len(wanted) + [jax.ShapeDtypeStruct((rows, LANES), jnp.float32)] * located,
        in_specs=[SCALARS] + whole_arrays(2),
        out_specs=whole_arrays(len(wanted) + located),
        compiler_params=pltpu.CompilerParams(vmem_limit_bytes=20 * 2**20),
        cost_estimate=pl.CostEstimate(flops=8 * rows * compact * held, bytes_accessed=8 * rows * held, transcendentals=0),
    )(places, near, following)


def merge_body(wanted, _, near_slots_ref, next_slots_ref, keep_ref, taken_ref, arrived_ref, *out_refs):
    rows = out_refs[0].shape[0]
    compact = keep_ref.shape[0]
    column = lax.broadcasted_iota(jnp.int32, (rows, compact), 1).astype(jnp.float32)
    high = (keep_ref[...] + taken_ref[...].astype(jnp.float32)).astype(jnp.bfloat16)
    for part, out_ref in zip(wanted, out_refs):
        slots = (near_slots_ref, next_slots_ref)[part][...]
        result = jnp.zeros((rows, keep_ref.shape[1]), jnp.float32)
        for index, source in enumerate((high, arrived_ref[...])):
            picks = (slots[:, index : index + 1] == column).astype(jnp.float32).astype(jnp.bfloat16)
            result += jnp.dot(picks, source, preferred_element_type=jnp.float32)
        out_ref[...] = result.astype(out_ref.dtype)


def merge(wanted, types, slots, keep, taken, arrived, token=None):
    token = slots[0] if token is None else token
    rows = slots[0].shape[0]
    compact, held = keep.shape
    return pl.pallas_call(
        functools.partial(merge_body, wanted),
        out_shape=[jax.ShapeDtypeStruct((rows, held), kind) for kind in types],
        in_specs=[pl.BlockSpec(memory_space=pl.ANY)] + whole_arrays(5),
        out_specs=whole_arrays(len(types)),
        compiler_params=pltpu.CompilerParams(vmem_limit_bytes=20 * 2**20),
        cost_estimate=pl.CostEstimate(flops=8 * rows * compact * held, bytes_accessed=8 * rows * held, transcendentals=0),
    )(token, *slots, keep, taken, arrived)


def ffn_body(
    places_ref, mine_near_ref, mine_far_ref, other_near_ref, other_far_ref, gate_v, up_v, down_v,
    keep_near_ref, keep_far_ref, send_near_ref, send_far_ref, rows_v, act_v,
):
    hidden, width = gate_v.shape
    first, second, held = split_widths(width)
    pair = mine_near_ref.shape[0]
    quad = pair // 2
    chunk = 2 * LANES
    def lay(near, far_ref, swapped, start, size):
        for place in range(4):
            if swapped:
                source, block = (near, far_ref)[place % 2], place // 2
            else:
                source, block = (near, far_ref)[place // 2], place % 2
            rows_v[pl.ds(place * quad, quad), start : start + size] = source[pl.ds(block * quad, quad), :size]

    lower = places_ref[0] == 0

    @pl.when(lower)
    def _():
        lay(mine_near_ref, mine_far_ref, False, 0, first)
        lay(other_near_ref, other_far_ref, True, first, second)

    @pl.when(jnp.logical_not(lower))
    def _():
        lay(other_near_ref, other_far_ref, True, 0, first)
        lay(mine_near_ref, mine_far_ref, False, first, second)

    tile = jnp.concatenate([mine_near_ref[:, held - LANES :], mine_far_ref[:, held - LANES :]], axis=0)
    tile = tile.astype(jnp.float32)
    lane = lax.broadcasted_iota(jnp.int32, (2 * pair, LANES), 1)
    listed = (lane >= LANES - ROUTING) & (lane < LANES - ROUTING // 2)
    chosen = listed & (tile == places_ref[1].astype(jnp.float32))
    weight = jnp.sum(
        jnp.where(chosen, pltpu.roll(tile, LANES - ROUTING // 2, 1), 0.0), axis=1, keepdims=True
    )

    for start in range(0, hidden, chunk):
        there = slice(start, min(start + chunk, hidden))
        gate = lax.dot_general(rows_v[...], gate_v[there, :], across, preferred_element_type=jnp.float32)
        up = lax.dot_general(rows_v[...], up_v[there, :], across, preferred_element_type=jnp.float32)
        act_v[:, there] = ((up + 1.0) * gate * jax.nn.sigmoid(swish_scale * gate)).astype(jnp.bfloat16)

    def keep_half(result, size):
        keep_near_ref[:, :size] = result[:pair]
        keep_far_ref[:, :size] = result[pair:]
        if size < held:
            keep_near_ref[:, size:] = jnp.zeros((pair, held - size), jnp.float32)
            keep_far_ref[:, size:] = jnp.zeros((pair, held - size), jnp.float32)

    def send_half(result, size):
        result = result.astype(jnp.bfloat16)
        for place in range(4):
            target, block = (send_near_ref, send_far_ref)[place % 2], place // 2
            target[pl.ds(block * quad, quad), :size] = result[place * quad : (place + 1) * quad]
        if size < held:
            send_near_ref[:, size:] = jnp.zeros((pair, held - size), jnp.bfloat16)
            send_far_ref[:, size:] = jnp.zeros((pair, held - size), jnp.bfloat16)

    def product(start, size):
        return weight * jnp.dot(act_v[...], down_v[:, start : start + size], preferred_element_type=jnp.float32)

    @pl.when(lower)
    def _():
        send_half(product(first, second), second)
        keep_half(product(0, first), first)

    @pl.when(jnp.logical_not(lower))
    def _():
        send_half(product(0, first), first)
        keep_half(product(first, second), second)


def ffn(places, mine_near, mine_far, other_near, other_far, gate_t, up_t, w_down):
    pair, held = mine_near.shape
    hidden, width = gate_t.shape
    total = 2 * pair
    return pl.pallas_call(
        ffn_body,
        out_shape=[jax.ShapeDtypeStruct((pair, held), jnp.float32)] * 2
        + [jax.ShapeDtypeStruct((pair, held), jnp.bfloat16)] * 2,
        in_specs=[SCALARS] + whole_arrays(7),
        out_specs=whole_arrays(4),
        scratch_shapes=[
            pltpu.VMEM((total, width), jnp.bfloat16),
            pltpu.VMEM((total, hidden), jnp.bfloat16),
        ],
        compiler_params=pltpu.CompilerParams(vmem_limit_bytes=20 * 2**20),
        cost_estimate=pl.CostEstimate(
            flops=6 * total * width * hidden,
            bytes_accessed=6 * width * hidden + 8 * total * held,
            transcendentals=total * hidden,
        ),
    )(places, mine_near, mine_far, other_near, other_far, gate_t, up_t, w_down)


def preload_body(_, *refs):
    count = (len(refs) - 1) // 2
    sems = refs[-1]
    copies = [pltpu.make_async_copy(refs[i], refs[count + i], sems.at[i]) for i in range(count)]
    for copy in copies:
        copy.start()
    for copy in copies:
        copy.wait()


def preload(token, *arrays):
    return pl.pallas_call(
        preload_body,
        out_shape=[pltpu.VMEM(a.shape, a.dtype) for a in arrays],
        in_specs=[pl.BlockSpec(memory_space=pl.ANY)] + [pl.BlockSpec(memory_space=pltpu.HBM)] * len(arrays),
        out_specs=whole_arrays(len(arrays)),
        scratch_shapes=[pltpu.SemaphoreType.DMA((len(arrays),))],
        compiler_params=pltpu.CompilerParams(vmem_limit_bytes=20 * 2**20),
    )(token, *arrays)


def prologue_body(top_count, places_ref, hidden_ref, packed_ref, mine_ref, give_ref):
    micro_count, tokens, width = hidden_ref.shape
    first, second, held = split_widths(width)
    start = -(-width // LANES) * LANES
    lane = lax.broadcasted_iota(jnp.int32, (tokens, LANES), 1)
    row = lax.broadcasted_iota(jnp.int32, (tokens, LANES), 0)
    here = lane % (ROUTING // 2)
    on_ids = (lane >= LANES - ROUTING) & (lane < LANES - ROUTING // 2)
    on_weights = lane >= LANES - ROUTING // 2

    def upright(place):
        at = start + place * tokens
        line = packed_ref[:, at // LANES * LANES : at // LANES * LANES + LANES]
        return jnp.sum(jnp.where(lane == row + at % LANES, line, 0.0), axis=1, keepdims=True)

    def store(ref, b, part, tile):
        size = part.shape[1]
        inside = size // LANES * LANES
        ref[b, :, :inside] = part[:, :inside].astype(jnp.bfloat16)
        if inside < size:
            rest = jnp.concatenate([part[:, inside:], jnp.zeros((tokens, LANES - size + inside), jnp.float32)], axis=1)
            tile = jnp.where(lane < size - inside, rest, tile)
        ref[b, :, inside:] = tile.astype(jnp.bfloat16)

    lower = places_ref[0] == 0
    for b in range(micro_count):
        residual = hidden_ref[b].astype(jnp.float32)
        scale = lax.rsqrt(jnp.mean(residual * residual, axis=-1, keepdims=True) + epsilon)
        normed = residual * scale * packed_ref[:, :width]
        tile = jnp.where(on_ids, -1.0, 0.0)
        for k in range(top_count):
            number = upright(b * top_count + k)
            weight = upright((micro_count + b) * top_count + k)
            high = weight.astype(jnp.bfloat16).astype(jnp.float32)
            middle = (weight - high).astype(jnp.bfloat16).astype(jnp.float32)
            for place, piece in enumerate((high, middle, weight - high - middle)):
                at = here == place * top_count + k
                tile = jnp.where(at & on_ids, number, jnp.where(at & on_weights, piece, tile))
        parts = normed[:, :first], normed[:, first:]

        @pl.when(lower)
        def _():
            store(mine_ref, b, parts[0], tile)
            store(give_ref, b, parts[1], tile)

        @pl.when(jnp.logical_not(lower))
        def _():
            store(mine_ref, b, parts[1], tile)
            store(give_ref, b, parts[0], tile)


def prologue(places, hidden, gain, ids, weights):
    micro_count, tokens, width = hidden.shape
    top_count = ids.shape[2]
    held = split_widths(width)[2]
    packed = jnp.concatenate(
        [
            jnp.pad(gain.astype(jnp.float32), (0, -width % LANES)),
            ids.transpose(0, 2, 1).reshape(-1).astype(jnp.float32),
            weights.transpose(0, 2, 1).reshape(-1),
        ]
    )
    packed = jnp.pad(packed, (0, -packed.shape[0] % LANES)).reshape(1, -1)
    return pl.pallas_call(
        functools.partial(prologue_body, top_count),
        out_shape=[jax.ShapeDtypeStruct((micro_count, tokens, held), jnp.bfloat16)] * 2,
        in_specs=[SCALARS] + whole_arrays(2),
        out_specs=whole_arrays(2),
        compiler_params=pltpu.CompilerParams(vmem_limit_bytes=20 * 2**20),
    )(places, hidden, packed)


def local(hidden, norm_gain, w_gate, w_up, w_down, expert_ids, route_weight):
    micro_count, tokens, width = hidden.shape
    top_count = expert_ids.shape[2]
    devices = lax.axis_size("req")
    experts = devices // HSPLIT
    rounded = HSPLIT * ((3 * tokens * top_count + 2 * experts * HSPLIT - 1) // (2 * experts * HSPLIT))
    capacity = min(tokens, max(HSPLIT, rounded))
    distant = devices // 8
    first, second, held = split_widths(width)
    position = lax.axis_index("req")
    core = position & 1
    lower = core == 0
    expert = position // HSPLIT
    places = jnp.stack([core, expert, expert ^ core]).astype(jnp.int32)

    def join(*blocks):
        return jnp.concatenate(blocks, axis=0)

    mine, give = prologue(places, hidden, norm_gain, expert_ids, route_weight)
    theirs = moved(give, other_core)
    pairs = [
        join(jnp.where(lower, mine[b], theirs[b]), jnp.where(lower, theirs[b], mine[b]))
        for b in range(micro_count)
    ]

    def tied(*arrays):
        return lax.optimization_barrier(arrays)

    def far_blocks(pair):
        return [moved(pair, far(j)) for j in range(1, distant)]

    chosen = tokens, capacity
    states = []

    def second_hop(state, apart):
        near, following = state["near"], state["next"]
        if apart:
            (send,) = select(*chosen, (1,), places, near, following)
        else:
            send, state["own"], *state["slots"] = select(*chosen, (1, 0), places, near, following)
        if len(states) > 1:
            send, states[-2]["arrived"] = tied(send, states[-2]["arrived"])
        state["arrived"] = moved(send, second_axis)
        if apart:
            following, _ = tied(following, send)
            state["own"], *state["slots"] = select(*chosen, (0,), places, near, following)

    pair = pairs[0]
    (gate_v,) = preload(pair, w_gate.T)
    if distant == 4:
        crossed = moved(pair, far(2))
        again, pairs[-1] = tied(pair, pairs[-1])
        beside = moved(again, far(1))
        crossed, gate_v = tied(crossed, gate_v)
        (up_v,) = preload(crossed, w_up.T)
        passed = moved(crossed, far(1))
        passed, up_v = tied(passed, up_v)
        blocks = [beside, crossed, passed]
    else:
        (up_v,) = preload(pair, w_up.T)
        blocks = far_blocks(pair)
    column = join(pair, *blocks)
    states.append({"near": column, "next": moved(column, first_axis)})
    down_v = None
    for pair in pairs[1:]:
        last = states[-1]
        pair, last["near"] = tied(pair, last["near"])
        blocks = far_blocks(pair)
        second_hop(last, True)
        *blocks, last["own"] = tied(*blocks, last["own"])
        column = join(pair, *blocks)
        following = moved(column, first_axis)
        if down_v is None:
            (down_v,) = preload(last["own"], w_down)
            following, down_v = tied(following, down_v)
        states.append({"near": column, "next": following})
    second_hop(states[-1], False)
    if down_v is None:
        (down_v,) = preload(states[-1]["own"], w_down)

    hops = []
    before = None
    for state in states:
        own, arrived = state["own"], state["arrived"]
        if before is not None:
            arrived, *before = tied(arrived, *before)
            hops.append(before)
        before = ffn(places, own, arrived, moved(own, other_core), moved(arrived, other_core), gate_v, up_v, down_v)
    hops.append(before)

    def rounded_sum(a, b):
        return (a + b.astype(jnp.float32)).astype(jnp.bfloat16)

    def far_hop(block):
        block = block.reshape(distant, -1, held)
        if distant == 4:
            through = moved(block[3].astype(jnp.bfloat16), far(1))
            beside = moved(block[1].astype(jnp.bfloat16), far(1))
            return [block[0], [beside], rounded_sum(block[2], through)]
        return [block[0], [moved(block[j].astype(jnp.bfloat16), far(j)) for j in range(1, distant)], None]

    def settled(kept, arrivals, cross):
        for arrival in arrivals if cross is None else arrivals + [moved(cross, far(2))]:
            kept = kept + arrival.astype(jnp.float32)
        return kept

    totals = []
    near = None
    for state, (keep_near, keep_far, send_near, send_far) in zip(states, hops):
        give = rounded_sum(keep_far, moved(send_far, other_core))
        parts = state["slots"], keep_near, moved(send_near, other_core), moved(give, second_axis)
        if near is None:
            kept, following = merge((0, 1), (jnp.float32, jnp.bfloat16), *parts)
        else:
            (following,) = merge((1,), (jnp.bfloat16,), *parts)
            (kept,) = merge((0,), (jnp.float32,), *parts, following)
            near, kept = tied(near, kept)
            totals.append(far_hop(near))
        near = kept + moved(following, first_axis).astype(jnp.float32)
    totals.append(far_hop(near))
    sums = jnp.stack([settled(*total) for total in totals])
    own = jnp.where(lower, sums[:, :tokens], sums[:, tokens:])
    give = jnp.where(lower, sums[:, tokens:], sums[:, :tokens]).astype(jnp.bfloat16)
    taken = moved(give, other_core).astype(jnp.float32)
    mixture = jnp.concatenate(
        [jnp.where(lower, own, taken)[:, :, :first], jnp.where(lower, taken, own)[:, :, :second]], axis=2
    )
    return (hidden.astype(jnp.float32) + mixture).astype(jnp.bfloat16)


def solution(mesh):
    return jax.shard_map(
        local,
        mesh=mesh,
        in_specs=(
            P(None, ("groups", "req"), None),
            P(),
            P(None, "req"),
            P(None, "req"),
            P("req", None),
            P(None, ("groups", "req"), None),
            P(None, ("groups", "req"), None),
        ),
        out_specs=P(None, ("groups", "req"), None),
        check_vma=False,
    )
```
